32 devices in a mesh: seq: 4 (over y, x), batch: 8 (over z, core).
Axes of the slice: x: 2, y: 2, z: 4, core: 2. Of those that a mesh axis runs over, the one named last changes fastest.
Arguments:
- tokens: bfloat16 [32, 1024, 1024], P('batch', 'seq'), may hold values from -6 to 6
- cotangent: bfloat16 [32, 1024, 1024], P('batch', 'seq'), may hold values from -6 to 6
- bins: int32 [32], P('batch'), may hold values from 0 to 63
- live_count: int32 [8], P('batch'), may hold values from 1 to 4, as said below
- w_qkv: bfloat16 [1024, 3072], replicated, may hold values from -0.1875 to 0.1875
- w_out: bfloat16 [1024, 1024], replicated, may hold values from -3.5 to 3.5
- w_up: bfloat16 [1024, 4096], replicated, may hold values from -0.1875 to 0.1875
- w_down: bfloat16 [4096, 1024], replicated, may hold values from -0.09375 to 0.09375
- gain_attn: float32 [64, 1024], replicated, may hold values from 0.1 to 1.9
- gain_mlp: float32 [64, 1024], replicated, may hold values from 0.1 to 1.9
Outputs:
- output: bfloat16 [32, 1024, 1024], P('batch', 'seq')
- grad_tokens: float32 [32, 1024, 1024], P('batch', 'seq')
- grad_qkv: float32 [1024, 3072], P('batch')
- grad_out: float32 [1024, 1024], P('batch')
- grad_up: float32 [1024, 4096], P('batch')
- grad_down: float32 [4096, 1024], P('batch')
- grad_gain_attn: float32 [64, 1024], P('batch')
- grad_gain_mlp: float32 [64, 1024], P('batch')
The draws below stay inside these ranges and needn't reach their ends.
Inputs may be any that keep to these rules, and one draw needn't show every extreme that they name: The first live_count slots of each index of batch hold live sequences; some index has 4 live and some has 1.
All inputs are finite; a program needn't handle non-finite values.
Results may differ from the reference program's by a relative error of at most 0.015.
Values may be sent and summed in bfloat16 or wider, within the bound.
A program may use at most 256 MiB of HBM per device.

```python
import math
import jax
import jax.numpy as jnp
from jax import lax

D = 1024
HEADS = 16
FF = 4096
HD = 64
LEN = 1024
SLOTS = 4
NBINS = 64
SEQS = 32
N_BATCH = 8


def draw_live_count(key, part):
    key = jax.random.fold_in(key, 7)
    key_counts, key_order = jax.random.split(key)
    number_groups = SEQS // SLOTS
    counts_drawn = jax.random.randint(key_counts, (number_groups,), 1, SLOTS + 1)
    shuffled = jax.random.permutation(key_order, number_groups)
    counts_drawn = counts_drawn.at[shuffled[0]].set(SLOTS)
    counts_drawn = counts_drawn.at[shuffled[1]].set(1)
    return counts_drawn.astype(jnp.int32)


def plant(entries, stream_key, low, largest):
    dims = entries.shape
    spot = [jax.random.randint(jax.random.fold_in(stream_key, axis), (), 0, dims[axis]) for axis in range(len(dims))]
    entries = entries.at[tuple(spot)].set(low)
    longest = dims.index(max(dims))
    spot[longest] = (spot[longest] + 1) % dims[longest]
    return entries.at[tuple(spot)].set(largest)


def level_of(key, shape, shards, smallest, top_value):
    def one(dim, shards_of):
        draws = jax.random.uniform(jax.random.fold_in(jax.random.fold_in(key, 6), dim), (shards_of,), jnp.float32, smallest / len(shards), top_value / len(shards))
        return jnp.repeat(jnp.exp(draws), shape[dim] // shards_of).reshape((-1,) + (1,) * (len(shape) - dim - 1))

    level = one(*shards[0])
    for cut in shards[1:]:
        level = level * one(*cut)
    return level


def normal_values(key, dims, deviation, limit, cuts=(), kind=jnp.bfloat16):
    values = jax.random.normal(key, dims, jnp.float32) * deviation
    if len(cuts) > 0:
        values = level_of(key, dims, cuts, -0.22, 0.18) * values
    return jnp.clip(values, min=-limit, max=limit).astype(kind)


def setup_inputs(seed: int = 0) -> dict:
    keys = jax.random.split(jax.random.key(seed), 11)
    return {
        "tokens": normal_values(keys[0], (SEQS, LEN, D), 1.0, 6.0, ((0, 8), (1, 4))),
        "cotangent": normal_values(keys[1], (SEQS, LEN, D), 1.0, 6.0, ((0, 8), (1, 4))),
        "bins": plant(jax.random.randint(keys[2], (SEQS,), 0, NBINS), jax.random.fold_in(keys[2], 1), 0, NBINS - 1).astype(jnp.int32),
        "live_count": draw_live_count(jax.random.fold_in(keys[10], 71), 0),
        "w_qkv": normal_values(keys[4], (D, 3 * D), D ** -0.5, 0.1875),
        "w_out": normal_values(keys[5], (D, D), (max(3 * D // LEN, 1)) ** -0.5, 3.5),
        "w_up": normal_values(keys[6], (D, FF), D ** -0.5, 0.1875),
        "w_down": normal_values(keys[7], (FF, D), FF ** -0.5, 0.09375),
        "gain_attn": jnp.clip(1.0 + 0.18 * jax.random.normal(keys[8], (NBINS, D), jnp.float32), 0.1, 1.9),
        "gain_mlp": jnp.clip(1.0 + 0.18 * jax.random.normal(keys[9], (NBINS, D), jnp.float32), 0.1, 1.9),
    }


@jax.custom_vjp
def low(v):
    return lax.optimization_barrier(v.astype(jnp.bfloat16)).astype(jnp.float32)

@jax.custom_vjp
def low_back(v):
    return v

def low_keep(v):
    return (low(v), None)

def low_pass(kept, grad):
    return (grad,)

def back_keep(v):
    return (v, None)

def back_low(kept, grad):
    return (low(grad),)
low.defvjp(low_keep, low_pass)
low_back.defvjp(back_keep, back_low)

def layer_norm(values_in):
    centred = values_in - lax.optimization_barrier(jnp.mean(values_in, axis=-1, keepdims=True))
    return centred * lax.rsqrt(lax.optimization_barrier(jnp.mean(centred * centred, axis=-1, keepdims=True)) + 1e-05)

def attend(queries, key_rows, values):
    block_rows = math.gcd(LEN, 512)
    blocks = queries.reshape(LEN // block_rows, block_rows, HEADS, HD)

    def block_fn(query_block):
        scores = jnp.einsum('qhd,khd->hqk', query_block, key_rows, precision=lax.Precision.HIGHEST) * HD ** (-0.5)
        scores = low_back(scores)
        softmax_rows = low(jax.nn.softmax(scores, axis=-1))
        return jnp.einsum('hqk,khd->qhd', softmax_rows, values, precision=lax.Precision.HIGHEST)
    return lax.map(jax.checkpoint(block_fn), blocks).reshape(LEN, HEADS, HD)

def layer_block(inputs, w_qkv, w_out, w_up, w_down, gain_attn, gain_mlp, bin_group):
    count_here = inputs.shape[0]
    ready_attn = low(layer_norm(inputs) * gain_attn[bin_group][:, None, :])
    packed = jnp.einsum('gtd,de->gte', ready_attn, w_qkv, precision=lax.Precision.HIGHEST)
    packed = low(low_back(packed))
    shaped = packed.reshape(count_here, LEN, HEADS, 3, HD)
    mixed_list = [attend(shaped[position, :, :, 0], shaped[position, :, :, 1], shaped[position, :, :, 2]) for position in range(count_here)]
    mixed_rows = low(low_back(jnp.stack(mixed_list).reshape(count_here, LEN, D)))
    attended = low_back(jnp.einsum('gtd,de->gte', mixed_rows, w_out, precision=lax.Precision.HIGHEST))
    hidden = inputs + attended
    ready_mlp = low(layer_norm(hidden) * gain_mlp[bin_group][:, None, :])
    upward = low_back(jnp.einsum('gtd,df->gtf', ready_mlp, w_up, precision=lax.Precision.HIGHEST))
    active = low(jax.nn.gelu(upward))
    branch = low_back(jnp.einsum('gtf,fd->gtd', active, w_down, precision=lax.Precision.HIGHEST))
    return hidden + branch

def reference(tokens, cotangent, bins, live_count, w_qkv, w_out, w_up, w_down, gain_attn, gain_mlp):
    weights = (w_qkv.astype(jnp.float32), w_out.astype(jnp.float32), w_up.astype(jnp.float32), w_down.astype(jnp.float32), gain_attn.astype(jnp.float32), gain_mlp.astype(jnp.float32))
    inputs = tokens.astype(jnp.float32).reshape(N_BATCH, SLOTS, LEN, D)
    grads_in = cotangent.astype(jnp.float32).reshape(N_BATCH, SLOTS, LEN, D)
    bin_groups = bins.reshape(N_BATCH, SLOTS).astype(jnp.int32)
    alive_mask = (jnp.arange(SLOTS, dtype=jnp.int32)[None, :] < live_count[:, None]).astype(jnp.float32)

    def group_step(running, pieces):
        group_in, group_grad, bin_group, alive_group = pieces

        def forward(inputs_here, wa, wb, wc, wd, table_a, table_m):
            return layer_block(inputs_here, wa, wb, wc, wd, table_a, table_m, bin_group)
        outputs, pullback = jax.vjp(forward, group_in, *weights)
        gradients = pullback(group_grad * alive_group[:, None, None])
        updated = tuple((total + piece for total, piece in zip(running, gradients[1:])))
        return (updated, (outputs.astype(jnp.bfloat16), gradients[0]))
    initial = tuple((jnp.zeros(weight.shape, jnp.float32) for weight in weights))
    totals, (outputs, grad_inputs) = lax.scan(group_step, initial, (inputs, grads_in, bin_groups, alive_mask))
    return (outputs.reshape(SEQS, LEN, D), grad_inputs.reshape(SEQS, LEN, D), totals[0], totals[1], totals[2], totals[3], totals[4], totals[5])
```

```python
import functools
import math

import jax
import jax.numpy as jnp
from jax import lax
from jax.experimental import pallas as pl
from jax.experimental.pallas import tpu as pltpu
from jax.sharding import PartitionSpec as P

F32 = jnp.float32
BF16 = jnp.bfloat16
HEAD = 64
LOG2E = math.log2(math.e)
GELU_C = math.sqrt(2 / math.pi)
GELU_K = 0.044715
VMEM = 60 * 2**20


def dot(a, b, ca, cb):
    return lax.dot_general(a, b, (((ca,), (cb,)), ((), ())), preferred_element_type=F32)


def nn(a, b):
    return dot(a, b, 1, 0)


def nt(a, b):
    return dot(a, b, 1, 1)


def tn(a, b):
    return dot(a, b, 0, 0)


def whole(shape):
    zeros = (0,) * len(shape)
    return pl.BlockSpec(shape, lambda i: zeros, pipeline_mode=pl.Buffered(1))


def params():
    return pltpu.CompilerParams(vmem_limit_bytes=VMEM)


def norm_rows(v):
    centred = v - jnp.mean(v, axis=-1, keepdims=True)
    inverse = lax.rsqrt(jnp.mean(centred * centred, axis=-1, keepdims=True) + 1e-05)
    return centred * inverse, inverse


def norm_back(g, normed, inverse):
    first = jnp.mean(g, axis=-1, keepdims=True)
    second = jnp.mean(g * normed, axis=-1, keepdims=True)
    return inverse * (g - first - normed * second)


def qkv_kernel(pieces, *refs):
    toks, (gain, w, x_out, ready_out, packed) = refs[:pieces], refs[pieces:]
    rows = toks[0].shape[0]

    @pl.when(pl.program_id(0) == 0)
    def _():
        for k in range(pieces):
            span = slice(k * rows, (k + 1) * rows)
            t = toks[k][...]
            x_out[span] = t
            ready_out[span] = (norm_rows(t.astype(F32))[0] * gain[...]).astype(BF16)

    packed[...] = nn(ready_out[...], w[...]).astype(BF16)


def qkv(toks, gain, w):
    rows, width = toks[0].shape
    length = rows * len(toks)
    cols = w.shape[1]
    block = min(1024, cols)
    return pl.pallas_call(
        functools.partial(qkv_kernel, len(toks)),
        grid=(cols // block,),
        in_specs=[whole((rows, width))] * len(toks)
        + [whole((1, width)), pl.BlockSpec((width, block), lambda i: (0, i))],
        out_specs=[
            whole((length, width)),
            whole((length, width)),
            pl.BlockSpec((length, block), lambda i: (0, i)),
        ],
        out_shape=[
            jax.ShapeDtypeStruct((length, width), BF16),
            jax.ShapeDtypeStruct((length, width), BF16),
            jax.ShapeDtypeStruct((length, cols), BF16),
        ],
        compiler_params=params(),
        name="norm_qkv",
    )(*toks, gain, w)


def split2(v):
    hi = v.astype(BF16)
    return hi, (v - hi.astype(F32)).astype(BF16)


def split3(v):
    a = v.astype(BF16).astype(F32)
    b = (v - a).astype(BF16).astype(F32)
    return a, b, v - a - b


def in_lanes(columns, first, rows):
    lane = lax.broadcasted_iota(jnp.int32, (rows, 128), 1)
    out = jnp.zeros((rows, 128), F32)
    for i, column in enumerate(columns):
        out = jnp.where(lane == first + i, column, out)
    return out.astype(BF16)


def lanes_between(rows, low, high):
    lane = lax.broadcasted_iota(jnp.int32, (rows, 128), 1)
    return ((lane >= low) & (lane < high)).astype(F32).astype(BF16)


def head_parts(p, h):
    base = 3 * HEAD * h
    return p[:, base : base + HEAD], p[:, base + HEAD : base + 2 * HEAD], p[:, base + 2 * HEAD : base + 3 * HEAD]


def attend_kernel(p_ref, o_ref, aux_ref, *, bq):
    length = p_ref.shape[0]

    def run(exact):
        mixed, auxes, low, high = [], [], [], []
        for h in range(2):
            q, k, v = head_parts(p_ref, h)
            scaled = q.astype(F32) * (LOG2E * HEAD**-0.5)
            qhi, qlo = split2(scaled)
            vv = jnp.concatenate([v, jnp.ones((length, HEAD), BF16)], axis=1)
            if exact:
                qq = jnp.concatenate([qhi, qlo], axis=1)
                kk = jnp.concatenate([k, k], axis=1)
            else:
                k32 = k.astype(F32)
                knorm = jnp.sqrt(jnp.max(jnp.sum(k32 * k32, axis=1, keepdims=True)))
                bound = jnp.sqrt(jnp.sum(scaled * scaled, axis=1, keepdims=True)) * knorm
                b1 = bound.astype(BF16).astype(F32)
                qq = jnp.concatenate([qhi, qlo, in_lanes([-b1], 0, length)], axis=1)
                kk = jnp.concatenate([k, k, lanes_between(length, 0, 1)], axis=1)
            parts, aux = [], []
            for i in range(length // bq):
                span = slice(i * bq, (i + 1) * bq)
                s = nt(qq[span], kk)
                if exact:
                    m = jnp.max(s, axis=1, keepdims=True)
                    s = s - m
                else:
                    m = b1[span]
                o = nn(jnp.exp2(s).astype(BF16), vv)
                total = o[:, HEAD : HEAD + 1]
                parts.append((o[:, :HEAD] * (1.0 / total)).astype(BF16))
                aux.append(in_lanes(split3(-(m + jnp.log2(total))), 4 * h, bq))
                low.append(jnp.min(total))
                high.append(jnp.max(total))
            mixed.append(jnp.concatenate(parts, axis=0))
            auxes.append(jnp.concatenate(aux, axis=0))
        o_ref[...] = jnp.concatenate(mixed, axis=1)
        aux_ref[...] = auxes[0] + auxes[1]
        return functools.reduce(jnp.minimum, low), functools.reduce(jnp.maximum, high)

    low, high = run(False)
    fine = (low > 2.0**-80) & (high < 2.0**80)

    @pl.when(jnp.logical_not(fine))
    def _():
        run(True)


def attend(packed):
    length, cols = packed.shape
    pairs = cols // (6 * HEAD)
    out = pl.BlockSpec((length, 2 * HEAD), lambda i: (0, i))
    shape = jax.ShapeDtypeStruct((length, pairs * 2 * HEAD), BF16)
    return pl.pallas_call(
        functools.partial(attend_kernel, bq=math.gcd(length, 256)),
        grid=(pairs,),
        in_specs=[pl.BlockSpec((length, 6 * HEAD), lambda i: (0, i))],
        out_specs=[out, out],
        out_shape=[shape, shape],
        compiler_params=params(),
        name="attend",
    )(packed)


def attend_back_math(p_ref, o_ref, aux_ref, do_ref, bq):
    length = p_ref.shape[0]
    aux = aux_ref[...]
    outs = []
    for h in range(2):
        q, k, v = head_parts(p_ref, h)
        do = do_ref[:, HEAD * h : HEAD * (h + 1)]
        o = o_ref[:, HEAD * h : HEAD * (h + 1)]
        qhi, qlo = split2(q.astype(F32) * (LOG2E * HEAD**-0.5))
        qq = jnp.concatenate([qhi, qlo, aux], axis=1)
        kk = jnp.concatenate([k, k, lanes_between(length, 4 * h, 4 * h + 3)], axis=1)
        minus = -jnp.sum(do.astype(F32) * o.astype(F32), axis=1, keepdims=True)
        dd = jnp.concatenate([do, in_lanes(split3(minus), 0, length)[:, :HEAD]], axis=1)
        vv = jnp.concatenate([v, lanes_between(length, 0, 3)[:, :HEAD]], axis=1)
        do_t, q_t = do.T, q.T
        dv_t = jnp.zeros((HEAD, length), F32)
        dk_t = jnp.zeros((HEAD, length), F32)
        dq = []
        for i in range(length // bq):
            span = slice(i * bq, (i + 1) * bq)
            p = jnp.exp2(nt(qq[span], kk))
            ds = (p * nt(dd[span], vv)).astype(BF16)
            dv_t = dv_t + nn(do_t[:, span], p.astype(BF16))
            dk_t = dk_t + nn(q_t[:, span], ds)
            dq.append((nn(ds, k) * HEAD**-0.5).astype(BF16))
        outs += [
            jnp.concatenate(dq, axis=0),
            (dk_t * HEAD**-0.5).astype(BF16).T,
            dv_t.astype(BF16).T,
        ]
    return jnp.concatenate(outs, axis=1)


def mlp_kernel(pieces, *refs):
    x, mixed, w_out, gain, alive = refs[:5]
    cots = refs[5 : 5 + pieces]
    w_up, hidden, ready, gout, act, slope, grad_down = refs[5 + pieces :]
    rows = cots[0].shape[0]

    @pl.when(pl.program_id(0) == 0)
    def _():
        for k in range(pieces):
            span = slice(k * rows, (k + 1) * rows)
            gout[span] = cots[k][...] * alive[...].astype(BF16)
            h = x[span].astype(F32) + nn(mixed[span], w_out[...])
            hidden[span] = h
            ready[span] = (norm_rows(h)[0] * gain[...]).astype(BF16)

    u = nn(ready[...], w_up[...])
    u2 = u * u
    t = jnp.tanh(u * (GELU_C + (GELU_C * GELU_K) * u2))
    half = 0.5 + 0.5 * t
    a = (u * half).astype(BF16)
    act[...] = a
    slope[...] = (half + u * (1 - t * t) * (0.5 * GELU_C + (1.5 * GELU_C * GELU_K) * u2)).astype(BF16)
    grad_down[...] = tn(a, gout[...]).astype(BF16)


def mlp(x, mixed, w_out, gain, alive, cots, w_up):
    length, width = x.shape
    inner = w_up.shape[1]
    rows = length // len(cots)
    block = min(1024, inner)
    cols = pl.BlockSpec((length, block), lambda i: (0, i))
    return pl.pallas_call(
        functools.partial(mlp_kernel, len(cots)),
        grid=(inner // block,),
        in_specs=[
            whole((length, width)),
            whole((length, width)),
            whole((width, width)),
            whole((1, width)),
            whole((1, width)),
        ]
        + [whole((rows, width))] * len(cots)
        + [pl.BlockSpec((width, block), lambda i: (0, i))],
        out_specs=[whole((length, width))] * 3 + [cols, cols, pl.BlockSpec((block, width), lambda i: (i, 0))],
        out_shape=[
            jax.ShapeDtypeStruct((length, width), F32),
            jax.ShapeDtypeStruct((length, width), BF16),
            jax.ShapeDtypeStruct((length, width), BF16),
            jax.ShapeDtypeStruct((length, inner), BF16),
            jax.ShapeDtypeStruct((length, inner), BF16),
            jax.ShapeDtypeStruct((inner, width), BF16),
        ],
        compiler_params=params(),
        name="mlp",
    )(x, mixed, w_out, gain, alive, *cots, w_up)


def mlp_back_kernel(
    gout, act, slope, w_down, w_up, ready, hidden, gain, mixed, w_out,
    out, grad_up, grad_hidden, grad_out, grad_mixed, table, out_sum, back_sum,
):
    i = pl.program_id(0)

    @pl.when(i == 0)
    def _():
        out_sum[...] = hidden[...]
        back_sum[...] = jnp.zeros_like(back_sum)

    gu = (nt(gout[...], w_down[...]) * slope[...].astype(F32)).astype(BF16)
    grad_up[...] = tn(ready[...], gu).astype(BF16)
    back_sum[...] += nt(gu, w_up[...])
    out_sum[...] += nn(act[...], w_down[...])

    @pl.when(i == pl.num_programs(0) - 1)
    def _():
        length = gout.shape[0]
        step = math.gcd(length, 256)
        total = jnp.zeros((1, gain.shape[1]), F32)
        for r in range(length // step):
            span = slice(r * step, (r + 1) * step)
            normed, inverse = norm_rows(hidden[span])
            g = back_sum[span]
            total = total + jnp.sum(g * normed, axis=0, keepdims=True)
            grad_hidden[span] = gout[span].astype(F32) + norm_back(g * gain[...], normed, inverse)
            out[span] = out_sum[span].astype(BF16)
        table[...] = total
        low = grad_hidden[...].astype(BF16)
        grad_mixed[...] = nt(low, w_out[...]).astype(BF16)
        grad_out[...] = tn(mixed[...], low).astype(BF16)


def mlp_back(gout, act, slope, w_down, w_up, ready, hidden, gain, mixed, w_out):
    length, width = gout.shape
    inner = w_up.shape[1]
    block = min(1024, inner)
    cols = pl.BlockSpec((length, block), lambda i: (0, i))
    square = whole((length, width))
    return pl.pallas_call(
        mlp_back_kernel,
        grid=(inner // block,),
        in_specs=[
            square,
            cols,
            cols,
            pl.BlockSpec((block, width), lambda i: (i, 0)),
            pl.BlockSpec((width, block), lambda i: (0, i)),
            square,
            square,
            whole((1, width)),
            square,
            whole((width, width)),
        ],
        out_specs=[
            square,
            pl.BlockSpec((width, block), lambda i: (0, i)),
            square,
            whole((width, width)),
            square,
            whole((1, width)),
        ],
        out_shape=[
            jax.ShapeDtypeStruct((length, width), BF16),
            jax.ShapeDtypeStruct((width, inner), BF16),
            jax.ShapeDtypeStruct((length, width), F32),
            jax.ShapeDtypeStruct((width, width), BF16),
            jax.ShapeDtypeStruct((length, width), BF16),
            jax.ShapeDtypeStruct((1, width), F32),
        ],
        scratch_shapes=[pltpu.VMEM((length, width), F32)] * 2,
        compiler_params=params(),
        name="mlp_back",
    )(gout, act, slope, w_down, w_up, ready, hidden, gain, mixed, w_out)


def attn_back_kernel(
    packed, mixed, aux, grad_mixed, w_qkv, ready, x, grad_hidden, gain,
    grad_qkv, grad_x, table, back_sum, *, bq,
):
    i = pl.program_id(0)

    @pl.when(i == 0)
    def _():
        back_sum[...] = jnp.zeros_like(back_sum)

    gp = attend_back_math(packed, mixed, aux, grad_mixed, bq)
    grad_qkv[...] = tn(ready[...], gp).astype(BF16)
    back_sum[...] += nt(gp, w_qkv[...])

    @pl.when(i == pl.num_programs(0) - 1)
    def _():
        length = x.shape[0]
        step = math.gcd(length, 256)
        total = jnp.zeros((1, gain.shape[1]), F32)
        for r in range(length // step):
            span = slice(r * step, (r + 1) * step)
            normed, inverse = norm_rows(x[span].astype(F32))
            g = back_sum[span]
            total = total + jnp.sum(g * normed, axis=0, keepdims=True)
            grad_x[span] = (grad_hidden[span] + norm_back(g * gain[...], normed, inverse)).astype(BF16)
        table[...] = total


def attn_back(packed, mixed, aux, grad_mixed, w_qkv, ready, x, grad_hidden, gain):
    length, width = x.shape
    cols = packed.shape[1]
    pairs = cols // (6 * HEAD)
    pair = pl.BlockSpec((length, 2 * HEAD), lambda i: (0, i))
    square = whole((length, width))
    return pl.pallas_call(
        functools.partial(attn_back_kernel, bq=math.gcd(length, 256)),
        grid=(pairs,),
        in_specs=[
            pl.BlockSpec((length, 6 * HEAD), lambda i: (0, i)),
            pair,
            pair,
            pair,
            pl.BlockSpec((width, 6 * HEAD), lambda i: (0, i)),
            square,
            square,
            square,
            whole((1, width)),
        ],
        out_specs=[
            pl.BlockSpec((width, 6 * HEAD), lambda i: (0, i)),
            square,
            whole((1, width)),
        ],
        out_shape=[
            jax.ShapeDtypeStruct((width, cols), BF16),
            jax.ShapeDtypeStruct((length, width), BF16),
            jax.ShapeDtypeStruct((1, width), F32),
        ],
        scratch_shapes=[pltpu.VMEM((length, width), F32)],
        compiler_params=params(),
        name="attn_back",
    )(packed, mixed, aux, grad_mixed, w_qkv, ready, x, grad_hidden, gain)


def exchange(pieces, me, ways):
    return [pieces[0]] + [
        lax.ppermute(pieces[k], "seq", [(s, s ^ k) for s in range(ways)]) for k in range(1, ways)
    ]


def by_partner(slots, me, ways):
    return [lax.dynamic_index_in_dim(slots, me ^ k, 0, keepdims=False) for k in range(ways)]


def to_slots(pieces, me, ways):
    stacked = jnp.stack(pieces)
    return jnp.take(stacked, jnp.arange(ways) ^ me, axis=0)


def body(tokens, cotangent, bins, live_count, w_qkv, w_out, w_up, w_down, gain_attn, gain_mlp):
    slots, rows, width = tokens.shape
    ways = lax.axis_size("seq")
    me = lax.axis_index("seq")
    toks = exchange(by_partner(tokens, me, ways), me, ways)
    cots = exchange(by_partner(cotangent, me, ways), me, ways)
    my_bin = lax.dynamic_index_in_dim(bins, me, 0)
    row_attn = lax.dynamic_slice_in_dim(gain_attn, my_bin[0], 1, 0)
    row_mlp = lax.dynamic_slice_in_dim(gain_mlp, my_bin[0], 1, 0)
    alive = jnp.broadcast_to((me < live_count[0]).astype(F32), (1, width))

    x, ready_attn, packed = qkv(toks, row_attn, w_qkv)
    mixed, aux = attend(packed)
    hidden, ready_mlp, gout, act, slope, grad_down = mlp(x, mixed, w_out, row_mlp, alive, cots, w_up)
    out, grad_up, grad_hidden, grad_out, grad_mixed, sum_mlp = mlp_back(
        gout, act, slope, w_down, w_up, ready_mlp, hidden, row_mlp, mixed, w_out
    )
    grad_qkv, grad_x, sum_attn = attn_back(
        packed, mixed, aux, grad_mixed, w_qkv, ready_attn, x, grad_hidden, row_attn
    )

    def back_to_slots(rows_out):
        parts = rows_out.reshape(ways, rows, width)
        return to_slots(exchange([parts[k] for k in range(ways)], me, ways), me, ways)

    output = back_to_slots(out)
    grad_tokens = back_to_slots(grad_x).astype(F32)
    onehot = (jnp.arange(gain_attn.shape[0], dtype=jnp.int32) == my_bin[0]).astype(F32)[:, None]

    def total(v, low):
        share = lax.psum_scatter(v, "batch", scatter_dimension=0, tiled=True)
        return lax.psum(share.astype(low), "seq").astype(F32)

    return (
        output,
        grad_tokens,
        total(grad_qkv, BF16),
        total(grad_out, BF16),
        total(grad_up, BF16),
        total(grad_down, BF16),
        total(onehot * sum_attn, F32),
        total(onehot * sum_mlp, F32),
    )


def solution(mesh):
    placed = (
        P("batch", "seq", None),
        P("batch", "seq", None),
        P("batch"),
        P("batch"),
        P(),
        P(),
        P(),
        P(),
        P(),
        P(),
    )
    return jax.shard_map(
        body,
        mesh=mesh,
        in_specs=placed,
        out_specs=(
            P("batch", "seq", None),
            P("batch", "seq", None),
            P("batch", None),
            P("batch", None),
            P("batch", None),
            P("batch", None),
            P("batch", None),
            P("batch", None),
        ),
        check_vma=False,
    )
```

```python
import functools
import math

import jax
import jax.numpy as jnp
from jax import lax
from jax.experimental import pallas as pl
from jax.experimental.pallas import tpu as pltpu
from jax.sharding import PartitionSpec as P

F32 = jnp.float32
BF16 = jnp.bfloat16
HEAD = 64
LOG2E = math.log2(math.e)
GELU_C = math.sqrt(2 / math.pi)
GELU_K = 0.044715
VMEM = 60 * 2**20


def dot(a, b, ca, cb):
    return lax.dot_general(a, b, (((ca,), (cb,)), ((), ())), preferred_element_type=F32)


def nn(a, b):
    return dot(a, b, 1, 0)


def nt(a, b):
    return dot(a, b, 1, 1)


def tn(a, b):
    return dot(a, b, 0, 0)


def whole(shape):
    zeros = (0,) * len(shape)
    return pl.BlockSpec(shape, lambda i: zeros, pipeline_mode=pl.Buffered(1))


def params():
    return pltpu.CompilerParams(vmem_limit_bytes=VMEM)


def norm_rows(v):
    centred = v - jnp.mean(v, axis=-1, keepdims=True)
    inverse = lax.rsqrt(jnp.mean(centred * centred, axis=-1, keepdims=True) + 1e-05)
    return centred * inverse, inverse


def norm_back(g, normed, inverse):
    first = jnp.mean(g, axis=-1, keepdims=True)
    second = jnp.mean(g * normed, axis=-1, keepdims=True)
    return inverse * (g - first - normed * second)


def qkv_kernel(pieces, *refs):
    toks, (gain, w, x_out, ready_out, packed) = refs[:pieces], refs[pieces:]
    rows = toks[0].shape[0]

    @pl.when(pl.program_id(0) == 0)
    def _():
        for k in range(pieces):
            span = slice(k * rows, (k + 1) * rows)
            t = toks[k][...]
            x_out[span] = t
            ready_out[span] = (norm_rows(t.astype(F32))[0] * gain[...]).astype(BF16)

    packed[...] = nn(ready_out[...], w[...]).astype(BF16)


def qkv(toks, gain, w):
    rows, width = toks[0].shape
    length = rows * len(toks)
    cols = w.shape[1]
    block = min(1024, cols)
    return pl.pallas_call(
        functools.partial(qkv_kernel, len(toks)),
        grid=(cols // block,),
        in_specs=[whole((rows, width))] * len(toks)
        + [whole((1, width)), pl.BlockSpec((width, block), lambda i: (0, i))],
        out_specs=[
            whole((length, width)),
            whole((length, width)),
            pl.BlockSpec((length, block), lambda i: (0, i)),
        ],
        out_shape=[
            jax.ShapeDtypeStruct((length, width), BF16),
            jax.ShapeDtypeStruct((length, width), BF16),
            jax.ShapeDtypeStruct((length, cols), BF16),
        ],
        compiler_params=params(),
        name="norm_qkv",
    )(*toks, gain, w)


def split2(v):
    hi = v.astype(BF16)
    return hi, (v - hi.astype(F32)).astype(BF16)


def split3(v):
    a = v.astype(BF16).astype(F32)
    b = (v - a).astype(BF16).astype(F32)
    return a, b, v - a - b


def in_lanes(columns, first, rows):
    lane = lax.broadcasted_iota(jnp.int32, (rows, 128), 1)
    out = jnp.zeros((rows, 128), F32)
    for i, column in enumerate(columns):
        out = jnp.where(lane == first + i, column, out)
    return out.astype(BF16)


def lanes_between(rows, low, high):
    lane = lax.broadcasted_iota(jnp.int32, (rows, 128), 1)
    return ((lane >= low) & (lane < high)).astype(F32).astype(BF16)


def head_parts(p, h):
    base = 3 * HEAD * h
    return p[:, base : base + HEAD], p[:, base + HEAD : base + 2 * HEAD], p[:, base + 2 * HEAD : base + 3 * HEAD]


def attend_kernel(p_ref, o_ref, aux_ref, *, bq):
    length = p_ref.shape[0]

    def run(exact):
        mixed, auxes, low, high = [], [], [], []
        for h in range(2):
            q, k, v = head_parts(p_ref, h)
            scaled = q.astype(F32) * (LOG2E * HEAD**-0.5)
            qhi, qlo = split2(scaled)
            vv = jnp.concatenate([v, jnp.ones((length, HEAD), BF16)], axis=1)
            if exact:
                qq = jnp.concatenate([qhi, qlo], axis=1)
                kk = jnp.concatenate([k, k], axis=1)
            else:
                k32 = k.astype(F32)
                knorm = jnp.sqrt(jnp.max(jnp.sum(k32 * k32, axis=1, keepdims=True)))
                bound = jnp.sqrt(jnp.sum(scaled * scaled, axis=1, keepdims=True)) * knorm
                b1 = bound.astype(BF16).astype(F32)
                qq = jnp.concatenate([qhi, qlo, in_lanes([-b1], 0, length)], axis=1)
                kk = jnp.concatenate([k, k, lanes_between(length, 0, 1)], axis=1)
            parts, aux = [], []
            for i in range(length // bq):
                span = slice(i * bq, (i + 1) * bq)
                s = nt(qq[span], kk)
                if exact:
                    m = jnp.max(s, axis=1, keepdims=True)
                    s = s - m
                else:
                    m = b1[span]
                o = nn(jnp.exp2(s).astype(BF16), vv)
                total = o[:, HEAD : HEAD + 1]
                parts.append((o[:, :HEAD] * (1.0 / total)).astype(BF16))
                aux.append(in_lanes(split3(-(m + jnp.log2(total))), 4 * h, bq))
                low.append(jnp.min(total))
                high.append(jnp.max(total))
            mixed.append(jnp.concatenate(parts, axis=0))
            auxes.append(jnp.concatenate(aux, axis=0))
        o_ref[...] = jnp.concatenate(mixed, axis=1)
        aux_ref[...] = auxes[0] + auxes[1]
        return functools.reduce(jnp.minimum, low), functools.reduce(jnp.maximum, high)

    low, high = run(False)
    fine = (low > 2.0**-80) & (high < 2.0**80)

    @pl.when(jnp.logical_not(fine))
    def _():
        run(True)


def attend(packed):
    length, cols = packed.shape
    pairs = cols // (6 * HEAD)
    out = pl.BlockSpec((length, 2 * HEAD), lambda i: (0, i))
    shape = jax.ShapeDtypeStruct((length, pairs * 2 * HEAD), BF16)
    return pl.pallas_call(
        functools.partial(attend_kernel, bq=math.gcd(length, 256)),
        grid=(pairs,),
        in_specs=[pl.BlockSpec((length, 6 * HEAD), lambda i: (0, i))],
        out_specs=[out, out],
        out_shape=[shape, shape],
        compiler_params=params(),
        name="attend",
    )(packed)


def attend_back_math(p_ref, o_ref, aux_ref, do_ref, bq):
    length = p_ref.shape[0]
    aux = aux_ref[...]
    outs = []
    for h in range(2):
        q, k, v = head_parts(p_ref, h)
        do = do_ref[:, HEAD * h : HEAD * (h + 1)]
        o = o_ref[:, HEAD * h : HEAD * (h + 1)]
        qhi, qlo = split2(q.astype(F32) * (LOG2E * HEAD**-0.5))
        qq = jnp.concatenate([qhi, qlo, aux], axis=1)
        kk = jnp.concatenate([k, k, lanes_between(length, 4 * h, 4 * h + 3)], axis=1)
        minus = -jnp.sum(do.astype(F32) * o.astype(F32), axis=1, keepdims=True)
        dd = jnp.concatenate([do, in_lanes(split3(minus), 0, length)[:, :HEAD]], axis=1)
        vv = jnp.concatenate([v, lanes_between(length, 0, 3)[:, :HEAD]], axis=1)
        do_t, q_t = do.T, q.T
        dv_t = jnp.zeros((HEAD, length), F32)
        dk_t = jnp.zeros((HEAD, length), F32)
        dq = []
        for i in range(length // bq):
            span = slice(i * bq, (i + 1) * bq)
            p = jnp.exp2(nt(qq[span], kk))
            ds = (p * nt(dd[span], vv)).astype(BF16)
            dv_t = dv_t + nn(do_t[:, span], p.astype(BF16))
            dk_t = dk_t + nn(q_t[:, span], ds)
            dq.append((nn(ds, k) * HEAD**-0.5).astype(BF16))
        outs += [
            jnp.concatenate(dq, axis=0),
            (dk_t * HEAD**-0.5).astype(BF16).T,
            dv_t.astype(BF16).T,
        ]
    return jnp.concatenate(outs, axis=1)


def mlp_kernel(pieces, *refs):
    x, mixed, w_out, gain, alive = refs[:5]
    cots = refs[5 : 5 + pieces]
    w_up, hidden, ready, gout, act, slope, grad_down = refs[5 + pieces :]
    rows = cots[0].shape[0]

    @pl.when(pl.program_id(0) == 0)
    def _():
        for k in range(pieces):
            span = slice(k * rows, (k + 1) * rows)
            gout[span] = cots[k][...] * alive[...].astype(BF16)
            h = x[span].astype(F32) + nn(mixed[span], w_out[...])
            hidden[span] = h
            ready[span] = (norm_rows(h)[0] * gain[...]).astype(BF16)

    u = nn(ready[...], w_up[...])
    u2 = u * u
    t = jnp.tanh(u * (GELU_C + (GELU_C * GELU_K) * u2))
    half = 0.5 + 0.5 * t
    a = (u * half).astype(BF16)
    act[...] = a
    slope[...] = (half + u * (1 - t * t) * (0.5 * GELU_C + (1.5 * GELU_C * GELU_K) * u2)).astype(BF16)
    grad_down[...] = tn(a, gout[...]).astype(BF16)


def mlp(x, mixed, w_out, gain, alive, cots, w_up):
    length, width = x.shape
    inner = w_up.shape[1]
    rows = length // len(cots)
    block = min(1024, inner)
    cols = pl.BlockSpec((length, block), lambda i: (0, i))
    return pl.pallas_call(
        functools.partial(mlp_kernel, len(cots)),
        grid=(inner // block,),
        in_specs=[
            whole((length, width)),
            whole((length, width)),
            whole((width, width)),
            whole((1, width)),
            whole((1, width)),
        ]
        + [whole((rows, width))] * len(cots)
        + [pl.BlockSpec((width, block), lambda i: (0, i))],
        out_specs=[whole((length, width))] * 3 + [cols, cols, pl.BlockSpec((block, width), lambda i: (i, 0))],
        out_shape=[
            jax.ShapeDtypeStruct((length, width), F32),
            jax.ShapeDtypeStruct((length, width), BF16),
            jax.ShapeDtypeStruct((length, width), BF16),
            jax.ShapeDtypeStruct((length, inner), BF16),
            jax.ShapeDtypeStruct((length, inner), BF16),
            jax.ShapeDtypeStruct((inner, width), BF16),
        ],
        compiler_params=params(),
        name="mlp",
    )(x, mixed, w_out, gain, alive, *cots, w_up)


def mlp_back_kernel(side, *refs):
    jobs = len(side.jobs)
    gout, act, slope, w_down, w_up, ready, hidden, gain, mixed, w_out = refs[:10]
    refs = refs[10:]
    sources, refs = refs[:jobs], refs[jobs:]
    out, grad_up, grad_hidden, grad_out, grad_mixed, table = refs[:6]
    refs = refs[6:]
    finals, refs = refs[:jobs], refs[jobs:]
    out_sum, back_sum, mixed_here, w_here, late = refs[:5]
    side.bind(sources, finals, refs[5:])
    i = pl.program_id(0)
    last = pl.num_programs(0) - 1
    loads = [
        pltpu.make_async_copy(hidden, grad_hidden, late.at[0]),
        pltpu.make_async_copy(mixed, mixed_here, late.at[1]),
        pltpu.make_async_copy(w_out, w_here, late.at[2]),
    ]

    @pl.when(i == 0)
    def _():
        for load in loads:
            load.start()
        out_sum[...] = jnp.zeros_like(out_sum)
        back_sum[...] = jnp.zeros_like(back_sum)

    side.at_step(i, pl.num_programs(0))
    gu = (nt(gout[...], w_down[...]) * slope[...].astype(F32)).astype(BF16)
    grad_up[...] = tn(ready[...], gu).astype(BF16)
    back_sum[...] += nt(gu, w_up[...])
    out_sum[...] += nn(act[...], w_down[...])

    @pl.when(i == last)
    def _():
        for load in loads:
            load.wait()
        length = gout.shape[0]
        step = math.gcd(length, 256)
        total = jnp.zeros((1, gain.shape[1]), F32)
        for r in range(length // step):
            span = slice(r * step, (r + 1) * step)
            h = grad_hidden[span]
            out[span] = (h + out_sum[span]).astype(BF16)
            normed, inverse = norm_rows(h)
            g = back_sum[span]
            total = total + jnp.sum(g * normed, axis=0, keepdims=True)
            grad_hidden[span] = gout[span].astype(F32) + norm_back(g * gain[...], normed, inverse)
        table[...] = total
        low = grad_hidden[...].astype(BF16)
        grad_mixed[...] = nt(low, w_here[...]).astype(BF16)
        grad_out[...] = tn(mixed_here[...], low).astype(BF16)
        side.at_end()


def mlp_back(gout, act, slope, w_down, w_up, ready, hidden, gain, mixed, w_out, side):
    length, width = gout.shape
    inner = w_up.shape[1]
    block = min(512, inner)
    cols = pl.BlockSpec((length, block), lambda i: (0, i))
    square = whole((length, width))
    remote = pl.BlockSpec(memory_space=pl.ANY)
    return pl.pallas_call(
        functools.partial(mlp_back_kernel, side),
        grid=(inner // block,),
        in_specs=[
            square,
            cols,
            cols,
            pl.BlockSpec((block, width), lambda i: (i, 0)),
            pl.BlockSpec((width, block), lambda i: (0, i)),
            square,
            remote,
            whole((1, width)),
            remote,
            remote,
        ]
        + side.in_specs(),
        out_specs=[
            square,
            pl.BlockSpec((width, block), lambda i: (0, i)),
            square,
            whole((width, width)),
            square,
            whole((1, width)),
        ]
        + side.out_specs(),
        out_shape=[
            jax.ShapeDtypeStruct((length, width), BF16),
            jax.ShapeDtypeStruct((width, inner), BF16),
            jax.ShapeDtypeStruct((length, width), F32),
            jax.ShapeDtypeStruct((width, width), BF16),
            jax.ShapeDtypeStruct((length, width), BF16),
            jax.ShapeDtypeStruct((1, width), F32),
        ]
        + side.out_shape(),
        scratch_shapes=[pltpu.VMEM((length, width), F32)] * 2
        + [pltpu.VMEM((length, width), BF16), pltpu.VMEM((width, width), BF16), pltpu.SemaphoreType.DMA((3,))]
        + side.scratch(),
        compiler_params=side.params(),
        name="mlp_back",
    )(gout, act, slope, w_down, w_up, ready, hidden, gain, mixed, w_out, *side.sources)


def attn_back_kernel(side, bq, *refs):
    jobs = len(side.jobs)
    packed, mixed, aux, grad_mixed, w_qkv, ready, x, grad_hidden, gain = refs[:9]
    refs = refs[9:]
    sources, refs = refs[:jobs], refs[jobs:]
    grad_qkv, grad_x, table = refs[:3]
    refs = refs[3:]
    finals, refs = refs[:jobs], refs[jobs:]
    back_sum = refs[0]
    side.bind(sources, finals, refs[1:])
    i = pl.program_id(0)

    @pl.when(i == 0)
    def _():
        back_sum[...] = jnp.zeros_like(back_sum)

    side.at_step(i, pl.num_programs(0))
    gp = attend_back_math(packed, mixed, aux, grad_mixed, bq)
    grad_qkv[...] = tn(ready[...], gp).astype(BF16)
    back_sum[...] += nt(gp, w_qkv[...])

    @pl.when(i == pl.num_programs(0) - 1)
    def _():
        length = x.shape[0]
        step = math.gcd(length, 256)
        total = jnp.zeros((1, gain.shape[1]), F32)
        for r in range(length // step):
            span = slice(r * step, (r + 1) * step)
            normed, inverse = norm_rows(x[span].astype(F32))
            g = back_sum[span]
            total = total + jnp.sum(g * normed, axis=0, keepdims=True)
            grad_x[span] = (grad_hidden[span] + norm_back(g * gain[...], normed, inverse)).astype(BF16)
        table[...] = total
        side.at_end()


def attn_back(packed, mixed, aux, grad_mixed, w_qkv, ready, x, grad_hidden, gain, side):
    length, width = x.shape
    cols = packed.shape[1]
    pairs = cols // (6 * HEAD)
    pair = pl.BlockSpec((length, 2 * HEAD), lambda i: (0, i))
    square = whole((length, width))
    return pl.pallas_call(
        functools.partial(attn_back_kernel, side, math.gcd(length, 256)),
        grid=(pairs,),
        in_specs=[
            pl.BlockSpec((length, 6 * HEAD), lambda i: (0, i)),
            pair,
            pair,
            pair,
            pl.BlockSpec((width, 6 * HEAD), lambda i: (0, i)),
            square,
            square,
            square,
            whole((1, width)),
        ]
        + side.in_specs(),
        out_specs=[
            pl.BlockSpec((width, 6 * HEAD), lambda i: (0, i)),
            square,
            whole((1, width)),
        ]
        + side.out_specs(),
        out_shape=[
            jax.ShapeDtypeStruct((width, cols), BF16),
            jax.ShapeDtypeStruct((length, width), BF16),
            jax.ShapeDtypeStruct((1, width), F32),
        ]
        + side.out_shape(),
        scratch_shapes=[pltpu.VMEM((length, width), F32)] + side.scratch(),
        compiler_params=side.params(),
        name="attn_back",
    )(packed, mixed, aux, grad_mixed, w_qkv, ready, x, grad_hidden, gain, *side.sources)


MESH = pl.DeviceIdType.MESH


class Place:
    def __init__(self, ways, line):
        self.ways, self.line = ways, line
        self.me = lax.axis_index("seq")
        self.b = lax.axis_index("batch")
        self.core = lax.rem(self.b, 2)
        self.z = self.b // 2

    def other_core(self):
        return {"batch": self.b + 1 - 2 * self.core}

    def along(self, step):
        return {"batch": self.b + 2 * step}

    def plane(self, k):
        return {"seq": self.partner(k)}

    def partner(self, k):
        out = self.me
        for bit in range(k.bit_length()):
            if k >> bit & 1:
                out = out + (1 << bit) * (1 - 2 * lax.rem(self.me // (1 << bit), 2))
        return out

    def greet(self):
        barrier = pltpu.get_barrier_semaphore()

        def tell(where):
            pl.semaphore_signal(barrier, inc=1, device_id=where, device_id_type=MESH)

        tell(self.other_core())
        for k in range(1, self.ways):
            tell(self.plane(k))

        @pl.when(self.z > 0)
        def _():
            tell(self.along(-1))

        @pl.when(self.z < self.line - 1)
        def _():
            tell(self.along(1))

        ends = (self.z == 0).astype(jnp.int32) + (self.z == self.line - 1).astype(jnp.int32)
        pl.semaphore_wait(barrier, self.ways + 2 - ends)


def add_rows(dst, srcs, rows, step=16):
    def one(i, carry):
        at = pl.multiple_of(i * step, step)
        total = dst(at)[...].astype(F32)
        for src in srcs:
            total = total + src(at)[...].astype(F32)
        dst(at)[...] = total.astype(BF16)
        return carry

    lax.fori_loop(0, rows // step, one, 0)


class Reduce:
    def __init__(self, ways, line, rows, cols, split):
        self.ways, self.line, self.rows, self.cols, self.split = ways, line, rows, cols, split
        self.part = cols // ways
        self.last = 8

    def out(self):
        shape = (self.rows, self.cols)
        return whole(shape), jax.ShapeDtypeStruct(shape, BF16)

    def scratch(self):
        line, rows, cols, split, part = self.line, self.rows, self.cols, self.split, self.part
        hops, rest, others = line - 1, rows - split, self.ways - 1
        shapes = [pltpu.VMEM((line, rows, cols), BF16), pltpu.VMEM((line, rows, cols), BF16)]
        if rest:
            shapes += [
                pltpu.VMEM((hops, rest, cols), BF16),
                pltpu.VMEM((hops, rest, cols), BF16),
                pltpu.VMEM((others, rest, part), BF16),
            ]
        if split:
            shapes += [
                pltpu.VMEM((others, line, split, part), BF16),
                pltpu.VMEM((hops, split, part), BF16),
                pltpu.VMEM((hops, split, part), BF16),
            ]
        n = 2 * (others * 2 + 2 * hops) + 2
        return shapes + [
            pltpu.VMEM((rows, cols), BF16),
            pltpu.SemaphoreType.DMA((n,)),
            pltpu.SemaphoreType.DMA((n,)),
        ]

    def bind(self, place, source, final, refs):
        refs = list(refs)
        self.place, self.source, self.result = place, source, final
        self.own, self.near = refs[:2]
        refs = refs[2:]
        if self.rows - self.split:
            self.z_right, self.z_left, self.z_part = refs[:3]
            refs = refs[3:]
        if self.split:
            self.x_part, self.x_right, self.x_left = refs[:3]
            refs = refs[3:]
        self.final, self.send, self.recv = refs
        self.ids = {}
        return self

    def sem(self, key):
        if key not in self.ids:
            self.ids[key] = len(self.ids) + 1
        return self.ids[key]

    def copy(self, key, src, dst, where):
        n = self.sem(key)
        return pltpu.make_async_remote_copy(
            src_ref=src, dst_ref=dst, send_sem=self.send.at[n], recv_sem=self.recv.at[n],
            device_id=where, device_id_type=MESH,
        )

    def span(self, quarter):
        return pl.ds(pl.multiple_of(quarter * self.part, self.part), self.part)

    def core_copy(self):
        p = self.place
        return self.copy("core", self.source.at[:, 1 - p.core], self.near, p.other_core())

    def own_copy(self):
        p = self.place
        return pltpu.make_async_copy(self.source.at[:, p.core], self.own, self.send.at[0])

    def x_rs(self, k):
        p = self.place
        return self.copy(
            ("x_rs", k),
            self.own.at[:, pl.ds(0, self.split), self.span(p.partner(k))],
            self.x_part.at[k - 1],
            p.plane(k),
        )

    def x_ag(self, k):
        p = self.place
        here = (pl.ds(0, self.split), self.span(p.me))
        return self.copy(("x_ag", k), self.final.at[here], self.final.at[here], p.plane(k))

    def x_ag_in(self, k):
        p = self.place
        here = (pl.ds(0, self.split), self.span(p.partner(k)))
        return self.copy(("x_ag", k), self.final.at[here], self.final.at[here], p.plane(k))

    def z_rs(self, k):
        p = self.place
        return self.copy(
            ("z_rs", k),
            self.own.at[p.z, pl.ds(self.split, self.rows - self.split), self.span(p.partner(k))],
            self.z_part.at[k - 1],
            p.plane(k),
        )

    def z_ag(self, k, quarter):
        here = (pl.ds(self.split, self.rows - self.split), self.span(quarter))
        return self.copy(("z_ag", k), self.final.at[here], self.final.at[here], self.place.plane(k))

    def line_row(self, kind, j):
        if kind == "x":
            return self.own.at[j, pl.ds(0, self.split), self.span(self.place.me)]
        return self.own.at[j, pl.ds(self.split, self.rows - self.split)]

    def line_in(self, kind, right):
        if kind == "x":
            return self.x_right if right else self.x_left
        return self.z_right if right else self.z_left

    def line_copy(self, kind, right, t, j):
        return self.copy(
            (kind, right, t),
            self.line_row(kind, j),
            self.line_in(kind, right).at[t - 1],
            self.place.along(1 if right else -1),
        )

    def line_step(self, kind, t):
        p, line = self.place, self.line
        rows = self.split if kind == "x" else self.rows - self.split
        for right in (True, False):
            at = p.z if right else line - 1 - p.z
            if t < line:
                j = line + p.z - t if right else p.z + t - line

                @pl.when(at <= t - 1)
                def _(right=right, at=at, j=j):
                    if t > 1:

                        @pl.when((at >= 1) & (at <= t - 1))
                        def _():
                            self.line_arrive(kind, right, t - 1, j, rows)

                    self.line_copy(kind, right, t, j).start()

            else:

                @pl.when(at >= 1)
                def _(right=right):
                    self.line_arrive(kind, right, t - 1, p.z, rows)

    def line_arrive(self, kind, right, t, j, rows):
        p = self.place
        self.copy(
            (kind, right, t),
            self.line_row(kind, j),
            self.line_in(kind, right).at[t - 1],
            p.along(-1 if right else 1),
        ).wait_recv()
        buffer = self.line_in(kind, right)
        if kind == "x":
            mine = lambda r: self.own.at[j, pl.ds(r, 16), self.span(p.me)]
        else:
            mine = lambda r: self.own.at[j, pl.ds(self.split + r, 16)]
        add_rows(mine, [lambda r: buffer.at[t - 1, pl.ds(r, 16)]], rows)

    def line_sent(self, kind):
        p, line = self.place, self.line
        for t in range(1, line):
            for right in (True, False):
                at = p.z if right else line - 1 - p.z

                @pl.when(at <= t - 1)
                def _(right=right, t=t):
                    self.line_copy(kind, right, t, p.z).wait_send()

    def finish_part(self, first, rows, buffers, j):
        p = self.place

        def one(i, carry):
            r = pl.multiple_of(i * 16, 16)
            total = self.own[j, pl.ds(first + r, 16), self.span(p.me)].astype(F32)
            for buffer in buffers:
                total = total + buffer(r)[...].astype(F32)
            self.final[pl.ds(first + r, 16), self.span(p.me)] = total.astype(BF16)
            return carry

        lax.fori_loop(0, rows // 16, one, 0)

    def phase(self, n):
        p, others = self.place, range(1, self.ways)
        rest = self.rows - self.split
        if n == 0:
            self.own_copy().start()
            self.core_copy().start()
        if n == 1:
            self.own_copy().wait()
            self.core_copy().wait_recv()

            def one(z, carry):
                add_rows(
                    lambda r: self.own.at[z, pl.ds(r, 16)],
                    [lambda r: self.near.at[z, pl.ds(r, 16)]],
                    self.rows,
                )
                return carry

            lax.fori_loop(0, self.line, one, 0)
            if self.split:
                for k in others:
                    self.x_rs(k).start()
        if rest and 1 <= n <= 4:
            self.line_step("z", n)
        if n == 4:
            if rest:
                for k in others:
                    self.z_rs(k).start()
            if self.split:
                for k in others:
                    self.x_rs(k).wait_recv()

                def sum_x(z, carry):
                    add_rows(
                        lambda r: self.own.at[z, pl.ds(r, 16), self.span(p.me)],
                        [
                            functools.partial(lambda k, r: self.x_part.at[k - 1, z, pl.ds(r, 16)], k)
                            for k in others
                        ],
                        self.split,
                    )
                    return carry

                lax.fori_loop(0, self.line, sum_x, 0)
        if self.split and 4 <= n <= 7:
            self.line_step("x", n - 3)
        if n == 5 and rest:
            for k in others:
                self.z_rs(k).wait_recv()
            self.finish_part(
                self.split,
                rest,
                [functools.partial(lambda k, r: self.z_part.at[k - 1, pl.ds(r, 16)], k) for k in others],
                p.z,
            )
            for k in others:
                self.z_ag(k, p.me).start()
        if n == 7 and self.split:
            self.finish_part(0, self.split, [], p.z)
            for k in others:
                self.x_ag(k).start()
        if n == 8:
            for k in others:
                if rest:
                    self.z_ag(k, p.partner(k)).wait_recv()
                    self.z_ag(k, p.me).wait_send()
                    self.z_rs(k).wait_send()
                if self.split:
                    self.x_ag_in(k).wait_recv()
                    self.x_ag(k).wait_send()
                    self.x_rs(k).wait_send()
            if rest:
                self.line_sent("z")
            if self.split:
                self.line_sent("x")
            self.core_copy().wait_send()
            self.result[...] = self.final[...]


class Swap:
    last = 8

    def __init__(self, ways, rows, cols):
        self.ways, self.shape = ways, (ways, rows, cols)

    def scratch(self):
        return [pltpu.SemaphoreType.DMA((self.ways,)), pltpu.SemaphoreType.DMA((self.ways,))]

    def out(self):
        return pl.BlockSpec(memory_space=pl.ANY), jax.ShapeDtypeStruct(self.shape, BF16)

    def bind(self, place, source, final, refs):
        self.place, self.source, self.final = place, source, final
        self.send, self.recv = refs
        return self

    def copy(self, k, slot):
        return pltpu.make_async_remote_copy(
            src_ref=self.source.at[k], dst_ref=self.final.at[slot],
            send_sem=self.send.at[k], recv_sem=self.recv.at[k],
            device_id=self.place.plane(k), device_id_type=MESH,
        )

    def stay(self):
        return pltpu.make_async_copy(self.source.at[0], self.final.at[self.place.me], self.send.at[0])

    def phase(self, n):
        p = self.place
        if n == 0:
            self.stay().start()
            for k in range(1, self.ways):
                self.copy(k, p.me).start()
        if n == self.last:
            self.stay().wait()
            for k in range(1, self.ways):
                self.copy(k, p.partner(k)).wait_recv()
                self.copy(k, p.me).wait_send()


class Side:
    steps = 9

    def __init__(self, jobs, sources, ways, line, ident):
        self.jobs, self.sources, self.ways, self.line, self.ident = jobs, sources, ways, line, ident

    def in_specs(self):
        return [pl.BlockSpec(memory_space=pl.ANY)] * len(self.jobs)

    def out_specs(self):
        return [job.out()[0] for job in self.jobs]

    def out_shape(self):
        return [job.out()[1] for job in self.jobs]

    def scratch(self):
        return [s for job in self.jobs for s in job.scratch()]

    def params(self):
        if not self.jobs:
            return pltpu.CompilerParams(vmem_limit_bytes=VMEM)
        return pltpu.CompilerParams(vmem_limit_bytes=VMEM, collective_id=self.ident, has_side_effects=True)

    def bind(self, sources, finals, refs):
        if not self.jobs:
            return
        refs = list(refs)
        self.place = Place(self.ways, self.line)
        for job, source, final in zip(self.jobs, sources, finals):
            many = len(job.scratch())
            job.bind(self.place, source, final, refs[:many])
            refs = refs[many:]

    def phase(self, n):
        if not self.jobs:
            return
        if n == 0:
            self.place.greet()
        for job in self.jobs:
            job.phase(n)

    def at_step(self, i, steps):
        if not self.jobs:
            return
        for n in range(self.steps - 1):

            @pl.when(i == n * steps // (self.steps - 1))
            def _(n=n):
                self.phase(n)

    def at_end(self):
        self.phase(self.steps - 1)


def tail_kernel(side, *refs):
    jobs = len(side.jobs)
    side.bind(refs[:jobs], refs[jobs : 2 * jobs], refs[2 * jobs :])
    for n in range(side.steps):
        side.phase(n)


def tail(side):
    return pl.pallas_call(
        functools.partial(tail_kernel, side),
        in_specs=side.in_specs(),
        out_specs=[pl.BlockSpec(memory_space=pltpu.VMEM) if isinstance(job, Reduce) else job.out()[0] for job in side.jobs],
        out_shape=side.out_shape(),
        scratch_shapes=side.scratch(),
        compiler_params=side.params(),
        name="tail",
    )(*side.sources)


def exchange(pieces, me, ways):
    return [pieces[0]] + [
        lax.ppermute(pieces[k], "seq", [(s, s ^ k) for s in range(ways)]) for k in range(1, ways)
    ]


def by_partner(slots, me, ways):
    return [lax.dynamic_index_in_dim(slots, me ^ k, 0, keepdims=False) for k in range(ways)]


def to_slots(pieces, me, ways):
    stacked = jnp.stack(pieces)
    return jnp.take(stacked, jnp.arange(ways) ^ me, axis=0)


def body(tokens, cotangent, bins, live_count, w_qkv, w_out, w_up, w_down, gain_attn, gain_mlp):
    slots, rows, width = tokens.shape
    ways = lax.axis_size("seq")
    me = lax.axis_index("seq")
    toks = exchange(by_partner(tokens, me, ways), me, ways)
    cots = exchange(by_partner(cotangent, me, ways), me, ways)
    my_bin = lax.dynamic_index_in_dim(bins, me, 0)
    row_attn = lax.dynamic_slice_in_dim(gain_attn, my_bin[0], 1, 0)
    row_mlp = lax.dynamic_slice_in_dim(gain_mlp, my_bin[0], 1, 0)
    alive = jnp.broadcast_to((me < live_count[0]).astype(F32), (1, width))

    x, ready_attn, packed = qkv(toks, row_attn, w_qkv)
    mixed, aux = attend(packed)
    hidden, ready_mlp, gout, act, slope, grad_down = mlp(x, mixed, w_out, row_mlp, alive, cots, w_up)
    batch_ways = lax.axis_size("batch")
    line = batch_ways // 2
    block_rows = width // batch_ways
    carried = ways == slots == 4 and line == 4 and block_rows % 64 == 0
    if carried:

        def cut(rows_total):
            return (5 * rows_total // 8) // 16 * 16

        def reduce_of(v):
            here = v.shape[0] // batch_ways
            return Reduce(ways, line, here, v.shape[1], cut(here) if here >= 64 else 0)

        def blocks(v):
            return v.reshape(line, 2, v.shape[0] // batch_ways, v.shape[1])

        def side(ident, *arrays):
            return Side([reduce_of(v) for v in arrays], [blocks(v) for v in arrays], ways, line, ident)

        def add_swap(made, v):
            made.jobs.append(Swap(ways, rows, width))
            made.sources.append(v.reshape(ways, rows, width))
            return made

        first = side(1, grad_down)
    else:
        first = Side([], [], ways, line, 0)
    out, grad_up, grad_hidden, grad_out, grad_mixed, sum_mlp, *done = mlp_back(
        gout, act, slope, w_down, w_up, ready_mlp, hidden, row_mlp, mixed, w_out, first
    )
    second = add_swap(side(2, grad_up, grad_out), out) if carried else first
    grad_qkv, grad_x, sum_attn, *done_next = attn_back(
        packed, mixed, aux, grad_mixed, w_qkv, ready_attn, x, grad_hidden, row_attn, second
    )
    onehot = (jnp.arange(gain_attn.shape[0], dtype=jnp.int32) == my_bin[0]).astype(F32)[:, None]

    if carried:
        bins_here = gain_attn.shape[0] // batch_ways
        tables = jnp.concatenate(
            [(onehot * v).reshape(batch_ways, bins_here, width) for v in (sum_attn, sum_mlp)], axis=1
        )
        tables = tables.astype(BF16).reshape(batch_ways * 2 * bins_here, width)
        third = add_swap(side(3, grad_qkv, tables), grad_x)
        sum_qkv, sum_tables, grad_tokens = tail(third)
        return (
            done_next[2],
            grad_tokens.astype(F32),
            sum_qkv.astype(F32),
            done_next[1].astype(F32),
            done_next[0].astype(F32),
            done[0].astype(F32),
            sum_tables[:bins_here].astype(F32),
            sum_tables[bins_here:].astype(F32),
        )

    def back_to_slots(rows_out):
        parts = rows_out.reshape(ways, rows, width)
        return to_slots(exchange([parts[k] for k in range(ways)], me, ways), me, ways)

    def total(v, low):
        share = lax.psum_scatter(v, "batch", scatter_dimension=0, tiled=True)
        return lax.psum(share.astype(low), "seq").astype(F32)

    return (
        back_to_slots(out),
        back_to_slots(grad_x).astype(F32),
        total(grad_qkv, BF16),
        total(grad_out, BF16),
        total(grad_up, BF16),
        total(grad_down, BF16),
        total(onehot * sum_attn, F32),
        total(onehot * sum_mlp, F32),
    )


def solution(mesh):
    placed = (
        P("batch", "seq", None),
        P("batch", "seq", None),
        P("batch"),
        P("batch"),
        P(),
        P(),
        P(),
        P(),
        P(),
        P(),
    )
    return jax.shard_map(
        body,
        mesh=mesh,
        in_specs=placed,
        out_specs=(
            P("batch", "seq", None),
            P("batch", "seq", None),
            P("batch", None),
            P("batch", None),
            P("batch", None),
            P("batch", None),
            P("batch", None),
            P("batch", None),
        ),
        check_vma=False,
    )
```

```python
import functools
import math

import jax
import jax.numpy as jnp
from jax import lax
from jax.experimental import pallas as pl
from jax.experimental.pallas import tpu as pltpu
from jax.sharding import PartitionSpec as P

F32 = jnp.float32
BF16 = jnp.bfloat16
HEAD = 64
LOG2E = math.log2(math.e)
GELU_C = math.sqrt(2 / math.pi)
GELU_K = 0.044715
VMEM = 60 * 2**20


def dot(a, b, ca, cb):
    return lax.dot_general(a, b, (((ca,), (cb,)), ((), ())), preferred_element_type=F32)


def nn(a, b):
    return dot(a, b, 1, 0)


def nt(a, b):
    return dot(a, b, 1, 1)


def tn(a, b):
    return dot(a, b, 0, 0)


def whole(shape):
    zeros = (0,) * len(shape)
    return pl.BlockSpec(shape, lambda i: zeros, pipeline_mode=pl.Buffered(1))


def params():
    return pltpu.CompilerParams(vmem_limit_bytes=VMEM)


def norm_rows(v):
    centred = v - jnp.mean(v, axis=-1, keepdims=True)
    inverse = lax.rsqrt(jnp.mean(centred * centred, axis=-1, keepdims=True) + 1e-05)
    return centred * inverse, inverse


def norm_back(g, normed, inverse):
    first = jnp.mean(g, axis=-1, keepdims=True)
    second = jnp.mean(g * normed, axis=-1, keepdims=True)
    return inverse * (g - first - normed * second)


def entry_kernel(ways, steps, *refs):
    tokens, gain, w, x_out, ready_out, packed_out, w_out = refs[:7]
    here, w_here, w_turned, ready_here, packed_here, send, recv, local, leave = refs[7:]
    place = Place(ways, 0)
    rows, width = here.shape[1:]
    cols = w_here.shape[1]
    load_w = pltpu.make_async_copy(w, w_here, local.at[0])
    load_own = pltpu.make_async_copy(tokens.at[place.me], here.at[0], local.at[1])
    load_w.start()
    load_own.start()

    def move(k):
        return pltpu.make_async_remote_copy(
            src_ref=tokens.at[place.partner(k)], dst_ref=here.at[k],
            send_sem=send.at[k], recv_sem=recv.at[k],
            device_id=place.plane(k), device_id_type=MESH,
        )

    def span(k):
        return pl.ds(k * rows, rows)

    def leaving(k):
        return [
            pltpu.make_async_copy(here.at[k], x_out.at[span(k)], leave.at[0, k]),
            pltpu.make_async_copy(ready_here.at[k], ready_out.at[:, span(k)], leave.at[1, k]),
            pltpu.make_async_copy(packed_here.at[k], packed_out.at[:, span(k)], leave.at[2, k]),
        ]

    def project(k):
        ready = (norm_rows(here[k].astype(F32))[0] * gain[...]).astype(BF16)
        ready_here[k] = ready.T
        for c in range(0, cols, steps):
            packed_here[k, c : c + steps] = nt(w_turned[c : c + steps], ready).astype(BF16)
        for copy in leaving(k):
            copy.start()

    place.greet_plane()
    for k in range(1, ways - 1):
        move(k).start()
    load_w.wait()

    def turn(c, carry):
        at = pl.ds(pl.multiple_of(c * 256, 256), 256)
        w_turned[at] = w_here[:, at].T
        return carry

    lax.fori_loop(0, cols // 256, turn, 0)
    save_w = pltpu.make_async_copy(w_turned, w_out, local.at[2])
    save_w.start()
    load_own.wait()
    project(0)
    for k in range(1, ways - 1):
        move(k).wait_send()
    move(ways - 1).start()
    for k in range(1, ways):
        move(k).wait_recv()
        project(k)
    move(ways - 1).wait_send()
    save_w.wait()
    for k in range(ways):
        for copy in leaving(k):
            copy.wait()


def entry(tokens, gain, w):
    ways, rows, width = tokens.shape
    cols = w.shape[1]
    length = ways * rows
    remote = pl.BlockSpec(memory_space=pl.ANY)
    return pl.pallas_call(
        functools.partial(entry_kernel, ways, math.gcd(cols, 1024)),
        in_specs=[remote, pl.BlockSpec(memory_space=pltpu.VMEM), remote],
        out_specs=[remote] * 4,
        out_shape=[
            jax.ShapeDtypeStruct((length, width), BF16),
            jax.ShapeDtypeStruct((width, length), BF16),
            jax.ShapeDtypeStruct((cols, length), BF16),
            jax.ShapeDtypeStruct((cols, width), BF16),
        ],
        scratch_shapes=[
            pltpu.VMEM((ways, rows, width), BF16),
            pltpu.VMEM((width, cols), BF16),
            pltpu.VMEM((cols, width), BF16),
            pltpu.VMEM((ways, width, rows), BF16),
            pltpu.VMEM((ways, cols, rows), BF16),
            pltpu.SemaphoreType.DMA((ways,)),
            pltpu.SemaphoreType.DMA((ways,)),
            pltpu.SemaphoreType.DMA((3,)),
            pltpu.SemaphoreType.DMA((3, ways)),
        ],
        compiler_params=pltpu.CompilerParams(vmem_limit_bytes=VMEM, collective_id=0, has_side_effects=True),
        name="entry",
    )(tokens, gain, w)


def split2(v):
    hi = v.astype(BF16)
    return hi, (v - hi.astype(F32)).astype(BF16)


def split3(v):
    a = v.astype(BF16).astype(F32)
    b = (v - a).astype(BF16).astype(F32)
    return a, b, v - a - b


def in_rows(rows, cols):
    at = lax.broadcasted_iota(jnp.int32, (16, cols), 0)
    out = jnp.zeros((16, cols), F32)
    for i, row in enumerate(rows):
        out = jnp.where(at == i, row, out)
    return out.astype(BF16)


def ones_rows(many, cols):
    return (lax.broadcasted_iota(jnp.int32, (16, cols), 0) < many).astype(F32).astype(BF16)


def head_parts(p, h):
    base = 3 * HEAD * h
    return [p[base + HEAD * j : base + HEAD * (j + 1)] for j in range(3)]


def attend_kernel(p_ref, o_ref, aux_ref, *, bq):
    length = p_ref.shape[1]

    def run(exact):
        work, low, high = [], [], []
        for h in range(2):
            q, k, v = head_parts(p_ref, h)
            scaled = q.astype(F32) * (LOG2E * HEAD**-0.5)
            qhi, qlo = split2(scaled)
            if exact:
                shift = None
                qq = jnp.concatenate([qhi, qlo], axis=0)
                kk = jnp.concatenate([k, k], axis=0).T
            else:
                k32 = k.astype(F32)
                longest = jnp.sqrt(jnp.max(jnp.sum(k32 * k32, axis=0, keepdims=True)))
                bound = jnp.sqrt(jnp.sum(scaled * scaled, axis=0, keepdims=True)) * longest
                shift = bound.astype(BF16).astype(F32)
                qq = jnp.concatenate([qhi, qlo, in_rows([-shift], length)], axis=0)
                kk = jnp.concatenate([k, k, ones_rows(1, length)], axis=0).T
            vv = jnp.concatenate([v, ones_rows(1, length)], axis=0)
            for i in range(length // bq):
                span = slice(i * bq, (i + 1) * bq)
                work.append((h, span, kk, qq[:, span], vv, None if exact else shift[:, span]))
        following = nn(work[0][2], work[0][3])
        for n, (h, span, _, _, vv, m) in enumerate(work):
            s = following
            if n + 1 < len(work):
                following = nn(work[n + 1][2], work[n + 1][3])
            if exact:
                m = jnp.max(s, axis=0, keepdims=True)
                s = s - m
            o = nn(vv, jnp.exp2(s).astype(BF16))
            total = o[HEAD : HEAD + 1]
            o_ref[HEAD * h : HEAD * (h + 1), span] = (o[:HEAD] * (1.0 / total)).astype(BF16)
            aux_ref[h : h + 1, span] = -(m + jnp.log2(total))
            low.append(jnp.min(total))
            high.append(jnp.max(total))
        return functools.reduce(jnp.minimum, low), functools.reduce(jnp.maximum, high)

    low, high = run(False)
    fine = (low > 2.0**-80) & (high < 2.0**80)

    @pl.when(jnp.logical_not(fine))
    def _():
        run(True)


def attend(packed):
    cols, length = packed.shape
    pairs = cols // (6 * HEAD)
    return pl.pallas_call(
        functools.partial(attend_kernel, bq=math.gcd(length, 256)),
        grid=(pairs,),
        in_specs=[pl.BlockSpec((6 * HEAD, length), lambda i: (i, 0))],
        out_specs=[
            pl.BlockSpec((2 * HEAD, length), lambda i: (i, 0)),
            pl.BlockSpec((None, 8, length), lambda i: (i, 0, 0)),
        ],
        out_shape=[
            jax.ShapeDtypeStruct((pairs * 2 * HEAD, length), BF16),
            jax.ShapeDtypeStruct((pairs, 8, length), F32),
        ],
        compiler_params=params(),
        name="attend",
    )(packed)


def attend_back_math(p_ref, o_ref, aux_ref, do_ref, bq):
    length = p_ref.shape[1]
    outs = []
    for h in range(2):
        q, k, v = head_parts(p_ref, h)
        do = do_ref[HEAD * h : HEAD * (h + 1)]
        o = o_ref[HEAD * h : HEAD * (h + 1)]
        qhi, qlo = split2(q.astype(F32) * (LOG2E * HEAD**-0.5))
        qq = jnp.concatenate([qhi, qlo, in_rows(split3(aux_ref[h : h + 1]), length)], axis=0).T
        kk = jnp.concatenate([k, k, ones_rows(3, length)], axis=0)
        minus = -jnp.sum(do.astype(F32) * o.astype(F32), axis=0, keepdims=True)
        dd = jnp.concatenate([do, in_rows(split3(minus), length)], axis=0).T
        vv = jnp.concatenate([v, ones_rows(3, length)], axis=0)
        dv = jnp.zeros((HEAD, length), F32)
        dk = jnp.zeros((HEAD, length), F32)
        dq = []
        spans = [slice(i * bq, (i + 1) * bq) for i in range(length // bq)]
        following = nn(qq[spans[0]], kk), nn(dd[spans[0]], vv)
        for i, span in enumerate(spans):
            s, g = following
            if i + 1 < len(spans):
                following = nn(qq[spans[i + 1]], kk), nn(dd[spans[i + 1]], vv)
            p = jnp.exp2(s)
            ds = (p * g).astype(BF16)
            dv = dv + nn(do[:, span], p.astype(BF16))
            dk = dk + nn(q[:, span], ds)
            dq.append((nt(k, ds) * HEAD**-0.5).astype(BF16))
        outs += [jnp.concatenate(dq, axis=1), (dk * HEAD**-0.5).astype(BF16), dv.astype(BF16)]
    return jnp.concatenate(outs, axis=0)


def mlp_kernel(pieces, *refs):
    x, mixed, w_out, gain, alive = refs[:5]
    cots = refs[5 : 5 + pieces]
    w_up, hidden, ready, gout, act, slope, grad_down = refs[5 + pieces :]
    rows = cots[0].shape[0]

    @pl.when(pl.program_id(0) == 0)
    def _():
        for k in range(pieces):
            span = slice(k * rows, (k + 1) * rows)
            gout[span] = cots[k][...] * alive[...].astype(BF16)
            h = x[span].astype(F32) + tn(mixed[:, span], w_out[...])
            hidden[span] = h
            ready[span] = (norm_rows(h)[0] * gain[...]).astype(BF16)

    u = nn(ready[...], w_up[...])
    u2 = u * u
    t = jnp.tanh(u * (GELU_C + (GELU_C * GELU_K) * u2))
    half = 0.5 + 0.5 * t
    a = (u * half).astype(BF16)
    act[...] = a
    slope[...] = (half + u * (1 - t * t) * (0.5 * GELU_C + (1.5 * GELU_C * GELU_K) * u2)).astype(BF16)
    grad_down[...] = tn(a, gout[...]).astype(BF16)


def mlp(x, mixed, w_out, gain, alive, cots, w_up):
    length, width = x.shape
    inner = w_up.shape[1]
    rows = length // len(cots)
    block = min(1024, inner)
    cols = pl.BlockSpec((length, block), lambda i: (0, i))
    return pl.pallas_call(
        functools.partial(mlp_kernel, len(cots)),
        grid=(inner // block,),
        in_specs=[
            whole((length, width)),
            whole((length, width)),
            whole((width, width)),
            whole((1, width)),
            whole((1, width)),
        ]
        + [whole((rows, width))] * len(cots)
        + [pl.BlockSpec((width, block), lambda i: (0, i))],
        out_specs=[whole((length, width))] * 3 + [cols, cols, pl.BlockSpec((block, width), lambda i: (i, 0))],
        out_shape=[
            jax.ShapeDtypeStruct((length, width), F32),
            jax.ShapeDtypeStruct((length, width), BF16),
            jax.ShapeDtypeStruct((length, width), BF16),
            jax.ShapeDtypeStruct((length, inner), BF16),
            jax.ShapeDtypeStruct((length, inner), BF16),
            jax.ShapeDtypeStruct((inner, width), BF16),
        ],
        compiler_params=params(),
        name="mlp",
    )(x, mixed, w_out, gain, alive, *cots, w_up)


def mlp_back_kernel(side, *refs):
    jobs = len(side.jobs)
    gout, act, slope, w_down, w_up, ready, hidden, gain, mixed, w_out = refs[:10]
    refs = refs[10:]
    sources, refs = refs[:jobs], refs[jobs:]
    out, grad_up, grad_hidden, grad_out, grad_mixed, table = refs[:6]
    refs = refs[6:]
    finals, refs = refs[:jobs], refs[jobs:]
    out_sum, back_sum, mixed_here, w_here, late = refs[:5]
    side.bind(sources, finals, refs[5:])
    i = pl.program_id(0)
    last = pl.num_programs(0) - 1
    loads = [
        pltpu.make_async_copy(hidden, grad_hidden, late.at[0]),
        pltpu.make_async_copy(mixed, mixed_here, late.at[1]),
        pltpu.make_async_copy(w_out, w_here, late.at[2]),
    ]

    @pl.when(i == 0)
    def _():
        for load in loads:
            load.start()
        out_sum[...] = jnp.zeros_like(out_sum)
        back_sum[...] = jnp.zeros_like(back_sum)

    side.at_step(i, pl.num_programs(0))
    gu = (nt(gout[...], w_down[...]) * slope[...].astype(F32)).astype(BF16)
    grad_up[...] = tn(ready[...], gu).astype(BF16)
    back_sum[...] += nt(gu, w_up[...])
    out_sum[...] += nn(act[...], w_down[...])

    @pl.when(i == last)
    def _():
        for load in loads:
            load.wait()
        length = gout.shape[0]
        step = math.gcd(length, 256)
        total = jnp.zeros((1, gain.shape[1]), F32)
        for r in range(length // step):
            span = slice(r * step, (r + 1) * step)
            h = grad_hidden[span]
            out[span] = (h + out_sum[span]).astype(BF16)
            normed, inverse = norm_rows(h)
            g = back_sum[span]
            total = total + jnp.sum(g * normed, axis=0, keepdims=True)
            grad_hidden[span] = gout[span].astype(F32) + norm_back(g * gain[...], normed, inverse)
        table[...] = total
        low = grad_hidden[...].astype(BF16)
        grad_mixed[...] = nt(w_here[...], low).astype(BF16)
        grad_out[...] = nn(mixed_here[...], low).astype(BF16)
        side.at_end()


def mlp_back(gout, act, slope, w_down, w_up, ready, hidden, gain, mixed, w_out, side):
    length, width = gout.shape
    inner = w_up.shape[1]
    block = min(512, inner)
    cols = pl.BlockSpec((length, block), lambda i: (0, i))
    square = whole((length, width))
    remote = pl.BlockSpec(memory_space=pl.ANY)
    return pl.pallas_call(
        functools.partial(mlp_back_kernel, side),
        grid=(inner // block,),
        in_specs=[
            square,
            cols,
            cols,
            pl.BlockSpec((block, width), lambda i: (i, 0)),
            pl.BlockSpec((width, block), lambda i: (0, i)),
            square,
            remote,
            whole((1, width)),
            remote,
            remote,
        ]
        + side.in_specs(),
        out_specs=[
            square,
            pl.BlockSpec((width, block), lambda i: (0, i)),
            square,
            whole((width, width)),
            square,
            whole((1, width)),
        ]
        + side.out_specs(),
        out_shape=[
            jax.ShapeDtypeStruct((length, width), BF16),
            jax.ShapeDtypeStruct((width, inner), BF16),
            jax.ShapeDtypeStruct((length, width), F32),
            jax.ShapeDtypeStruct((width, width), BF16),
            jax.ShapeDtypeStruct((length, width), BF16),
            jax.ShapeDtypeStruct((1, width), F32),
        ]
        + side.out_shape(),
        scratch_shapes=[pltpu.VMEM((length, width), F32)] * 2
        + [pltpu.VMEM((length, width), BF16), pltpu.VMEM((width, width), BF16), pltpu.SemaphoreType.DMA((3,))]
        + side.scratch(),
        compiler_params=side.params(),
        name="mlp_back",
    )(gout, act, slope, w_down, w_up, ready, hidden, gain, mixed, w_out, *side.sources)


def attn_back_kernel(side, bq, *refs):
    jobs = len(side.jobs)
    packed, mixed, aux, grad_mixed, w_qkv, ready, x, grad_hidden, gain = refs[:9]
    refs = refs[9:]
    sources, refs = refs[:jobs], refs[jobs:]
    grad_qkv, grad_x, table = refs[:3]
    refs = refs[3:]
    finals, refs = refs[:jobs], refs[jobs:]
    back_sum = refs[0]
    side.bind(sources, finals, refs[1:])
    i = pl.program_id(0)

    @pl.when(i == 0)
    def _():
        back_sum[...] = jnp.zeros_like(back_sum)

    side.at_step(i, pl.num_programs(0))
    gp = attend_back_math(packed, mixed, aux, grad_mixed, bq)
    grad_qkv[...] = nt(ready[...], gp).astype(BF16)
    back_sum[...] += tn(gp, w_qkv[...])

    @pl.when(i == pl.num_programs(0) - 1)
    def _():
        length = x.shape[0]
        step = math.gcd(length, 256)
        total = jnp.zeros((1, gain.shape[1]), F32)
        for r in range(length // step):
            span = slice(r * step, (r + 1) * step)
            normed, inverse = norm_rows(x[span].astype(F32))
            g = back_sum[span]
            total = total + jnp.sum(g * normed, axis=0, keepdims=True)
            grad_x[span] = (grad_hidden[span] + norm_back(g * gain[...], normed, inverse)).astype(BF16)
        table[...] = total
        side.at_end()


def attn_back(packed, mixed, aux, grad_mixed, w_qkv, ready, x, grad_hidden, gain, side):
    length, width = x.shape
    cols = packed.shape[0]
    pairs = cols // (6 * HEAD)
    pair = pl.BlockSpec((2 * HEAD, length), lambda i: (i, 0))
    square = whole((length, width))
    return pl.pallas_call(
        functools.partial(attn_back_kernel, side, math.gcd(length, 256)),
        grid=(pairs,),
        in_specs=[
            pl.BlockSpec((6 * HEAD, length), lambda i: (i, 0)),
            pair,
            pl.BlockSpec((None, 8, length), lambda i: (i, 0, 0)),
            pair,
            pl.BlockSpec((6 * HEAD, width), lambda i: (i, 0)),
            square,
            square,
            square,
            whole((1, width)),
        ]
        + side.in_specs(),
        out_specs=[
            pl.BlockSpec((width, 6 * HEAD), lambda i: (0, i)),
            square,
            whole((1, width)),
        ]
        + side.out_specs(),
        out_shape=[
            jax.ShapeDtypeStruct((width, cols), BF16),
            jax.ShapeDtypeStruct((length, width), BF16),
            jax.ShapeDtypeStruct((1, width), F32),
        ]
        + side.out_shape(),
        scratch_shapes=[pltpu.VMEM((length, width), F32)] + side.scratch(),
        compiler_params=side.params(),
        name="attn_back",
    )(packed, mixed, aux, grad_mixed, w_qkv, ready, x, grad_hidden, gain, *side.sources)


MESH = pl.DeviceIdType.MESH


class Place:
    def __init__(self, ways, line):
        self.ways, self.line = ways, line
        self.me = lax.axis_index("seq")
        self.b = lax.axis_index("batch")
        self.core = lax.rem(self.b, 2)
        self.z = self.b // 2

    def other_core(self):
        return {"batch": self.b + 1 - 2 * self.core}

    def along(self, step):
        return {"batch": self.b + 2 * step}

    def plane(self, k):
        return {"seq": self.partner(k)}

    def partner(self, k):
        out = self.me
        for bit in range(k.bit_length()):
            if k >> bit & 1:
                out = out + (1 << bit) * (1 - 2 * lax.rem(self.me // (1 << bit), 2))
        return out

    def greet_plane(self):
        barrier = pltpu.get_barrier_semaphore()
        for k in range(1, self.ways):
            pl.semaphore_signal(barrier, inc=1, device_id=self.plane(k), device_id_type=MESH)
        pl.semaphore_wait(barrier, self.ways - 1)

    def greet(self):
        barrier = pltpu.get_barrier_semaphore()

        def tell(where):
            pl.semaphore_signal(barrier, inc=1, device_id=where, device_id_type=MESH)

        tell(self.other_core())
        for k in range(1, self.ways):
            tell(self.plane(k))

        @pl.when(self.z > 0)
        def _():
            tell(self.along(-1))

        @pl.when(self.z < self.line - 1)
        def _():
            tell(self.along(1))

        ends = (self.z == 0).astype(jnp.int32) + (self.z == self.line - 1).astype(jnp.int32)
        pl.semaphore_wait(barrier, self.ways + 2 - ends)


def add_rows(dst, srcs, rows, step=16):
    def one(i, carry):
        at = pl.multiple_of(i * step, step)
        total = dst(at)[...].astype(F32)
        for src in srcs:
            total = total + src(at)[...].astype(F32)
        dst(at)[...] = total.astype(BF16)
        return carry

    lax.fori_loop(0, rows // step, one, 0)


class Reduce:
    def __init__(self, ways, line, rows, cols, split, first=0):
        self.ways, self.line, self.rows, self.cols, self.split = ways, line, rows, cols, split
        self.here = pl.ds(first, cols)
        self.part = cols // ways
        self.last = 8

    def scratch(self):
        line, rows, cols, split, part = self.line, self.rows, self.cols, self.split, self.part
        hops, rest, others = line - 1, rows - split, self.ways - 1
        shapes = [pltpu.VMEM((line, rows, cols), BF16), pltpu.VMEM((line, rows, cols), BF16)]
        if rest:
            shapes += [
                pltpu.VMEM((hops, rest, cols), BF16),
                pltpu.VMEM((hops, rest, cols), BF16),
                pltpu.VMEM((others, rest, part), BF16),
            ]
        if split:
            shapes += [
                pltpu.VMEM((others, line, split, part), BF16),
                pltpu.VMEM((hops, split, part), BF16),
                pltpu.VMEM((hops, split, part), BF16),
            ]
        n = 2 * (others * 2 + 2 * hops) + 2
        return shapes + [
            pltpu.VMEM((rows, cols), BF16),
            pltpu.SemaphoreType.DMA((n,)),
            pltpu.SemaphoreType.DMA((n,)),
        ]

    def bind(self, place, source, final, refs):
        refs = list(refs)
        self.place, self.source, self.result = place, source, final
        self.own, self.near = refs[:2]
        refs = refs[2:]
        if self.rows - self.split:
            self.z_right, self.z_left, self.z_part = refs[:3]
            refs = refs[3:]
        if self.split:
            self.x_part, self.x_right, self.x_left = refs[:3]
            refs = refs[3:]
        self.final, self.send, self.recv = refs
        self.ids = {}
        return self

    def sem(self, key):
        if key not in self.ids:
            self.ids[key] = len(self.ids) + 1
        return self.ids[key]

    def copy(self, key, src, dst, where):
        n = self.sem(key)
        return pltpu.make_async_remote_copy(
            src_ref=src, dst_ref=dst, send_sem=self.send.at[n], recv_sem=self.recv.at[n],
            device_id=where, device_id_type=MESH,
        )

    def span(self, quarter):
        return pl.ds(pl.multiple_of(quarter * self.part, self.part), self.part)

    def core_copy(self):
        p = self.place
        return self.copy("core", self.source.at[:, 1 - p.core, :, self.here], self.near, p.other_core())

    def own_copy(self):
        p = self.place
        return pltpu.make_async_copy(self.source.at[:, p.core, :, self.here], self.own, self.send.at[0])

    def x_rs(self, k):
        p = self.place
        return self.copy(
            ("x_rs", k),
            self.own.at[:, pl.ds(0, self.split), self.span(p.partner(k))],
            self.x_part.at[k - 1],
            p.plane(k),
        )

    def x_ag(self, k):
        p = self.place
        here = (pl.ds(0, self.split), self.span(p.me))
        return self.copy(("x_ag", k), self.final.at[here], self.final.at[here], p.plane(k))

    def x_ag_in(self, k):
        p = self.place
        here = (pl.ds(0, self.split), self.span(p.partner(k)))
        return self.copy(("x_ag", k), self.final.at[here], self.final.at[here], p.plane(k))

    def z_rs(self, k):
        p = self.place
        return self.copy(
            ("z_rs", k),
            self.own.at[p.z, pl.ds(self.split, self.rows - self.split), self.span(p.partner(k))],
            self.z_part.at[k - 1],
            p.plane(k),
        )

    def z_ag(self, k, quarter):
        here = (pl.ds(self.split, self.rows - self.split), self.span(quarter))
        return self.copy(("z_ag", k), self.final.at[here], self.final.at[here], self.place.plane(k))

    def line_row(self, kind, j):
        if kind == "x":
            return self.own.at[j, pl.ds(0, self.split), self.span(self.place.me)]
        return self.own.at[j, pl.ds(self.split, self.rows - self.split)]

    def line_in(self, kind, right):
        if kind == "x":
            return self.x_right if right else self.x_left
        return self.z_right if right else self.z_left

    def line_copy(self, kind, right, t, j):
        return self.copy(
            (kind, right, t),
            self.line_row(kind, j),
            self.line_in(kind, right).at[t - 1],
            self.place.along(1 if right else -1),
        )

    def line_step(self, kind, t):
        p, line = self.place, self.line
        rows = self.split if kind == "x" else self.rows - self.split
        for right in (True, False):
            at = p.z if right else line - 1 - p.z
            if t < line:
                j = line + p.z - t if right else p.z + t - line

                @pl.when(at <= t - 1)
                def _(right=right, at=at, j=j):
                    if t > 1:

                        @pl.when((at >= 1) & (at <= t - 1))
                        def _():
                            self.line_arrive(kind, right, t - 1, j, rows)

                    self.line_copy(kind, right, t, j).start()

            else:

                @pl.when(at >= 1)
                def _(right=right):
                    self.line_arrive(kind, right, t - 1, p.z, rows)

    def line_arrive(self, kind, right, t, j, rows):
        p = self.place
        self.copy(
            (kind, right, t),
            self.line_row(kind, j),
            self.line_in(kind, right).at[t - 1],
            p.along(-1 if right else 1),
        ).wait_recv()
        buffer = self.line_in(kind, right)
        if kind == "x":
            mine = lambda r: self.own.at[j, pl.ds(r, 16), self.span(p.me)]
        else:
            mine = lambda r: self.own.at[j, pl.ds(self.split + r, 16)]
        add_rows(mine, [lambda r: buffer.at[t - 1, pl.ds(r, 16)]], rows)

    def line_sent(self, kind):
        p, line = self.place, self.line
        for t in range(1, line):
            for right in (True, False):
                at = p.z if right else line - 1 - p.z

                @pl.when(at <= t - 1)
                def _(right=right, t=t):
                    self.line_copy(kind, right, t, p.z).wait_send()

    def finish_part(self, first, rows, buffers, j):
        p = self.place

        def one(i, carry):
            r = pl.multiple_of(i * 16, 16)
            total = self.own[j, pl.ds(first + r, 16), self.span(p.me)].astype(F32)
            for buffer in buffers:
                total = total + buffer(r)[...].astype(F32)
            self.final[pl.ds(first + r, 16), self.span(p.me)] = total.astype(BF16)
            return carry

        lax.fori_loop(0, rows // 16, one, 0)

    def phase(self, n):
        p, others = self.place, range(1, self.ways)
        rest = self.rows - self.split
        if n == 0:
            self.own_copy().start()
            self.core_copy().start()
        if n == 1:
            self.own_copy().wait()
            self.core_copy().wait_recv()

            def one(z, carry):
                add_rows(
                    lambda r: self.own.at[z, pl.ds(r, 16)],
                    [lambda r: self.near.at[z, pl.ds(r, 16)]],
                    self.rows,
                )
                return carry

            lax.fori_loop(0, self.line, one, 0)
            if self.split:
                for k in others:
                    self.x_rs(k).start()
        if rest and 1 <= n <= 4:
            self.line_step("z", n)
        if n == 4:
            if rest:
                for k in others:
                    self.z_rs(k).start()
            if self.split:
                for k in others:
                    self.x_rs(k).wait_recv()

                def sum_x(z, carry):
                    add_rows(
                        lambda r: self.own.at[z, pl.ds(r, 16), self.span(p.me)],
                        [
                            functools.partial(lambda k, r: self.x_part.at[k - 1, z, pl.ds(r, 16)], k)
                            for k in others
                        ],
                        self.split,
                    )
                    return carry

                lax.fori_loop(0, self.line, sum_x, 0)
        if self.split and 4 <= n <= 7:
            self.line_step("x", n - 3)
        if n == 5 and rest:
            for k in others:
                self.z_rs(k).wait_recv()
            self.finish_part(
                self.split,
                rest,
                [functools.partial(lambda k, r: self.z_part.at[k - 1, pl.ds(r, 16)], k) for k in others],
                p.z,
            )
            for k in others:
                self.z_ag(k, p.me).start()
        if n == 7 and self.split:
            self.finish_part(0, self.split, [], p.z)
            for k in others:
                self.x_ag(k).start()
        if n == 8:
            for k in others:
                if rest:
                    self.z_ag(k, p.partner(k)).wait_recv()
                    self.z_ag(k, p.me).wait_send()
                    self.z_rs(k).wait_send()
                if self.split:
                    self.x_ag_in(k).wait_recv()
                    self.x_ag(k).wait_send()
                    self.x_rs(k).wait_send()
            if rest:
                self.line_sent("z")
            if self.split:
                self.line_sent("x")
            self.core_copy().wait_send()
            self.result[:, self.here] = self.final[...]


class Sums:
    last = 8

    def __init__(self, ways, line, rows, cols, split, parts):
        width = cols // parts
        self.shape = (rows, cols)
        self.parts = [Reduce(ways, line, rows, width, split, i * width) for i in range(parts)]

    def out(self):
        return whole(self.shape), jax.ShapeDtypeStruct(self.shape, BF16)

    def scratch(self):
        return [s for part in self.parts for s in part.scratch()]

    def bind(self, place, source, final, refs):
        refs = list(refs)
        for part in self.parts:
            many = len(part.scratch())
            part.bind(place, source, final, refs[:many])
            refs = refs[many:]

    def phase(self, n):
        for part in self.parts:
            part.phase(n)


class Swap:
    last = 8

    def __init__(self, ways, rows, cols):
        self.ways, self.shape = ways, (ways, rows, cols)

    def scratch(self):
        return [pltpu.SemaphoreType.DMA((self.ways,)), pltpu.SemaphoreType.DMA((self.ways,))]

    def out(self):
        return pl.BlockSpec(memory_space=pl.ANY), jax.ShapeDtypeStruct(self.shape, BF16)

    def bind(self, place, source, final, refs):
        self.place, self.source, self.final = place, source, final
        self.send, self.recv = refs
        return self

    def copy(self, k, slot):
        return pltpu.make_async_remote_copy(
            src_ref=self.source.at[k], dst_ref=self.final.at[slot],
            send_sem=self.send.at[k], recv_sem=self.recv.at[k],
            device_id=self.place.plane(k), device_id_type=MESH,
        )

    def stay(self):
        return pltpu.make_async_copy(self.source.at[0], self.final.at[self.place.me], self.send.at[0])

    def phase(self, n):
        p = self.place
        if n == 0:
            self.stay().start()
            for k in range(1, self.ways):
                self.copy(k, p.me).start()
        if n == self.last:
            self.stay().wait()
            for k in range(1, self.ways):
                self.copy(k, p.partner(k)).wait_recv()
                self.copy(k, p.me).wait_send()


class Side:
    steps = 9

    def __init__(self, jobs, sources, ways, line, ident):
        self.jobs, self.sources, self.ways, self.line, self.ident = jobs, sources, ways, line, ident

    def in_specs(self):
        return [pl.BlockSpec(memory_space=pl.ANY)] * len(self.jobs)

    def out_specs(self):
        return [job.out()[0] for job in self.jobs]

    def out_shape(self):
        return [job.out()[1] for job in self.jobs]

    def scratch(self):
        return [s for job in self.jobs for s in job.scratch()]

    def params(self):
        if not self.jobs:
            return pltpu.CompilerParams(vmem_limit_bytes=VMEM)
        return pltpu.CompilerParams(vmem_limit_bytes=VMEM, collective_id=self.ident, has_side_effects=True)

    def bind(self, sources, finals, refs):
        if not self.jobs:
            return
        refs = list(refs)
        self.place = Place(self.ways, self.line)
        for job, source, final in zip(self.jobs, sources, finals):
            many = len(job.scratch())
            job.bind(self.place, source, final, refs[:many])
            refs = refs[many:]

    def phase(self, n):
        if not self.jobs:
            return
        if n == 0:
            self.place.greet()
        for job in self.jobs:
            job.phase(n)

    def at_step(self, i, steps):
        if not self.jobs:
            return
        for n in range(self.steps - 1):

            @pl.when(i == n * steps // (self.steps - 1))
            def _(n=n):
                self.phase(n)

    def at_end(self):
        self.phase(self.steps - 1)


def tail_kernel(side, *refs):
    jobs = len(side.jobs)
    side.bind(refs[:jobs], refs[jobs : 2 * jobs], refs[2 * jobs :])
    for n in range(side.steps):
        side.phase(n)


def tail(side):
    return pl.pallas_call(
        functools.partial(tail_kernel, side),
        in_specs=side.in_specs(),
        out_specs=[pl.BlockSpec(memory_space=pltpu.VMEM) if isinstance(job, Sums) else job.out()[0] for job in side.jobs],
        out_shape=side.out_shape(),
        scratch_shapes=side.scratch(),
        compiler_params=side.params(),
        name="tail",
    )(*side.sources)


def finish_kernel(*refs):
    many = len(refs) // 2
    for source, target in zip(refs[:many], refs[many:]):
        target[...] = source[...].astype(target.dtype)


def finish(arrays, kinds, steps):
    def spec(v):
        block = (v.shape[0] // steps,) + v.shape[1:]
        zeros = (0,) * (v.ndim - 1)
        return pl.BlockSpec(block, lambda i: (i,) + zeros)

    return pl.pallas_call(
        finish_kernel,
        grid=(steps,),
        in_specs=[spec(v) for v in arrays],
        out_specs=[spec(v) for v in arrays],
        out_shape=[jax.ShapeDtypeStruct(v.shape, kind) for v, kind in zip(arrays, kinds)],
        compiler_params=params(),
        name="finish",
    )(*arrays)


def exchange(pieces, me, ways):
    return [pieces[0]] + [
        lax.ppermute(pieces[k], "seq", [(s, s ^ k) for s in range(ways)]) for k in range(1, ways)
    ]


def by_partner(slots, me, ways):
    return [lax.dynamic_index_in_dim(slots, me ^ k, 0, keepdims=False) for k in range(ways)]


def to_slots(pieces, me, ways):
    stacked = jnp.stack(pieces)
    return jnp.take(stacked, jnp.arange(ways) ^ me, axis=0)


def body(tokens, cotangent, bins, live_count, w_qkv, w_out, w_up, w_down, gain_attn, gain_mlp):
    slots, rows, width = tokens.shape
    ways = lax.axis_size("seq")
    me = lax.axis_index("seq")
    my_bin = lax.dynamic_index_in_dim(bins, me, 0)
    row_attn = lax.dynamic_slice_in_dim(gain_attn, my_bin[0], 1, 0)
    row_mlp = lax.dynamic_slice_in_dim(gain_mlp, my_bin[0], 1, 0)
    alive = jnp.broadcast_to((me < live_count[0]).astype(F32), (1, width))

    x, ready_attn, packed, w_turned = entry(tokens, row_attn, w_qkv)
    packed, later = lax.optimization_barrier((packed, cotangent))
    cots = exchange(by_partner(later, me, ways), me, ways)
    mixed, aux = attend(packed)
    hidden, ready_mlp, gout, act, slope, grad_down = mlp(x, mixed, w_out, row_mlp, alive, cots, w_up)
    batch_ways = lax.axis_size("batch")
    line = batch_ways // 2
    block_rows = width // batch_ways
    carried = ways == slots == 4 and line == 4 and block_rows % 64 == 0
    if carried:

        def reduce_of(v, share, parts):
            here = v.shape[0] // batch_ways
            return Sums(ways, line, here, v.shape[1], int(here * share) // 16 * 16, parts)

        def blocks(v):
            return v.reshape(line, 2, v.shape[0] // batch_ways, v.shape[1])

        def side(ident, *plans):
            jobs = [reduce_of(*plan) for plan in plans]
            return Side(jobs, [blocks(plan[0]) for plan in plans], ways, line, ident)

        def add_swap(made, v):
            made.jobs.append(Swap(ways, rows, width))
            made.sources.append(v.reshape(ways, rows, width))
            return made

        first = side(1, (grad_down, 0.6, 2))
    else:
        first = Side([], [], ways, line, 0)
    out, grad_up, grad_hidden, grad_out, grad_mixed, sum_mlp, *done = mlp_back(
        gout, act, slope, w_down, w_up, ready_mlp, hidden, row_mlp, mixed, w_out, first
    )
    second = add_swap(side(2, (grad_up, 0.5, 2), (grad_out, 0.5, 1)), out) if carried else first
    grad_qkv, grad_x, sum_attn, *done_next = attn_back(
        packed, mixed, aux, grad_mixed, w_turned, ready_attn, x, grad_hidden, row_attn, second
    )
    onehot = (jnp.arange(gain_attn.shape[0], dtype=jnp.int32) == my_bin[0]).astype(F32)[:, None]

    if carried:
        bins_here = gain_attn.shape[0] // batch_ways
        tables = jnp.concatenate(
            [(onehot * v).reshape(batch_ways, bins_here, width) for v in (sum_attn, sum_mlp)], axis=1
        )
        tables = tables.astype(BF16).reshape(batch_ways * 2 * bins_here, width)
        third = add_swap(side(3, (grad_qkv, 0.375, 2), (tables, 0, 1)), grad_x)
        sum_qkv, sum_tables, grad_tokens = tail(third)
        arrays = (done_next[2], grad_tokens, sum_qkv, done_next[1], done_next[0], done[0])
        kinds = (BF16,) + (F32,) * 5
        return (
            *finish(arrays, kinds, ways),
            sum_tables[:bins_here].astype(F32),
            sum_tables[bins_here:].astype(F32),
        )

    def back_to_slots(rows_out):
        parts = rows_out.reshape(ways, rows, width)
        return to_slots(exchange([parts[k] for k in range(ways)], me, ways), me, ways)

    def total(v, low):
        share = lax.psum_scatter(v, "batch", scatter_dimension=0, tiled=True)
        return lax.psum(share.astype(low), "seq").astype(F32)

    return (
        back_to_slots(out),
        back_to_slots(grad_x).astype(F32),
        total(grad_qkv, BF16),
        total(grad_out, BF16),
        total(grad_up, BF16),
        total(grad_down, BF16),
        total(onehot * sum_attn, F32),
        total(onehot * sum_mlp, F32),
    )


def solution(mesh):
    placed = (
        P("batch", "seq", None),
        P("batch", "seq", None),
        P("batch"),
        P("batch"),
        P(),
        P(),
        P(),
        P(),
        P(),
        P(),
    )
    return jax.shard_map(
        body,
        mesh=mesh,
        in_specs=placed,
        out_specs=(
            P("batch", "seq", None),
            P("batch", "seq", None),
            P("batch", None),
            P("batch", None),
            P("batch", None),
            P("batch", None),
            P("batch", None),
            P("batch", None),
        ),
        check_vma=False,
    )
```

```python
import functools
import math

import jax
import jax.numpy as jnp
from jax import lax
from jax.experimental import pallas as pl
from jax.experimental.pallas import tpu as pltpu
from jax.sharding import PartitionSpec as P

F32 = jnp.float32
BF16 = jnp.bfloat16
HEAD = 64
HEADS = 16
LOG2E = math.log2(math.e)
GELU_C = math.sqrt(2 / math.pi)
GELU_K = 0.044715
VMEM = 63 * 2**20
DOWN_SHARES = (0.65,)
UP_SHARES = (0.5,)
OUT_SHARES = (0.5,)
QKV_SHARES = (0.5, 0.25)


def dot(a, b, ca, cb):
    return lax.dot_general(a, b, (((ca,), (cb,)), ((), ())), preferred_element_type=F32)


def nn(a, b):
    return dot(a, b, 1, 0)


def nt(a, b):
    return dot(a, b, 1, 1)


def tn(a, b):
    return dot(a, b, 0, 0)


def whole(shape):
    zeros = (0,) * len(shape)
    return pl.BlockSpec(shape, lambda i: zeros, pipeline_mode=pl.Buffered(1))


def params():
    return pltpu.CompilerParams(vmem_limit_bytes=VMEM)


def norm_rows(v):
    centred = v - jnp.mean(v, axis=-1, keepdims=True)
    inverse = lax.rsqrt(jnp.mean(centred * centred, axis=-1, keepdims=True) + 1e-05)
    return centred * inverse, inverse


def norm_back(g, normed, inverse):
    first = jnp.mean(g, axis=-1, keepdims=True)
    second = jnp.mean(g * normed, axis=-1, keepdims=True)
    return inverse * (g - first - normed * second)


def entry_kernel(ways, steps, *refs):
    bins, live, tokens, gain_attn, gain_mlp, w, x_out, ready_out, packed_out, w_out, own_rows = refs[:11]
    here, w_here, w_turned, ready_here, packed_here, send, recv, local, leave = refs[11:]
    place = Place(ways, 0)
    own_bin = bins[place.me]
    gain = gain_attn[pl.ds(own_bin, 1)]
    own_rows[0:1] = gain
    own_rows[1:2] = gain_mlp[pl.ds(own_bin, 1)]
    own_rows[2:3] = jnp.where(place.me < live[0], jnp.ones_like(gain), jnp.zeros_like(gain))
    own_rows[3:8] = jnp.zeros((5, gain.shape[1]), F32)
    rows, width = here.shape[1:]
    cols = w_here.shape[1]
    load_w = pltpu.make_async_copy(w, w_here, local.at[0])
    load_own = pltpu.make_async_copy(tokens.at[place.me], here.at[0], local.at[1])
    load_w.start()
    load_own.start()

    def move(k):
        return pltpu.make_async_remote_copy(
            src_ref=tokens.at[place.partner(k)], dst_ref=here.at[k],
            send_sem=send.at[k], recv_sem=recv.at[k],
            device_id=place.plane(k), device_id_type=MESH,
        )

    def span(k):
        return pl.ds(k * rows, rows)

    def leaving(k):
        return [
            pltpu.make_async_copy(here.at[k], x_out.at[span(k)], leave.at[0, k]),
            pltpu.make_async_copy(ready_here.at[k], ready_out.at[:, span(k)], leave.at[1, k]),
            pltpu.make_async_copy(packed_here.at[k], packed_out.at[:, span(k)], leave.at[2, k]),
        ]

    def project(k):
        ready = (norm_rows(here[k].astype(F32))[0] * gain).astype(BF16)
        ready_here[k] = ready.T
        for c in range(0, cols, steps):
            packed_here[k, c : c + steps] = nt(w_turned[c : c + steps], ready).astype(BF16)
        for copy in leaving(k):
            copy.start()

    place.greet_plane()
    for k in range(1, ways - 1):
        move(k).start()
    load_w.wait()

    def turn(c, carry):
        at = pl.ds(pl.multiple_of(c * 256, 256), 256)
        w_turned[at] = w_here[:, at].T
        return carry

    lax.fori_loop(0, cols // 256, turn, 0)
    save_w = pltpu.make_async_copy(w_turned, w_out, local.at[2])
    save_w.start()
    load_own.wait()
    project(0)
    for k in range(1, ways - 1):
        move(k).wait_send()
    move(ways - 1).start()
    for k in range(1, ways):
        move(k).wait_recv()
        project(k)
    move(ways - 1).wait_send()
    save_w.wait()
    for k in range(ways):
        for copy in leaving(k):
            copy.wait()


def entry(bins, live, tokens, gain_attn, gain_mlp, w):
    ways, rows, width = tokens.shape
    cols = w.shape[1]
    length = ways * rows
    remote = pl.BlockSpec(memory_space=pl.ANY)
    return pl.pallas_call(
        functools.partial(entry_kernel, ways, math.gcd(cols, 1024)),
        in_specs=[pl.BlockSpec(memory_space=pltpu.SMEM)] * 2
        + [remote]
        + [pl.BlockSpec(memory_space=pltpu.VMEM)] * 2
        + [remote],
        out_specs=[remote] * 4 + [pl.BlockSpec(memory_space=pltpu.VMEM)],
        out_shape=[
            jax.ShapeDtypeStruct((length, width), BF16),
            jax.ShapeDtypeStruct((width, length), BF16),
            jax.ShapeDtypeStruct((cols, length), BF16),
            jax.ShapeDtypeStruct((cols, width), BF16),
            jax.ShapeDtypeStruct((8, width), F32),
        ],
        scratch_shapes=[
            pltpu.VMEM((ways, rows, width), BF16),
            pltpu.VMEM((width, cols), BF16),
            pltpu.VMEM((cols, width), BF16),
            pltpu.VMEM((ways, width, rows), BF16),
            pltpu.VMEM((ways, cols, rows), BF16),
            pltpu.SemaphoreType.DMA((ways,)),
            pltpu.SemaphoreType.DMA((ways,)),
            pltpu.SemaphoreType.DMA((3,)),
            pltpu.SemaphoreType.DMA((3, ways)),
        ],
        compiler_params=pltpu.CompilerParams(vmem_limit_bytes=VMEM, collective_id=0, has_side_effects=True),
        name="entry",
    )(bins, live, tokens, gain_attn, gain_mlp, w)


def split2(v):
    hi = v.astype(BF16)
    return hi, (v - hi.astype(F32)).astype(BF16)


def split3(v):
    a = v.astype(BF16).astype(F32)
    b = (v - a).astype(BF16).astype(F32)
    return a, b, v - a - b


def in_rows(rows, cols):
    at = lax.broadcasted_iota(jnp.int32, (16, cols), 0)
    out = jnp.zeros((16, cols), F32)
    for i, row in enumerate(rows):
        out = jnp.where(at == i, row, out)
    return out.astype(BF16)


def ones_rows(many, cols):
    return (lax.broadcasted_iota(jnp.int32, (16, cols), 0) < many).astype(F32).astype(BF16)


def head_parts(p, h):
    base = 3 * HEAD * h
    return [p[base + HEAD * j : base + HEAD * (j + 1)] for j in range(3)]


def attend_kernel(p_ref, o_ref, aux_ref, *, bq):
    length = p_ref.shape[1]

    def run(exact):
        work, low, high = [], [], []
        for h in range(2):
            q, k, v = head_parts(p_ref, h)
            scaled = q.astype(F32) * (LOG2E * HEAD**-0.5)
            qhi, qlo = split2(scaled)
            if exact:
                shift = None
                qq = jnp.concatenate([qhi, qlo], axis=0)
                kk = jnp.concatenate([k, k], axis=0).T
            else:
                k32 = k.astype(F32)
                longest = jnp.sqrt(jnp.max(jnp.sum(k32 * k32, axis=0, keepdims=True)))
                bound = jnp.sqrt(jnp.sum(scaled * scaled, axis=0, keepdims=True)) * longest
                shift = bound.astype(BF16).astype(F32)
                qq = jnp.concatenate([qhi, qlo, in_rows([-shift], length)], axis=0)
                kk = jnp.concatenate([k, k, ones_rows(1, length)], axis=0).T
            vv = jnp.concatenate([v, ones_rows(1, length)], axis=0)
            for i in range(length // bq):
                span = slice(i * bq, (i + 1) * bq)
                work.append((h, span, kk, qq[:, span], vv, None if exact else shift[:, span]))
        following = nn(work[0][2], work[0][3])
        for n, (h, span, _, _, vv, m) in enumerate(work):
            s = following
            if n + 1 < len(work):
                following = nn(work[n + 1][2], work[n + 1][3])
            if exact:
                m = jnp.max(s, axis=0, keepdims=True)
                s = s - m
            o = nn(vv, jnp.exp2(s).astype(BF16))
            total = o[HEAD : HEAD + 1]
            o_ref[HEAD * h : HEAD * (h + 1), span] = (o[:HEAD] * (1.0 / total)).astype(BF16)
            aux_ref[h : h + 1, span] = -(m + jnp.log2(total))
            low.append(jnp.min(total))
            high.append(jnp.max(total))
        return functools.reduce(jnp.minimum, low), functools.reduce(jnp.maximum, high)

    low, high = run(False)
    fine = (low > 2.0**-80) & (high < 2.0**80)

    @pl.when(jnp.logical_not(fine))
    def _():
        run(True)


def attend(packed):
    cols, length = packed.shape
    pairs = cols // (6 * HEAD)
    return pl.pallas_call(
        functools.partial(attend_kernel, bq=math.gcd(length, 256)),
        grid=(pairs,),
        in_specs=[pl.BlockSpec((6 * HEAD, length), lambda i: (i, 0))],
        out_specs=[
            pl.BlockSpec((2 * HEAD, length), lambda i: (i, 0)),
            pl.BlockSpec((None, 8, length), lambda i: (i, 0, 0)),
        ],
        out_shape=[
            jax.ShapeDtypeStruct((pairs * 2 * HEAD, length), BF16),
            jax.ShapeDtypeStruct((pairs, 8, length), F32),
        ],
        compiler_params=params(),
        name="attend",
    )(packed)


def attend_back_head(p_ref, o_ref, aux_ref, do_ref, bq, h):
    length = p_ref.shape[1]
    q, k, v = head_parts(p_ref, h)
    do = do_ref[HEAD * h : HEAD * (h + 1)]
    o = o_ref[HEAD * h : HEAD * (h + 1)]
    qhi, qlo = split2(q.astype(F32) * (LOG2E * HEAD**-0.5))
    qq = jnp.concatenate([qhi, qlo, in_rows(split3(aux_ref[h : h + 1]), length)], axis=0).T
    kk = jnp.concatenate([k, k, ones_rows(3, length)], axis=0)
    minus = -jnp.sum(do.astype(F32) * o.astype(F32), axis=0, keepdims=True)
    dd = jnp.concatenate([do, in_rows(split3(minus), length)], axis=0).T
    vv = jnp.concatenate([v, ones_rows(3, length)], axis=0)
    dv = jnp.zeros((HEAD, length), F32)
    dk = jnp.zeros((HEAD, length), F32)
    dq = []
    spans = [slice(i * bq, (i + 1) * bq) for i in range(length // bq)]
    following = nn(qq[spans[0]], kk), nn(dd[spans[0]], vv)
    for i, span in enumerate(spans):
        s, g = following
        if i + 1 < len(spans):
            following = nn(qq[spans[i + 1]], kk), nn(dd[spans[i + 1]], vv)
        p = jnp.exp2(s)
        ds = (p * g).astype(BF16)
        dv = dv + nn(do[:, span], p.astype(BF16))
        dk = dk + nn(q[:, span], ds)
        dq.append((nt(k, ds) * HEAD**-0.5).astype(BF16))
    return [jnp.concatenate(dq, axis=1), (dk * HEAD**-0.5).astype(BF16), dv.astype(BF16)]


MESH = pl.DeviceIdType.MESH


class Place:
    def __init__(self, ways, line):
        self.ways, self.line = ways, line
        self.me = lax.axis_index("seq")
        self.b = lax.axis_index("batch")
        self.core = lax.rem(self.b, 2)
        self.z = self.b // 2

    def other_core(self):
        return {"batch": self.b + 1 - 2 * self.core}

    def along(self, step):
        return {"batch": self.b + 2 * step}

    def plane(self, k):
        return {"seq": self.partner(k)}

    def partner(self, k):
        out = self.me
        for bit in range(k.bit_length()):
            if k >> bit & 1:
                out = out + (1 << bit) * (1 - 2 * lax.rem(self.me // (1 << bit), 2))
        return out

    def greet_core(self):
        barrier = pltpu.get_barrier_semaphore()
        pl.semaphore_signal(barrier, inc=1, device_id=self.other_core(), device_id_type=MESH)
        pl.semaphore_wait(barrier, 1)

    def greet_plane(self):
        barrier = pltpu.get_barrier_semaphore()
        for k in range(1, self.ways):
            pl.semaphore_signal(barrier, inc=1, device_id=self.plane(k), device_id_type=MESH)
        pl.semaphore_wait(barrier, self.ways - 1)

    def hail(self):
        barrier = pltpu.get_barrier_semaphore()

        def tell(where):
            pl.semaphore_signal(barrier, inc=1, device_id=where, device_id_type=MESH)

        tell(self.other_core())
        for k in range(1, self.ways):
            tell(self.plane(k))

        @pl.when(self.z > 0)
        def _():
            tell(self.along(-1))

        @pl.when(self.z < self.line - 1)
        def _():
            tell(self.along(1))

    def greet(self):
        ends = (self.z == 0).astype(jnp.int32) + (self.z == self.line - 1).astype(jnp.int32)
        pl.semaphore_wait(pltpu.get_barrier_semaphore(), self.ways + 2 - ends)


def add_rows(dst, srcs, rows, cols):
    step = row_step(rows, cols)

    def one(i, carry):
        at = pl.multiple_of(i * step, step)
        total = dst(at, step)[...]
        for src in srcs:
            total = total + src(at, step)[...]
        dst(at, step)[...] = total
        return carry

    lax.fori_loop(0, rows // step, one, 0)


def row_step(rows, cols):
    for step in (64, 48, 32):
        if rows % step == 0 and step * cols <= 32768:
            return step
    return 16


class Way:
    def __init__(self, place, order, part):
        bits = lax.rem(place.me, 2), place.me // 2
        self.a, self.b = (bits[0], bits[1]) if order == 0 else (bits[1], bits[0])
        self.first, self.second = (1, 2) if order == 0 else (2, 1)
        self.part = part

    def half(self, a):
        return pl.ds(pl.multiple_of(a * 2 * self.part, 2 * self.part), 2 * self.part)

    def quarter(self, a, b):
        return pl.ds(pl.multiple_of((2 * a + b) * self.part, self.part), self.part)


class Reduce:
    def __init__(self, ways, line, rows, cols, split, first, paired, does):
        self.ways, self.line, self.rows, self.cols, self.split = ways, line, rows, cols, split
        self.front, self.back = does != "back", does != "front"
        self.here = pl.ds(first, cols)
        self.part = cols // 4
        self.paired = paired

    def buffers(self):
        line, rows, cols, split, part = self.line, self.rows, self.cols, self.split, self.part
        hops, rest = line - 1, rows - split
        shapes = {}
        if self.front:
            shapes["own"] = (line, rows, cols)
            if not self.paired:
                shapes["near"] = (line, rows, cols)
            if rest:
                shapes["z_right"] = shapes["z_left"] = (hops, rest, cols)
            if split:
                shapes["x_half"] = (line, split, 2 * part)
        if self.back:
            if rest:
                shapes["z_half"] = (rest, 2 * part)
                shapes["z_part"] = (rest, part)
                if not self.front:
                    shapes["z_row"] = (rest, cols)
            if split:
                shapes["x_right"] = shapes["x_left"] = (hops, split, part)
            shapes["final"] = (rows, cols)
        if split:
            shapes["x_part"] = (line, split, part)
        return shapes

    def scratch(self):
        n = 2 + 2 * 2 * (self.line - 1) + 2 * 8
        return [pltpu.VMEM(shape, BF16) for shape in self.buffers().values()] + [
            pltpu.SemaphoreType.DMA((n,)),
            pltpu.SemaphoreType.DMA((n,)),
        ]

    def bind(self, place, source, final, refs):
        refs = list(refs)
        self.place, self.source, self.result = place, source, final
        for name in self.buffers():
            setattr(self, name, refs.pop(0))
        self.send, self.recv = refs
        self.orders = [Way(place, order, self.part) for order in (0, 1)]
        self.ids = {}
        return self

    def copy(self, key, src, dst, where):
        n = self.ids.setdefault(key, len(self.ids) + 1)
        return pltpu.make_async_remote_copy(
            src_ref=src, dst_ref=dst, send_sem=self.send.at[n], recv_sem=self.recv.at[n],
            device_id=where, device_id_type=MESH,
        )

    def core_copy(self):
        p = self.place
        return self.copy("core", self.source.at[:, 1 - p.core, :, self.here], self.near, p.other_core())

    def own_copy(self):
        p = self.place
        if self.paired:
            return pltpu.make_async_copy(self.source.at[:, :, self.here], self.own, self.send.at[0])
        return pltpu.make_async_copy(self.source.at[:, p.core, :, self.here], self.own, self.send.at[0])

    def done_copy(self):
        return pltpu.make_async_copy(self.final, self.result.at[:, self.here], self.send.at[0])

    def kind_rows(self, kind):
        return (0, self.split) if kind == "x" else (self.split, self.rows - self.split)

    def mine(self, kind, start, many, columns):
        if kind == "x":
            return self.own.at[:, pl.ds(start, many), columns]
        if not self.front:
            return self.z_row.at[pl.ds(start - self.split, many), columns]
        return self.own.at[self.place.z, pl.ds(start, many), columns]

    def landing(self, buffer, kind, start, many):
        return buffer.at[:, pl.ds(start, many)] if kind == "x" else buffer.at[pl.ds(start, many)]

    def scatter(self, kind, stage, order):
        way = self.orders[order]
        first, many = self.kind_rows(kind)
        many = many // 2
        at = order * many
        if stage == 1:
            columns, where, buffer = way.half(1 - way.a), way.first, self.x_half if kind == "x" else self.z_half
        else:
            columns, where, buffer = way.quarter(way.a, 1 - way.b), way.second, self.x_part if kind == "x" else self.z_part
        return self.copy(
            (kind, "scatter", stage, order),
            self.mine(kind, first + at, many, columns),
            self.landing(buffer, kind, at, many),
            self.place.plane(where),
        )

    def gather(self, kind, stage, order, arriving=False):
        way = self.orders[order]
        first, many = self.kind_rows(kind)
        many = many // 2
        rows = pl.ds(first + order * many, many)
        if stage == 1:
            columns, where = way.quarter(way.a, 1 - way.b if arriving else way.b), way.second
        else:
            columns, where = way.half(1 - way.a if arriving else way.a), way.first
        view = self.final.at[rows, columns]
        return self.copy((kind, "gather", stage, order), view, view, self.place.plane(where))

    def scatter_start(self, kind, stage):
        for order in (0, 1):
            self.scatter(kind, stage, order).start()

    def scatter_add(self, kind, stage):
        first, many = self.kind_rows(kind)
        many = many // 2
        for order in (0, 1):
            self.scatter(kind, stage, order).wait_recv()
        for order in (0, 1):
            way = self.orders[order]
            at = order * many
            columns = way.half(way.a) if stage == 1 else way.quarter(way.a, way.b)
            if kind == "x":
                buffer = self.x_half if stage == 1 else self.x_part

                def each(j, carry, buffer=buffer, columns=columns, at=at):
                    here = lambda r, n: self.own.at[j, pl.ds(first + at + r, n), columns]
                    came = lambda r, n: buffer.at[j, pl.ds(at + r, n)]
                    add_rows(*((here, [came]) if stage == 1 else (came, [here])), many, buffer.shape[-1])
                    return carry

                lax.fori_loop(0, self.line, each, 0)
            else:
                buffer = self.z_half if stage == 1 else self.z_part
                here = lambda r, n, at=at, columns=columns: self.mine("z", first + at + r, n, columns)
                came = lambda r, n, at=at, buffer=buffer: buffer.at[pl.ds(at + r, n)]
                add_rows(*((here, [came]) if stage == 1 else (came, [here])), many, buffer.shape[-1])

    def gather_start(self, kind, stage):
        if stage == 1:
            first, many = self.kind_rows(kind)
            many = many // 2
            for order in (0, 1):
                way = self.orders[order]
                rows = pl.ds(order * many, many)
                done = self.x_part[self.place.z, rows] if kind == "x" else self.z_part[rows]
                self.final[pl.ds(first + order * many, many), way.quarter(way.a, way.b)] = done
        for order in (0, 1):
            if stage == 2:
                self.gather(kind, 1, order, True).wait_recv()
            self.gather(kind, stage, order).start()

    def line_row(self, kind, j):
        if kind == "x":
            return self.x_part.at[j]
        return self.own.at[j, pl.ds(self.split, self.rows - self.split)]

    def line_in(self, kind, right):
        if kind == "x":
            return self.x_right if right else self.x_left
        return self.z_right if right else self.z_left

    def line_copy(self, kind, right, t, j):
        return self.copy(
            (kind, right, t),
            self.line_row(kind, j),
            self.line_in(kind, right).at[t - 1],
            self.place.along(1 if right else -1),
        )

    def line_step(self, kind, t):
        p, line = self.place, self.line
        for right in (True, False):
            at = p.z if right else line - 1 - p.z
            if t < line:
                j = line + p.z - t if right else p.z + t - line

                @pl.when(at <= t - 1)
                def _(right=right, at=at, j=j):
                    if t > 1:

                        @pl.when(at >= 1)
                        def _():
                            self.line_arrive(kind, right, t - 1, j)

                    self.line_copy(kind, right, t, j).start()

            else:

                @pl.when(at >= 1)
                def _(right=right):
                    self.line_arrive(kind, right, t - 1, p.z)

    def line_arrive(self, kind, right, t, j):
        buffer = self.line_in(kind, right)
        self.copy(
            (kind, right, t),
            self.line_row(kind, j),
            buffer.at[t - 1],
            self.place.along(-1 if right else 1),
        ).wait_recv()
        if kind == "x":
            mine = lambda r, n: self.x_part.at[j, pl.ds(r, n)]
        else:
            mine = lambda r, n: self.own.at[j, pl.ds(self.split + r, n)]
        add_rows(mine, [lambda r, n: buffer.at[t - 1, pl.ds(r, n)]], self.kind_rows(kind)[1], buffer.shape[-1])

    def line_sent(self, kind):
        p, line = self.place, self.line
        for t in range(1, line):
            for right in (True, False):
                at = p.z if right else line - 1 - p.z

                @pl.when(at <= t - 1)
                def _(right=right, t=t):
                    self.line_copy(kind, right, t, p.z).wait_send()

    def saved(self):
        shapes = []
        if self.rows - self.split:
            shapes.append((self.rows - self.split, self.cols))
        if self.split:
            shapes.append((self.line, self.split, self.part))
        return shapes

    def save(self, refs):
        refs = list(refs)
        if self.rows - self.split:
            refs.pop(0)[...] = self.own[self.place.z, pl.ds(self.split, self.rows - self.split)]
        if self.split:
            refs.pop(0)[...] = self.x_part[...]

    def resume(self, refs):
        refs = list(refs)
        if self.rows - self.split:
            self.z_row[...] = refs.pop(0)[...]
        if self.split:
            self.x_part[...] = refs.pop(0)[...]

    def phase(self, n):
        x, z = bool(self.split), bool(self.rows - self.split)
        if n == 0:
            self.own_copy().start()
            if not self.paired:
                self.core_copy().start()
        if n == 1:
            self.own_copy().wait()
            if not self.paired:
                self.core_copy().wait_recv()

                def one(j, carry):
                    add_rows(
                        lambda r, n: self.own.at[j, pl.ds(r, n)],
                        [lambda r, n: self.near.at[j, pl.ds(r, n)]],
                        self.rows,
                        self.cols,
                    )
                    return carry

                lax.fori_loop(0, self.line, one, 0)
            if x:
                self.scatter_start("x", 1)
        if z and 1 <= n <= 4:
            self.line_step("z", n)
        if x and n == 3:
            self.scatter_add("x", 1)
            self.scatter_start("x", 2)
        if n == 4:
            if x:
                self.scatter_add("x", 2)
                for order in (0, 1):
                    for stage in (1, 2):
                        self.scatter("x", stage, order).wait_send()
            if z:
                self.line_sent("z")
            if not self.paired:
                self.core_copy().wait_send()
        if z and n == 5:
            self.scatter_start("z", 1)
        if x and 5 <= n <= 8:
            self.line_step("x", n - 4)
        if z and n == 6:
            self.scatter_add("z", 1)
            self.scatter_start("z", 2)
        if z and n == 7:
            self.scatter_add("z", 2)
            self.gather_start("z", 1)
        if n == 8:
            if x:
                self.gather_start("x", 1)
            if z:
                self.gather_start("z", 2)
        if x and n == 9:
            self.gather_start("x", 2)
        if n == 10:
            for kind, there in (("x", x), ("z", z)):
                if there:
                    for order in (0, 1):
                        self.gather(kind, 2, order, True).wait_recv()
                        for stage in (1, 2):
                            self.gather(kind, stage, order).wait_send()
                            if kind == "z":
                                self.scatter(kind, stage, order).wait_send()
            if x:
                self.line_sent("x")
            self.done_copy().start()
        if n == 11:
            self.done_copy().wait()


class Sums:
    def __init__(self, ways, line, rows, cols, shares, plan, paired=False, does="all"):
        width = cols // len(shares)
        self.shape, self.plan, self.does = (rows, cols), plan, does
        self.parts = [
            Reduce(ways, line, rows, width, int(rows * share) // 32 * 32, i * width, paired, does)
            for i, share in enumerate(shares)
        ]

    def out(self):
        if self.does == "front":
            return [(whole(v), jax.ShapeDtypeStruct(v, BF16)) for part in self.parts for v in part.saved()]
        return [(pl.BlockSpec(memory_space=pl.ANY), jax.ShapeDtypeStruct(self.shape, BF16))]

    def ins(self):
        if self.does == "back":
            return [whole(v) for part in self.parts for v in part.saved()]
        return [pl.BlockSpec(memory_space=pl.ANY)]

    def scratch(self):
        return [s for part in self.parts for s in part.scratch()]

    def bind(self, place, sources, finals, refs):
        refs = list(refs)
        self.sources, self.finals = sources, finals
        for part in self.parts:
            many = len(part.scratch())
            part.bind(place, sources[0], finals[0], refs[:many])
            refs = refs[many:]

    def phase(self, n):
        if n == 5 and self.does == "back":
            refs = list(self.sources)
            for part in self.parts:
                many = len(part.saved())
                part.resume(refs[:many])
                refs = refs[many:]
        for part in self.parts:
            part.phase(n)
        if n == 4 and self.does == "front":
            refs = list(self.finals)
            for part in self.parts:
                many = len(part.saved())
                part.save(refs[:many])
                refs = refs[many:]


class Swap:
    def __init__(self, ways, rows, cols, plan):
        self.ways, self.shape, self.plan = ways, (ways, rows, cols), plan

    def scratch(self):
        return [pltpu.SemaphoreType.DMA((self.ways,)), pltpu.SemaphoreType.DMA((self.ways,))]

    def out(self):
        return [(pl.BlockSpec(memory_space=pl.ANY), jax.ShapeDtypeStruct(self.shape, BF16))]

    def ins(self):
        return [pl.BlockSpec(memory_space=pl.ANY)]

    def bind(self, place, sources, finals, refs):
        self.place, self.source, self.final = place, sources[0], finals[0]
        self.send, self.recv = refs

    def copy(self, k, slot):
        return pltpu.make_async_remote_copy(
            src_ref=self.source.at[k], dst_ref=self.final.at[slot],
            send_sem=self.send.at[k], recv_sem=self.recv.at[k],
            device_id=self.place.plane(k), device_id_type=MESH,
        )

    def stay(self):
        return pltpu.make_async_copy(self.source.at[0], self.final.at[self.place.me], self.send.at[0])

    def phase(self, n):
        p = self.place
        if n == 0:
            self.stay().start()
            for k in range(1, self.ways - 1):
                self.copy(k, p.me).start()
        if n == 1:
            self.copy(self.ways - 1, p.me).start()
        if n == 2:
            self.stay().wait()
            for k in range(1, self.ways):
                self.copy(k, p.partner(k)).wait_recv()
                self.copy(k, p.me).wait_send()


class PairSum:
    def __init__(self, line, rows, cols, steps, piece, cut):
        self.shape, self.steps, self.piece, self.cut = (line, rows, cols), steps, piece, cut

    def out(self):
        return pl.BlockSpec(memory_space=pl.ANY), jax.ShapeDtypeStruct(self.shape, BF16)

    def scratch(self):
        line, rows, cols = self.piece
        sems = [pltpu.SemaphoreType.DMA((self.steps,))] * 3
        return [pltpu.VMEM((3, line, 2, rows, cols), BF16), pltpu.VMEM(self.shape, BF16)] + sems

    def bind(self, place, final, refs):
        self.place, self.final = place, final
        self.stage, self.near, self.send, self.recv, self.leave = refs

    def copy(self, i):
        p = self.place
        return pltpu.make_async_remote_copy(
            src_ref=self.stage.at[lax.rem(i, 3), :, 1 - p.core], dst_ref=self.near.at[self.cut(i)],
            send_sem=self.send.at[i], recv_sem=self.recv.at[i],
            device_id=p.other_core(), device_id_type=MESH,
        )

    def leaving(self, i):
        at = self.cut(i)
        return pltpu.make_async_copy(self.near.at[at], self.final.at[at], self.leave.at[i])

    def push(self, i, value):
        line, rows, cols = self.piece
        self.stage[lax.rem(i, 3)] = value.reshape(line, 2, rows, cols)
        self.copy(i).start()

    def take_late(self, i):
        pl.when(i >= 2)(lambda: self.take(i - 2))

    def take_rest(self, i):
        self.take(i - 1)
        self.take(i)
        for n in range(self.steps):
            self.leaving(n).wait()

    def take(self, i):
        line, rows, cols = self.piece
        self.copy(i).wait_recv()
        self.copy(i).wait_send()
        at = self.cut(i)
        for j in range(line):
            here = (pl.ds(at[0].start + j, 1),) + at[1:]
            self.near[here] = (self.stage[lax.rem(i, 3), j, self.place.core] + self.near[here][0])[None]
        self.leaving(i).start()


class Side:
    def __init__(self, ways, line, jobs):
        self.ways, self.line, self.jobs = ways, line, jobs

    def in_specs(self):
        return [spec for job in self.jobs for spec in job.ins()]

    def out_specs(self):
        return [spec for job in self.jobs for spec, _ in job.out()]

    def out_shape(self):
        return [shape for job in self.jobs for _, shape in job.out()]

    def scratch(self):
        return [s for job in self.jobs for s in job.scratch()]

    def bind(self, sources, finals, refs):
        refs, finals = list(refs), list(finals)
        self.place = Place(self.ways, self.line)
        for job, source in zip(self.jobs, sources):
            many, outs = len(job.scratch()), len(job.out())
            job.bind(self.place, source, finals[:outs], refs[:many])
            refs, finals = refs[many:], finals[outs:]

    def at(self, i, point):
        for job in self.jobs:
            for n in range(12):
                if n in job.plan and job.plan[n][1] == point:
                    if isinstance(i, int):
                        job.phase(n)
                    else:
                        pl.when(i == job.plan[n][0])(functools.partial(job.phase, n))


def remote_params(ident):
    return pltpu.CompilerParams(vmem_limit_bytes=VMEM, collective_id=ident, has_side_effects=True)


def mlp_kernel(pieces, *refs):
    x, mixed, w_out, own_rows = refs[:4]
    cots = refs[4 : 4 + pieces]
    w_up, hidden, ready, gout, act, slope, grad_down = refs[4 + pieces :]
    rows = cots[0].shape[0]

    @pl.when(pl.program_id(0) == 0)
    def _():
        for k in range(pieces):
            span = slice(k * rows, (k + 1) * rows)
            gout[span] = cots[k][...] * own_rows[2:3].astype(BF16)
            h = x[span].astype(F32) + tn(mixed[:, span], w_out[...])
            hidden[span] = h
            ready[span] = (norm_rows(h)[0] * own_rows[1:2]).astype(BF16)

    u = nn(ready[...], w_up[...])
    u2 = u * u
    t = jnp.tanh(u * (GELU_C + (GELU_C * GELU_K) * u2))
    half = 0.5 + 0.5 * t
    a = (u * half).astype(BF16)
    act[...] = a
    slope[...] = (half + u * (1 - t * t) * (0.5 * GELU_C + (1.5 * GELU_C * GELU_K) * u2)).astype(BF16)
    grad_down[...] = tn(a, gout[...]).astype(BF16)


def mlp(x, mixed, w_out, own_rows, cots, w_up):
    length, width = x.shape
    inner = w_up.shape[1]
    rows = length // len(cots)
    block = min(1024, inner)
    cols = pl.BlockSpec((length, block), lambda i: (0, i))
    return pl.pallas_call(
        functools.partial(mlp_kernel, len(cots)),
        grid=(inner // block,),
        in_specs=[
            whole((length, width)),
            whole((length, width)),
            whole((width, width)),
            whole((8, width)),
        ]
        + [whole((rows, width))] * len(cots)
        + [pl.BlockSpec((width, block), lambda i: (0, i))],
        out_specs=[whole((length, width))] * 3 + [cols, cols, pl.BlockSpec((block, width), lambda i: (i, 0))],
        out_shape=[
            jax.ShapeDtypeStruct((length, width), F32),
            jax.ShapeDtypeStruct((length, width), BF16),
            jax.ShapeDtypeStruct((length, width), BF16),
            jax.ShapeDtypeStruct((length, inner), BF16),
            jax.ShapeDtypeStruct((length, inner), BF16),
            jax.ShapeDtypeStruct((inner, width), BF16),
        ],
        compiler_params=params(),
        name="mlp",
    )(x, mixed, w_out, own_rows, *cots, w_up)


def mlp_back_kernel(side, *refs):
    gout, act, slope, w_down, ready, hidden, source = refs[:7]
    many = len(side.out_shape())
    out, grad_upward, grad_up = refs[7:10]
    out_sum = refs[10 + many]
    side.bind([[source]], refs[10 : 10 + many], refs[11 + many :])
    i = pl.program_id(0)
    last = pl.num_programs(0) - 1

    @pl.when(i == 0)
    def _():
        side.place.hail()
        out_sum[...] = hidden[...]
        side.place.greet()

    side.at(i, 0)
    gu = (nt(gout[...], w_down[...]) * slope[...].astype(F32)).astype(BF16)
    grad_upward[...] = gu
    grad_up[...] = tn(ready[...], gu).astype(BF16)
    side.at(i, 1)
    out_sum[...] += nn(act[...], w_down[...])

    @pl.when(i == last)
    def _():
        out[...] = out_sum[...].astype(BF16)
        side.at(i, "end")


def mlp_back(gout, act, slope, w_down, ready, hidden, grad_down, ways):
    length, width = gout.shape
    inner = w_down.shape[0]
    line, _, down_rows, _ = grad_down.shape
    block = inner // 8
    cols = pl.BlockSpec((length, block), lambda i: (0, i))
    square = whole((length, width))
    plan = {0: (0, 0), 1: (2, 0), 2: (4, 1), 3: (7, 0), 4: (7, "end")}
    side = Side(ways, line, [Sums(ways, line, down_rows, width, DOWN_SHARES, plan, False, "front")])
    return pl.pallas_call(
        functools.partial(mlp_back_kernel, side),
        grid=(8,),
        in_specs=[
            square,
            cols,
            cols,
            pl.BlockSpec((block, width), lambda i: (i, 0)),
            square,
            square,
        ]
        + side.in_specs(),
        out_specs=[square, cols, pl.BlockSpec((width, block), lambda i: (0, i))] + side.out_specs(),
        out_shape=[
            jax.ShapeDtypeStruct((length, width), BF16),
            jax.ShapeDtypeStruct((length, inner), BF16),
            jax.ShapeDtypeStruct((width, inner), BF16),
        ]
        + side.out_shape(),
        scratch_shapes=[pltpu.VMEM((length, width), F32)] + side.scratch(),
        compiler_params=remote_params(2),
        name="mlp_back",
    )(gout, act, slope, w_down, ready, hidden, grad_down)


def attn_back_kernel(side, pair_sum, bq, *refs):
    gu, w_up, hidden, gout, own_rows, mixed, w_out, packed, aux, w_qkv, ready, x = refs[:12]
    back_from = len(side.jobs[0].ins())
    carried, source_up, source_out = refs[12 : 12 + back_from], refs[12 + back_from], refs[13 + back_from]
    refs = refs[14 + back_from :]
    grad_qkv, grad_x, table_attn, table_mlp = refs[:4]
    many = len(side.out_shape())
    finals, refs = refs[4 : 4 + many], refs[4 + many :]
    back_sum, grad_hidden, grad_mixed, spare, grad_out, late = refs[:6]
    pairing = len(pair_sum.scratch())
    side.bind([carried, [source_up], [grad_out], [source_out]], finals, refs[6 + pairing :])
    pair_sum.bind(side.place, grad_qkv, refs[6 : 6 + pairing])
    i = pl.program_id(0)
    steps = pl.num_programs(0) // 2
    length, width = gout.shape
    span = math.gcd(length, 256)
    load_hidden = pltpu.make_async_copy(hidden, grad_hidden, late.at[0])
    load_w = pltpu.make_async_copy(w_out, spare, late.at[1])
    load_gout = pltpu.make_async_copy(gout, grad_x, late.at[2])
    load_x = pltpu.make_async_copy(x, spare, late.at[3])

    @pl.when(i == 0)
    def _():
        side.place.hail()
        load_hidden.start()
        load_w.start()
        load_gout.start()
        back_sum[...] = jnp.zeros_like(back_sum)

    pl.when(i == 1)(side.place.greet)
    side.at(i, 0)

    @pl.when(i < steps)
    def _():
        back_sum[...] += nt(gu[...], w_up[...])

    @pl.when(i == steps - 1)
    def _():
        load_hidden.wait()
        load_w.wait()
        load_gout.wait()
        total = jnp.zeros((1, width), F32)
        for r in range(length // span):
            here = slice(r * span, (r + 1) * span)
            normed, inverse = norm_rows(grad_hidden[here])
            g = back_sum[here]
            total = total + jnp.sum(g * normed, axis=0, keepdims=True)
            grad_hidden[here] = grad_x[here].astype(F32) + norm_back(g * own_rows[1:2], normed, inverse)
        table_mlp[...] = total
        side.at(i, "norm")
        low = grad_hidden[...].astype(BF16)
        grad_mixed[...] = nt(spare[...], low).astype(BF16)
        load_x.start()
        grad_out[...] = nn(mixed[...], low).astype(BF16).reshape(grad_out.shape)
        back_sum[...] = jnp.zeros_like(back_sum)
        side.at(i, "out")

    @pl.when(i >= steps)
    def _():
        pair = i - steps
        pair_sum.take_late(pair)
        rows = pl.ds(pl.multiple_of(pair * 2 * HEAD, 2 * HEAD), 2 * HEAD)
        parts = attend_back_head(packed, mixed[rows], aux, grad_mixed[rows], bq, 0)
        side.at(i, "mid")
        parts = parts + attend_back_head(packed, mixed[rows], aux, grad_mixed[rows], bq, 1)
        side.at(i, 1)
        gp = jnp.concatenate(parts, axis=0)
        pair_sum.push(pair, nt(ready[...], gp).astype(BF16))
        back_sum[...] += tn(gp, w_qkv[...])
        side.at(i, 2)

    @pl.when(i == pl.num_programs(0) - 1)
    def _():
        load_x.wait()
        total = jnp.zeros((1, width), F32)
        for r in range(length // span):
            here = slice(r * span, (r + 1) * span)
            normed, inverse = norm_rows(spare[here].astype(F32))
            g = back_sum[here]
            total = total + jnp.sum(g * normed, axis=0, keepdims=True)
            grad_x[here] = (grad_hidden[here] + norm_back(g * own_rows[0:1], normed, inverse)).astype(BF16)
        table_attn[...] = total
        pair_sum.take_rest(i - steps)
        side.at(i, "end")


def attn_back(gu, w_up, hidden, gout, own_rows, mixed, w_out, packed, aux, w_qkv, ready, x, carried, grad_up, out, ways):
    length, width = gout.shape
    inner = w_up.shape[1]
    cols = packed.shape[0]
    pairs = cols // (6 * HEAD)
    line, _, rows, _ = grad_up.shape
    block = inner // pairs
    square = whole((length, width))
    remote = pl.BlockSpec(memory_space=pl.ANY)
    first = lambda i: jnp.minimum(i, pairs - 1)
    second = lambda i: jnp.maximum(i - pairs, 0)
    plan_down = {5: (1, 0), 6: (5, 0), 7: (7, 0), 8: (7, "norm"), 9: (8, "mid"), 10: (9, 0), 11: (15, "end")}
    plan_up = {
        0: (1, 0), 1: (7, 0), 2: (8, 1), 3: (10, "mid"), 4: (12, 1), 5: (12, 1),
        6: (13, 0), 7: (13, 1), 8: (14, 0), 9: (14, "mid"), 10: (15, 0), 11: (15, "end"),
    }
    plan_out = {
        0: (7, "out"), 1: (8, "mid"), 2: (9, "mid"), 3: (11, 0), 4: (12, 2), 5: (12, 2),
        6: (13, "mid"), 7: (13, 2), 8: (14, "mid"), 9: (14, 1), 10: (15, "mid"), 11: (15, "end"),
    }
    plan_swap = {0: (8, "mid"), 1: (10, 1), 2: (15, 1)}
    side = Side(
        ways,
        line,
        [
            Sums(ways, line, inner // (2 * line), width, DOWN_SHARES, plan_down, False, "back"),
            Sums(ways, line, rows, inner, UP_SHARES, plan_up),
            Sums(ways, line, rows, width, OUT_SHARES, plan_out),
            Swap(ways, length // ways, width, plan_swap),
        ],
    )
    wide = 6 * HEAD
    pair_sum = PairSum(
        line, rows, cols, pairs, (line, rows, wide),
        lambda i: (pl.ds(0, line), slice(None), pl.ds(pl.multiple_of(i * wide, wide), wide)),
    )
    inner_jobs = side.jobs[0].ins() + [remote, remote]
    return pl.pallas_call(
        functools.partial(attn_back_kernel, side, pair_sum, math.gcd(length, 256)),
        grid=(2 * pairs,),
        in_specs=[
            pl.BlockSpec((length, block), lambda i: (0, first(i))),
            pl.BlockSpec((width, block), lambda i: (0, first(i))),
            remote,
            remote,
            whole((8, width)),
            whole((width, length)),
            remote,
            pl.BlockSpec((wide, length), lambda i: (second(i), 0)),
            pl.BlockSpec((None, 8, length), lambda i: (second(i), 0, 0)),
            pl.BlockSpec((wide, width), lambda i: (second(i), 0)),
            whole((width, length)),
            remote,
        ]
        + inner_jobs,
        out_specs=[pair_sum.out()[0], square, whole((1, width)), whole((1, width))] + side.out_specs(),
        out_shape=[
            pair_sum.out()[1],
            jax.ShapeDtypeStruct((length, width), BF16),
            jax.ShapeDtypeStruct((1, width), F32),
            jax.ShapeDtypeStruct((1, width), F32),
        ]
        + side.out_shape(),
        scratch_shapes=[
            pltpu.VMEM((length, width), F32),
            pltpu.VMEM((length, width), F32),
            pltpu.VMEM((width, length), BF16),
            pltpu.VMEM((length, width), BF16),
            pltpu.VMEM((line, 2, rows, width), BF16),
            pltpu.SemaphoreType.DMA((4,)),
        ]
        + pair_sum.scratch()
        + side.scratch(),
        compiler_params=remote_params(3),
        name="attn_back",
    )(gu, w_up, hidden, gout, own_rows, mixed, w_out, packed, aux, w_qkv, ready, x, *carried, grad_up, out)


def tail_kernel(side, *refs):
    jobs = len(side.jobs)
    side.bind([[ref] for ref in refs[:jobs]], refs[jobs : 2 * jobs], refs[2 * jobs :])
    side.place.hail()
    side.place.greet()
    for n in range(12):
        side.at(0, n)
        side.at(0, ("after", n))


def tail(ways, line, sums, pieces):
    plan = {n: (0, n) for n in range(12)}
    jobs = [Sums(ways, line, v.shape[-2], v.shape[-1], shares, plan, paired) for v, shares, paired in sums]
    side = Side(ways, line, jobs + [Swap(ways, pieces.shape[1], pieces.shape[2], {0: (0, ("after", 1)), 1: (0, ("after", 3)), 2: (0, 11)})])
    arrays = [v for v, _, _ in sums] + [pieces]
    return pl.pallas_call(
        functools.partial(tail_kernel, side),
        in_specs=[pl.BlockSpec(memory_space=pl.ANY)] * len(arrays),
        out_specs=side.out_specs(),
        out_shape=side.out_shape(),
        scratch_shapes=side.scratch(),
        compiler_params=remote_params(4),
        name="tail",
    )(*arrays)


def finish_kernel(groups, *refs):
    refs = list(refs)
    sources = [[refs.pop(0) for _ in range(many)] for many in groups]
    for parts, target in zip(sources, refs):
        at = 0
        for part in parts:
            cols = part.shape[-1]
            target[..., at : at + cols] = part[...].astype(target.dtype)
            at += cols


def finish(groups, kinds, steps):
    arrays = [v for group in groups for v in group]
    wholes = [
        jax.ShapeDtypeStruct(group[0].shape[:-1] + (sum(v.shape[-1] for v in group),), kind)
        for group, kind in zip(groups, kinds)
    ]

    def spec(v):
        block = (v.shape[0] // steps,) + v.shape[1:]
        zeros = (0,) * (v.ndim - 1)
        return pl.BlockSpec(block, lambda i: (i,) + zeros)

    return pl.pallas_call(
        functools.partial(finish_kernel, [len(group) for group in groups]),
        grid=(steps,),
        in_specs=[spec(v) for v in arrays],
        out_specs=[spec(v) for v in wholes],
        out_shape=wholes,
        compiler_params=params(),
        name="finish",
    )(*arrays)


def exchange(pieces, me, ways):
    return [pieces[0]] + [
        lax.ppermute(pieces[k], "seq", [(s, s ^ k) for s in range(ways)]) for k in range(1, ways)
    ]


def by_partner(slots, me, ways):
    return [lax.dynamic_index_in_dim(slots, me ^ k, 0, keepdims=False) for k in range(ways)]


def body(tokens, cotangent, bins, live_count, w_qkv, w_out, w_up, w_down, gain_attn, gain_mlp):
    slots, rows, width = tokens.shape
    ways = lax.axis_size("seq")
    batch_ways = lax.axis_size("batch")
    line = batch_ways // 2
    me = lax.axis_index("seq")
    x, ready_attn, packed, w_turned, own_rows = entry(bins, live_count, tokens, gain_attn, gain_mlp, w_qkv)
    packed, later = lax.optimization_barrier((packed, cotangent))
    cots = exchange(by_partner(later, me, ways), me, ways)
    mixed, aux = attend(packed)
    hidden, ready_mlp, gout, act, slope, grad_down = mlp(x, mixed, w_out, own_rows, cots, w_up)

    def blocks(v):
        return v.reshape(line, 2, v.shape[0] // batch_ways, v.shape[1])

    out, grad_upward, grad_up, *carried = mlp_back(
        gout, act, slope, w_down, ready_mlp, hidden, blocks(grad_down), ways
    )
    qkv_pair, grad_x, row_attn, row_mlp, sum_down, sum_up, sum_out, output = attn_back(
        grad_upward, w_up, hidden, gout, own_rows, mixed, w_out, packed, aux, w_turned, ready_attn, x,
        carried, blocks(grad_up), out.reshape(ways, rows, width), ways,
    )
    own_bin = lax.dynamic_index_in_dim(bins, me, 0)
    onehot = (jnp.arange(gain_attn.shape[0], dtype=jnp.int32) == own_bin[0]).astype(F32)[:, None]
    bins_here = gain_attn.shape[0] // batch_ways
    tables = jnp.concatenate(
        [(onehot * v).reshape(batch_ways, bins_here, width) for v in (row_attn, row_mlp)], axis=1
    )
    tables = tables.astype(BF16).reshape(line, 2, 32, -1)
    sum_qkv, sum_tables, grad_tokens = tail(
        ways,
        line,
        [(qkv_pair, QKV_SHARES, True), (tables, (0,), False)],
        grad_x.reshape(ways, rows, width),
    )
    sum_tables = sum_tables.reshape(2 * bins_here, width)
    fine = (2 * ways, slots * rows // (2 * ways), width)
    output, grad_tokens, *sums = finish(
        (
            [output.reshape(fine)],
            [grad_tokens.reshape(fine)],
            [sum_qkv],
            [sum_out],
            [sum_up],
            [sum_down],
        ),
        (BF16,) + (F32,) * 5,
        2 * ways,
    )
    return (
        output.reshape(tokens.shape),
        grad_tokens.reshape(tokens.shape),
        *sums,
        sum_tables[:bins_here].astype(F32),
        sum_tables[bins_here:].astype(F32),
    )


def plain_norm(values_in):
    centred = values_in - jnp.mean(values_in, axis=-1, keepdims=True)
    inverse = lax.rsqrt(jnp.mean(centred * centred, axis=-1, keepdims=True) + 1e-05)
    return (centred * inverse, inverse)


def plain_norm_back(grad_normed, normed, inverse):
    first_mean = jnp.mean(grad_normed, axis=-1, keepdims=True)
    second_mean = jnp.mean(grad_normed * normed, axis=-1, keepdims=True)
    return inverse * (grad_normed - first_mean - normed * second_mean)


def plain_weight_grad(left, right):
    return lax.dot_general(
        left, right, (((0,), (0,)), ((), ())), preferred_element_type=jnp.float32
    )


def plain_heads(packed, heads_here):
    shaped = packed.reshape(packed.shape[0], heads_here, 3, -1)
    return (shaped[:, :, 0], shaped[:, :, 1], shaped[:, :, 2])


def plain_attend(packed, heads_here, block_rows):
    queries, key_rows, values = plain_heads(packed, heads_here)
    length, head_size = (queries.shape[0], queries.shape[2])
    factor = head_size ** (-0.5)
    blocked = queries.reshape(length // block_rows, block_rows, heads_here, head_size)

    def per_block(query_block):
        scores = (
            jnp.einsum("qhd,khd->hqk", query_block, key_rows, preferred_element_type=jnp.float32)
            * factor
        )
        row_max = jnp.max(scores, axis=-1, keepdims=True)
        logsum = row_max + jnp.log(jnp.sum(jnp.exp(scores - row_max), axis=-1, keepdims=True))
        softmax_rows = jnp.exp(scores - logsum).astype(jnp.bfloat16)
        mixed_rows = jnp.einsum(
            "hqk,khd->qhd", softmax_rows, values, preferred_element_type=jnp.float32
        )
        return (
            mixed_rows.astype(jnp.bfloat16).reshape(block_rows, heads_here * head_size),
            logsum[..., 0],
        )

    mixed_rows, logsum = lax.map(per_block, blocked)
    return (mixed_rows.reshape(length, heads_here * head_size), logsum)


def plain_attend_back(packed, logsum, grad_mixed, heads_here, block_rows):
    queries, key_rows, values = plain_heads(packed, heads_here)
    length, head_size = (queries.shape[0], queries.shape[2])
    factor = head_size ** (-0.5)
    count_blocks = length // block_rows
    query_blocks = queries.reshape(count_blocks, block_rows, heads_here, head_size)
    grad_blocks = grad_mixed.reshape(count_blocks, block_rows, heads_here, head_size)

    def per_block(running, pieces):
        query_block, grad_block, logsum_block = pieces
        scores = (
            jnp.einsum("qhd,khd->hqk", query_block, key_rows, preferred_element_type=jnp.float32)
            * factor
        )
        softmax_rows = jnp.exp(scores - logsum_block[..., None])
        grad_values = running[1] + jnp.einsum(
            "hqk,qhd->khd",
            softmax_rows.astype(jnp.bfloat16),
            grad_block,
            preferred_element_type=jnp.float32,
        )
        grad_soft = jnp.einsum(
            "qhd,khd->hqk", grad_block, values, preferred_element_type=jnp.float32
        )
        inner = jnp.sum(softmax_rows * grad_soft, axis=-1, keepdims=True)
        grad_scores = (softmax_rows * (grad_soft - inner)).astype(jnp.bfloat16)
        grad_query = (
            jnp.einsum("hqk,khd->qhd", grad_scores, key_rows, preferred_element_type=jnp.float32)
            * factor
        )
        grad_keys = (
            running[0]
            + jnp.einsum(
                "hqk,qhd->khd", grad_scores, query_block, preferred_element_type=jnp.float32
            )
            * factor
        )
        return ((grad_keys, grad_values), grad_query)

    zeros_start = jnp.zeros((length, heads_here, head_size), jnp.float32)
    (grad_keys, grad_values), grad_queries = lax.scan(
        per_block, (zeros_start, zeros_start), (query_blocks, grad_blocks, logsum)
    )
    grad_queries = grad_queries.reshape(length, heads_here, head_size)
    stacked = jnp.stack([grad_queries, grad_keys, grad_values], axis=2)
    return stacked.reshape(length, heads_here * 3 * head_size).astype(jnp.bfloat16)


def plain_body(tokens, cotangent, bins, live_count, w_qkv, w_out, w_up, w_down, gain_attn, gain_mlp):
    slot_count, local_rows, model_width = tokens.shape
    seq_ways = lax.axis_size("seq")
    heads_here = HEADS // seq_ways
    length = local_rows * seq_ways
    block_rows = math.gcd(length, 512)
    row_count = slot_count * local_rows
    table_rows = gain_attn.shape[0]
    onehot = (bins[:, None] == jnp.arange(table_rows, dtype=jnp.int32)[None, :]).astype(jnp.float32)
    gains_attn = jnp.dot(onehot, gain_attn, precision=lax.Precision.HIGHEST)[:, None, :]
    gains_mlp = jnp.dot(onehot, gain_mlp, precision=lax.Precision.HIGHEST)[:, None, :]
    inputs = tokens.astype(jnp.float32)

    def attention_part():
        normed_attn, inverse_attn = plain_norm(inputs)
        ready_attn = (normed_attn * gains_attn).astype(jnp.bfloat16).reshape(row_count, model_width)
        packed = jnp.dot(ready_attn, w_qkv, preferred_element_type=jnp.float32).astype(jnp.bfloat16)
        packed = packed.reshape(slot_count, local_rows, 3 * model_width)
        item_rows = lax.all_to_all(packed, "seq", split_axis=2, concat_axis=1, tiled=True)
        mixed_items, logsum_items = lax.map(
            lambda single: plain_attend(single, heads_here, block_rows), item_rows
        )
        mixed_rows = lax.all_to_all(
            mixed_items, "seq", split_axis=1, concat_axis=2, tiled=True
        ).reshape(row_count, model_width)
        return (normed_attn, inverse_attn, ready_attn, item_rows, logsum_items, mixed_rows)

    def mlp_part(hidden):
        normed_mlp, inverse_mlp = plain_norm(hidden)
        ready_mlp = (normed_mlp * gains_mlp).astype(jnp.bfloat16).reshape(row_count, model_width)
        upward = jnp.dot(ready_mlp, w_up, preferred_element_type=jnp.float32)
        active = jax.nn.gelu(upward).astype(jnp.bfloat16)
        return (normed_mlp, inverse_mlp, ready_mlp, upward, active)

    saved_attn = attention_part()
    attended = jnp.dot(saved_attn[5], w_out, preferred_element_type=jnp.float32)
    hidden = inputs + attended.reshape(slot_count, local_rows, model_width)
    saved_mlp = mlp_part(hidden)
    branch = jnp.dot(saved_mlp[4], w_down, preferred_element_type=jnp.float32)
    output = (hidden + branch.reshape(slot_count, local_rows, model_width)).astype(jnp.bfloat16)
    saved_attn = attention_part()
    saved_mlp = mlp_part(hidden)
    normed_attn, inverse_attn, ready_attn, packed_heads, logsum, mixed_rows = saved_attn
    normed_mlp, inverse_mlp, ready_mlp, upward, active = saved_mlp
    alive_mask = (jnp.arange(slot_count, dtype=jnp.int32) < live_count[0]).astype(jnp.float32)
    grad_output = cotangent.astype(jnp.float32) * alive_mask[:, None, None]
    low_output = grad_output.astype(jnp.bfloat16).reshape(row_count, model_width)
    grad_down = plain_weight_grad(active, low_output)
    grad_active = jnp.dot(low_output, w_down.T, preferred_element_type=jnp.float32)
    gelu_values, gelu_pull = jax.vjp(jax.nn.gelu, upward)
    grad_upward = gelu_pull(grad_active)[0].astype(jnp.bfloat16)
    grad_up = plain_weight_grad(ready_mlp, grad_upward)
    grad_ready_mlp = jnp.dot(grad_upward, w_up.T, preferred_element_type=jnp.float32).reshape(
        slot_count, local_rows, model_width
    )
    table_mlp = jnp.dot(
        onehot.T, jnp.sum(grad_ready_mlp * normed_mlp, axis=1), precision=lax.Precision.HIGHEST
    )
    grad_hidden = grad_output + plain_norm_back(grad_ready_mlp * gains_mlp, normed_mlp, inverse_mlp)
    low_hidden = grad_hidden.astype(jnp.bfloat16).reshape(row_count, model_width)
    grad_out = plain_weight_grad(mixed_rows, low_hidden)
    grad_mixed = jnp.dot(low_hidden, w_out.T, preferred_element_type=jnp.float32).astype(
        jnp.bfloat16
    )
    grad_mixed = grad_mixed.reshape(slot_count, local_rows, model_width)
    grad_mixed_heads = lax.all_to_all(grad_mixed, "seq", split_axis=2, concat_axis=1, tiled=True)
    grad_packed_heads = lax.map(
        lambda pieces: plain_attend_back(pieces[0], pieces[1], pieces[2], heads_here, block_rows),
        (packed_heads, logsum, grad_mixed_heads),
    )
    grad_packed = lax.all_to_all(
        grad_packed_heads, "seq", split_axis=1, concat_axis=2, tiled=True
    ).reshape(row_count, 3 * model_width)
    grad_qkv = plain_weight_grad(ready_attn, grad_packed)
    grad_ready_attn = jnp.dot(grad_packed, w_qkv.T, preferred_element_type=jnp.float32).reshape(
        slot_count, local_rows, model_width
    )
    table_attn = jnp.dot(
        onehot.T, jnp.sum(grad_ready_attn * normed_attn, axis=1), precision=lax.Precision.HIGHEST
    )
    grad_tokens = grad_hidden + plain_norm_back(grad_ready_attn * gains_attn, normed_attn, inverse_attn)
    gradients = (grad_qkv, grad_out, grad_up, grad_down, table_attn, table_mlp)
    shares = (
        lax.psum_scatter(gradients[0], "batch", scatter_dimension=0, tiled=True),
        lax.psum_scatter(gradients[1], "batch", scatter_dimension=0, tiled=True),
        lax.psum_scatter(gradients[2], "batch", scatter_dimension=0, tiled=True),
        lax.psum_scatter(gradients[3], "batch", scatter_dimension=0, tiled=True),
        lax.psum_scatter(gradients[4], "batch", scatter_dimension=0, tiled=True),
        lax.psum_scatter(gradients[5], "batch", scatter_dimension=0, tiled=True),
    )
    summed = (
        lax.psum(shares[0].astype(jnp.bfloat16), "seq").astype(jnp.float32),
        lax.psum(shares[1].astype(jnp.bfloat16), "seq").astype(jnp.float32),
        lax.psum(shares[2].astype(jnp.bfloat16), "seq").astype(jnp.float32),
        lax.psum(shares[3].astype(jnp.bfloat16), "seq").astype(jnp.float32),
        lax.psum(shares[4].astype(jnp.bfloat16), "seq").astype(jnp.float32),
        lax.psum(shares[5].astype(jnp.bfloat16), "seq").astype(jnp.float32),
    )
    return (output, grad_tokens, summed[0], summed[1], summed[2], summed[3], summed[4], summed[5])


def solution(mesh):
    placed = (
        P("batch", "seq", None),
        P("batch", "seq", None),
        P("batch"),
        P("batch"),
        P(),
        P(),
        P(),
        P(),
        P(),
        P(),
    )
    fits = mesh.shape["seq"] == 4 and mesh.shape["batch"] == 8
    return jax.shard_map(
        body if fits else plain_body,
        mesh=mesh,
        in_specs=placed,
        out_specs=(
            P("batch", "seq", None),
            P("batch", "seq", None),
            P("batch", None),
            P("batch", None),
            P("batch", None),
            P("batch", None),
            P("batch", None),
            P("batch", None),
        ),
        check_vma=False,
    )
```

```python
import functools
import math

import jax
import jax.numpy as jnp
from jax import lax
from jax.experimental import pallas as pl
from jax.experimental.pallas import tpu as pltpu
from jax.sharding import PartitionSpec as P

F32 = jnp.float32
BF16 = jnp.bfloat16
HEAD = 64
HEADS = 16
LOG2E = math.log2(math.e)
GELU_C = math.sqrt(2 / math.pi)
GELU_K = 0.044715
VMEM = 63 * 2**20
DOWN_SHARES = (0.75,)
UP_SHARES = (0.5,)
OUT_SHARES = (0.5,)
QKV_SHARES = (0.5, 0.25)


def dot(a, b, ca, cb):
    return lax.dot_general(a, b, (((ca,), (cb,)), ((), ())), preferred_element_type=F32)


def nn(a, b):
    return dot(a, b, 1, 0)


def nt(a, b):
    return dot(a, b, 1, 1)


def tn(a, b):
    return dot(a, b, 0, 0)


def whole(shape):
    zeros = (0,) * len(shape)
    return pl.BlockSpec(shape, lambda i: zeros, pipeline_mode=pl.Buffered(1))


def params():
    return pltpu.CompilerParams(vmem_limit_bytes=VMEM)


def norm_rows(v):
    centred = v - jnp.mean(v, axis=-1, keepdims=True)
    inverse = lax.rsqrt(jnp.mean(centred * centred, axis=-1, keepdims=True) + 1e-05)
    return centred * inverse, inverse


def norm_back(g, normed, inverse):
    first = jnp.mean(g, axis=-1, keepdims=True)
    second = jnp.mean(g * normed, axis=-1, keepdims=True)
    return inverse * (g - first - normed * second)


def entry_kernel(ways, steps, *refs):
    bins, live, tokens, gain_attn, gain_mlp, w, x_out, ready_out, packed_out, w_out, own_rows = refs[:11]
    here, w_here, w_turned, ready_here, packed_here, send, recv, local, leave = refs[11:]
    place = Place(ways, 0)
    own_bin = bins[place.me]
    gain = gain_attn[pl.ds(own_bin, 1)]
    own_rows[0:1] = gain
    own_rows[1:2] = gain_mlp[pl.ds(own_bin, 1)]
    own_rows[2:3] = jnp.where(place.me < live[0], jnp.ones_like(gain), jnp.zeros_like(gain))
    own_rows[3:8] = jnp.zeros((5, gain.shape[1]), F32)
    rows, width = here.shape[1:]
    cols = w_here.shape[1]
    load_w = pltpu.make_async_copy(w, w_here, local.at[0])
    load_own = pltpu.make_async_copy(tokens.at[place.me], here.at[0], local.at[1])
    load_w.start()
    load_own.start()

    def move(k):
        return pltpu.make_async_remote_copy(
            src_ref=tokens.at[place.partner(k)], dst_ref=here.at[k],
            send_sem=send.at[k], recv_sem=recv.at[k],
            device_id=place.plane(k), device_id_type=MESH,
        )

    def span(k):
        return pl.ds(k * rows, rows)

    def leaving(k):
        return [
            pltpu.make_async_copy(here.at[k], x_out.at[span(k)], leave.at[0, k]),
            pltpu.make_async_copy(ready_here.at[k], ready_out.at[:, span(k)], leave.at[1, k]),
            pltpu.make_async_copy(packed_here.at[k], packed_out.at[:, span(k)], leave.at[2, k]),
        ]

    def project(k):
        ready = (norm_rows(here[k].astype(F32))[0] * gain).astype(BF16)
        ready_here[k] = ready.T
        for c in range(0, cols, steps):
            packed_here[k, c : c + steps] = nt(w_turned[c : c + steps], ready).astype(BF16)
        for copy in leaving(k):
            copy.start()

    place.greet_plane()
    for k in range(1, ways - 1):
        move(k).start()
    load_w.wait()

    def turn(c, carry):
        at = pl.ds(pl.multiple_of(c * 256, 256), 256)
        w_turned[at] = w_here[:, at].T
        return carry

    lax.fori_loop(0, cols // 256, turn, 0)
    save_w = pltpu.make_async_copy(w_turned, w_out, local.at[2])
    save_w.start()
    load_own.wait()
    project(0)
    for k in range(1, ways - 1):
        move(k).wait_send()
    move(ways - 1).start()
    for k in range(1, ways):
        move(k).wait_recv()
        project(k)
    move(ways - 1).wait_send()
    save_w.wait()
    for k in range(ways):
        for copy in leaving(k):
            copy.wait()


def entry(bins, live, tokens, gain_attn, gain_mlp, w):
    ways, rows, width = tokens.shape
    cols = w.shape[1]
    length = ways * rows
    remote = pl.BlockSpec(memory_space=pl.ANY)
    return pl.pallas_call(
        functools.partial(entry_kernel, ways, math.gcd(cols, 1024)),
        in_specs=[pl.BlockSpec(memory_space=pltpu.SMEM)] * 2
        + [remote]
        + [pl.BlockSpec(memory_space=pltpu.VMEM)] * 2
        + [remote],
        out_specs=[remote] * 4 + [pl.BlockSpec(memory_space=pltpu.VMEM)],
        out_shape=[
            jax.ShapeDtypeStruct((length, width), BF16),
            jax.ShapeDtypeStruct((width, length), BF16),
            jax.ShapeDtypeStruct((cols, length), BF16),
            jax.ShapeDtypeStruct((cols, width), BF16),
            jax.ShapeDtypeStruct((8, width), F32),
        ],
        scratch_shapes=[
            pltpu.VMEM((ways, rows, width), BF16),
            pltpu.VMEM((width, cols), BF16),
            pltpu.VMEM((cols, width), BF16),
            pltpu.VMEM((ways, width, rows), BF16),
            pltpu.VMEM((ways, cols, rows), BF16),
            pltpu.SemaphoreType.DMA((ways,)),
            pltpu.SemaphoreType.DMA((ways,)),
            pltpu.SemaphoreType.DMA((3,)),
            pltpu.SemaphoreType.DMA((3, ways)),
        ],
        compiler_params=pltpu.CompilerParams(vmem_limit_bytes=VMEM, collective_id=0, has_side_effects=True),
        name="entry",
    )(bins, live, tokens, gain_attn, gain_mlp, w)


def split2(v):
    hi = v.astype(BF16)
    return hi, (v - hi.astype(F32)).astype(BF16)


def split3(v):
    a = v.astype(BF16).astype(F32)
    b = (v - a).astype(BF16).astype(F32)
    return a, b, v - a - b


def in_rows(rows, cols):
    at = lax.broadcasted_iota(jnp.int32, (16, cols), 0)
    out = jnp.zeros((16, cols), F32)
    for i, row in enumerate(rows):
        out = jnp.where(at == i, row, out)
    return out.astype(BF16)


def ones_rows(many, cols):
    return (lax.broadcasted_iota(jnp.int32, (16, cols), 0) < many).astype(F32).astype(BF16)


def head_parts(p, h):
    base = 3 * HEAD * h
    return [p[base + HEAD * j : base + HEAD * (j + 1)] for j in range(3)]


def attend_kernel(p_ref, o_ref, aux_ref, *, bq):
    length = p_ref.shape[1]

    def run(exact):
        work, low, high = [], [], []
        for h in range(2):
            q, k, v = head_parts(p_ref, h)
            scaled = q.astype(F32) * (LOG2E * HEAD**-0.5)
            qhi, qlo = split2(scaled)
            if exact:
                shift = None
                qq = jnp.concatenate([qhi, qlo], axis=0)
                kk = jnp.concatenate([k, k], axis=0).T
            else:
                k32 = k.astype(F32)
                longest = jnp.sqrt(jnp.max(jnp.sum(k32 * k32, axis=0, keepdims=True)))
                bound = jnp.sqrt(jnp.sum(scaled * scaled, axis=0, keepdims=True)) * longest
                shift = bound.astype(BF16).astype(F32)
                qq = jnp.concatenate([qhi, qlo, in_rows([-shift], length)], axis=0)
                kk = jnp.concatenate([k, k, ones_rows(1, length)], axis=0).T
            vv = jnp.concatenate([v, ones_rows(1, length)], axis=0)
            for i in range(length // bq):
                span = slice(i * bq, (i + 1) * bq)
                work.append((h, span, kk, qq[:, span], vv, None if exact else shift[:, span]))
        following = nn(work[0][2], work[0][3])
        for n, (h, span, _, _, vv, m) in enumerate(work):
            s = following
            if n + 1 < len(work):
                following = nn(work[n + 1][2], work[n + 1][3])
            if exact:
                m = jnp.max(s, axis=0, keepdims=True)
                s = s - m
            o = nn(vv, jnp.exp2(s).astype(BF16))
            total = o[HEAD : HEAD + 1]
            o_ref[HEAD * h : HEAD * (h + 1), span] = (o[:HEAD] * (1.0 / total)).astype(BF16)
            aux_ref[h : h + 1, span] = -(m + jnp.log2(total))
            low.append(jnp.min(total))
            high.append(jnp.max(total))
        return functools.reduce(jnp.minimum, low), functools.reduce(jnp.maximum, high)

    low, high = run(False)
    fine = (low > 2.0**-80) & (high < 2.0**80)

    @pl.when(jnp.logical_not(fine))
    def _():
        run(True)


def attend(packed):
    cols, length = packed.shape
    pairs = cols // (6 * HEAD)
    return pl.pallas_call(
        functools.partial(attend_kernel, bq=math.gcd(length, 256)),
        grid=(pairs,),
        in_specs=[pl.BlockSpec((6 * HEAD, length), lambda i: (i, 0))],
        out_specs=[
            pl.BlockSpec((2 * HEAD, length), lambda i: (i, 0)),
            pl.BlockSpec((None, 8, length), lambda i: (i, 0, 0)),
        ],
        out_shape=[
            jax.ShapeDtypeStruct((pairs * 2 * HEAD, length), BF16),
            jax.ShapeDtypeStruct((pairs, 8, length), F32),
        ],
        compiler_params=params(),
        name="attend",
    )(packed)


def attend_back_head(p_ref, o_ref, aux_ref, do_ref, bq, h):
    length = p_ref.shape[1]
    q, k, v = head_parts(p_ref, h)
    do = do_ref[HEAD * h : HEAD * (h + 1)]
    o = o_ref[HEAD * h : HEAD * (h + 1)]
    qhi, qlo = split2(q.astype(F32) * (LOG2E * HEAD**-0.5))
    qq = jnp.concatenate([qhi, qlo, in_rows(split3(aux_ref[h : h + 1]), length)], axis=0).T
    kk = jnp.concatenate([k, k, ones_rows(3, length)], axis=0)
    minus = -jnp.sum(do.astype(F32) * o.astype(F32), axis=0, keepdims=True)
    dd = jnp.concatenate([do, in_rows(split3(minus), length)], axis=0).T
    vv = jnp.concatenate([v, ones_rows(3, length)], axis=0)
    dv = jnp.zeros((HEAD, length), F32)
    dk = jnp.zeros((HEAD, length), F32)
    dq = []
    spans = [slice(i * bq, (i + 1) * bq) for i in range(length // bq)]
    following = nn(qq[spans[0]], kk), nn(dd[spans[0]], vv)
    for i, span in enumerate(spans):
        s, g = following
        if i + 1 < len(spans):
            following = nn(qq[spans[i + 1]], kk), nn(dd[spans[i + 1]], vv)
        p = jnp.exp2(s)
        ds = (p * g).astype(BF16)
        dv = dv + nn(do[:, span], p.astype(BF16))
        dk = dk + nn(q[:, span], ds)
        dq.append((nt(k, ds) * HEAD**-0.5).astype(BF16))
    return [jnp.concatenate(dq, axis=1), (dk * HEAD**-0.5).astype(BF16), dv.astype(BF16)]


MESH = pl.DeviceIdType.MESH


class Place:
    def __init__(self, ways, line):
        self.ways, self.line = ways, line
        self.me = lax.axis_index("seq")
        self.b = lax.axis_index("batch")
        self.core = lax.rem(self.b, 2)
        self.z = self.b // 2

    def other_core(self):
        return {"batch": self.b + 1 - 2 * self.core}

    def along(self, step):
        return {"batch": self.b + 2 * step}

    def plane(self, k):
        return {"seq": self.partner(k)}

    def partner(self, k):
        out = self.me
        for bit in range(k.bit_length()):
            if k >> bit & 1:
                out = out + (1 << bit) * (1 - 2 * lax.rem(self.me // (1 << bit), 2))
        return out

    def greet_core(self):
        barrier = pltpu.get_barrier_semaphore()
        pl.semaphore_signal(barrier, inc=1, device_id=self.other_core(), device_id_type=MESH)
        pl.semaphore_wait(barrier, 1)

    def greet_plane(self):
        barrier = pltpu.get_barrier_semaphore()
        for k in range(1, self.ways):
            pl.semaphore_signal(barrier, inc=1, device_id=self.plane(k), device_id_type=MESH)
        pl.semaphore_wait(barrier, self.ways - 1)

    def hail(self):
        barrier = pltpu.get_barrier_semaphore()

        def tell(where):
            pl.semaphore_signal(barrier, inc=1, device_id=where, device_id_type=MESH)

        tell(self.other_core())
        for k in range(1, self.ways):
            tell(self.plane(k))

        @pl.when(self.z > 0)
        def _():
            tell(self.along(-1))

        @pl.when(self.z < self.line - 1)
        def _():
            tell(self.along(1))

    def greet(self):
        ends = (self.z == 0).astype(jnp.int32) + (self.z == self.line - 1).astype(jnp.int32)
        pl.semaphore_wait(pltpu.get_barrier_semaphore(), self.ways + 2 - ends)


def add_rows(dst, srcs, rows, cols):
    step = row_step(rows, cols)

    def one(i, carry):
        at = pl.multiple_of(i * step, step)
        total = dst(at, step)[...]
        for src in srcs:
            total = total + src(at, step)[...]
        dst(at, step)[...] = total
        return carry

    lax.fori_loop(0, rows // step, one, 0)


def row_step(rows, cols):
    for step in (64, 48, 32):
        if rows % step == 0 and step * cols <= 32768:
            return step
    return 16


class Way:
    def __init__(self, place, order, part):
        bits = lax.rem(place.me, 2), place.me // 2
        self.a, self.b = (bits[0], bits[1]) if order == 0 else (bits[1], bits[0])
        self.first, self.second = (1, 2) if order == 0 else (2, 1)
        self.part = part

    def half(self, a):
        return pl.ds(pl.multiple_of(a * 2 * self.part, 2 * self.part), 2 * self.part)

    def quarter(self, a, b):
        return pl.ds(pl.multiple_of((2 * a + b) * self.part, self.part), self.part)


class Reduce:
    def __init__(self, ways, line, rows, cols, split, first, paired, does):
        self.ways, self.line, self.rows, self.cols, self.split = ways, line, rows, cols, split
        self.front, self.back = does != "back", does != "front"
        self.here = pl.ds(first, cols)
        self.part = cols // 4
        self.paired = paired

    def buffers(self):
        line, rows, cols, split, part = self.line, self.rows, self.cols, self.split, self.part
        hops, rest = line - 1, rows - split
        shapes = {}
        if self.front:
            shapes["own"] = (line, rows, cols)
            if not self.paired:
                shapes["near"] = (line, rows, cols)
            if rest:
                shapes["z_right"] = shapes["z_left"] = (hops, rest, cols)
            if split:
                shapes["x_half"] = (line, split, 2 * part)
        if self.back:
            if rest:
                shapes["z_half"] = (rest, 2 * part)
                shapes["z_part"] = (rest, part)
                if not self.front:
                    shapes["z_row"] = (rest, cols)
            if split:
                shapes["x_right"] = shapes["x_left"] = (hops, split, part)
            shapes["final"] = (rows, cols)
        if split:
            shapes["x_part"] = (line, split, part)
        return shapes

    def scratch(self):
        n = 2 + 2 * 2 * (self.line - 1) + 2 * 8
        return [pltpu.VMEM(shape, BF16) for shape in self.buffers().values()] + [
            pltpu.SemaphoreType.DMA((n,)),
            pltpu.SemaphoreType.DMA((n,)),
        ]

    def bind(self, place, source, final, refs):
        refs = list(refs)
        self.place, self.source, self.result = place, source, final
        for name in self.buffers():
            setattr(self, name, refs.pop(0))
        self.send, self.recv = refs
        self.orders = [Way(place, order, self.part) for order in (0, 1)]
        self.ids = {}
        return self

    def copy(self, key, src, dst, where):
        n = self.ids.setdefault(key, len(self.ids) + 1)
        return pltpu.make_async_remote_copy(
            src_ref=src, dst_ref=dst, send_sem=self.send.at[n], recv_sem=self.recv.at[n],
            device_id=where, device_id_type=MESH,
        )

    def core_copy(self):
        p = self.place
        return self.copy("core", self.source.at[:, 1 - p.core, :, self.here], self.near, p.other_core())

    def own_copy(self):
        p = self.place
        if self.paired:
            return pltpu.make_async_copy(self.source.at[:, :, self.here], self.own, self.send.at[0])
        return pltpu.make_async_copy(self.source.at[:, p.core, :, self.here], self.own, self.send.at[0])

    def done_copy(self):
        return pltpu.make_async_copy(self.final, self.result.at[:, self.here], self.send.at[0])

    def kind_rows(self, kind):
        return (0, self.split) if kind == "x" else (self.split, self.rows - self.split)

    def mine(self, kind, start, many, columns):
        if kind == "x":
            return self.own.at[:, pl.ds(start, many), columns]
        if not self.front:
            return self.z_row.at[pl.ds(start - self.split, many), columns]
        return self.own.at[self.place.z, pl.ds(start, many), columns]

    def landing(self, buffer, kind, start, many):
        return buffer.at[:, pl.ds(start, many)] if kind == "x" else buffer.at[pl.ds(start, many)]

    def scatter(self, kind, stage, order):
        way = self.orders[order]
        first, many = self.kind_rows(kind)
        many = many // 2
        at = order * many
        if stage == 1:
            columns, where, buffer = way.half(1 - way.a), way.first, self.x_half if kind == "x" else self.z_half
        else:
            columns, where, buffer = way.quarter(way.a, 1 - way.b), way.second, self.x_part if kind == "x" else self.z_part
        return self.copy(
            (kind, "scatter", stage, order),
            self.mine(kind, first + at, many, columns),
            self.landing(buffer, kind, at, many),
            self.place.plane(where),
        )

    def gather(self, kind, stage, order, arriving=False):
        way = self.orders[order]
        first, many = self.kind_rows(kind)
        many = many // 2
        rows = pl.ds(first + order * many, many)
        if stage == 1:
            columns, where = way.quarter(way.a, 1 - way.b if arriving else way.b), way.second
        else:
            columns, where = way.half(1 - way.a if arriving else way.a), way.first
        view = self.final.at[rows, columns]
        return self.copy((kind, "gather", stage, order), view, view, self.place.plane(where))

    def scatter_start(self, kind, stage):
        for order in (0, 1):
            self.scatter(kind, stage, order).start()

    def scatter_add(self, kind, stage):
        first, many = self.kind_rows(kind)
        many = many // 2
        for order in (0, 1):
            self.scatter(kind, stage, order).wait_recv()
        for order in (0, 1):
            way = self.orders[order]
            at = order * many
            columns = way.half(way.a) if stage == 1 else way.quarter(way.a, way.b)
            if kind == "x":
                buffer = self.x_half if stage == 1 else self.x_part

                def each(j, carry, buffer=buffer, columns=columns, at=at):
                    here = lambda r, n: self.own.at[j, pl.ds(first + at + r, n), columns]
                    came = lambda r, n: buffer.at[j, pl.ds(at + r, n)]
                    add_rows(*((here, [came]) if stage == 1 else (came, [here])), many, buffer.shape[-1])
                    return carry

                lax.fori_loop(0, self.line, each, 0)
            else:
                buffer = self.z_half if stage == 1 else self.z_part
                here = lambda r, n, at=at, columns=columns: self.mine("z", first + at + r, n, columns)
                came = lambda r, n, at=at, buffer=buffer: buffer.at[pl.ds(at + r, n)]
                add_rows(*((here, [came]) if stage == 1 else (came, [here])), many, buffer.shape[-1])

    def gather_start(self, kind, stage):
        if stage == 1:
            first, many = self.kind_rows(kind)
            many = many // 2
            for order in (0, 1):
                way = self.orders[order]
                rows = pl.ds(order * many, many)
                done = self.x_part[self.place.z, rows] if kind == "x" else self.z_part[rows]
                self.final[pl.ds(first + order * many, many), way.quarter(way.a, way.b)] = done
        for order in (0, 1):
            if stage == 2:
                self.gather(kind, 1, order, True).wait_recv()
            self.gather(kind, stage, order).start()

    def line_row(self, kind, j):
        if kind == "x":
            return self.x_part.at[j]
        return self.own.at[j, pl.ds(self.split, self.rows - self.split)]

    def line_in(self, kind, right):
        if kind == "x":
            return self.x_right if right else self.x_left
        return self.z_right if right else self.z_left

    def line_copy(self, kind, right, t, j):
        return self.copy(
            (kind, right, t),
            self.line_row(kind, j),
            self.line_in(kind, right).at[t - 1],
            self.place.along(1 if right else -1),
        )

    def line_step(self, kind, t):
        p, line = self.place, self.line
        for right in (True, False):
            at = p.z if right else line - 1 - p.z
            if t < line:
                j = line + p.z - t if right else p.z + t - line

                @pl.when(at <= t - 1)
                def _(right=right, at=at, j=j):
                    if t > 1:

                        @pl.when(at >= 1)
                        def _():
                            self.line_arrive(kind, right, t - 1, j)

                    self.line_copy(kind, right, t, j).start()

            else:

                @pl.when(at >= 1)
                def _(right=right):
                    self.line_arrive(kind, right, t - 1, p.z)

    def line_arrive(self, kind, right, t, j):
        buffer = self.line_in(kind, right)
        self.copy(
            (kind, right, t),
            self.line_row(kind, j),
            buffer.at[t - 1],
            self.place.along(-1 if right else 1),
        ).wait_recv()
        if kind == "x":
            mine = lambda r, n: self.x_part.at[j, pl.ds(r, n)]
        else:
            mine = lambda r, n: self.own.at[j, pl.ds(self.split + r, n)]
        add_rows(mine, [lambda r, n: buffer.at[t - 1, pl.ds(r, n)]], self.kind_rows(kind)[1], buffer.shape[-1])

    def line_sent(self, kind):
        p, line = self.place, self.line
        for t in range(1, line):
            for right in (True, False):
                at = p.z if right else line - 1 - p.z

                @pl.when(at <= t - 1)
                def _(right=right, t=t):
                    self.line_copy(kind, right, t, p.z).wait_send()

    def saved(self):
        shapes = []
        if self.rows - self.split:
            shapes.append((self.rows - self.split, self.cols))
        if self.split:
            shapes.append((self.line, self.split, self.part))
        return shapes

    def save(self, refs):
        refs = list(refs)
        if self.rows - self.split:
            refs.pop(0)[...] = self.own[self.place.z, pl.ds(self.split, self.rows - self.split)]
        if self.split:
            refs.pop(0)[...] = self.x_part[...]

    def resume(self, refs):
        refs = list(refs)
        if self.rows - self.split:
            self.z_row[...] = refs.pop(0)[...]
        if self.split:
            self.x_part[...] = refs.pop(0)[...]

    def phase(self, n):
        x, z = bool(self.split), bool(self.rows - self.split)
        if n == 0:
            self.own_copy().start()
            if not self.paired:
                self.core_copy().start()
        if n == 1:
            self.own_copy().wait()
            if not self.paired:
                self.core_copy().wait_recv()

                def one(j, carry):
                    add_rows(
                        lambda r, n: self.own.at[j, pl.ds(r, n)],
                        [lambda r, n: self.near.at[j, pl.ds(r, n)]],
                        self.rows,
                        self.cols,
                    )
                    return carry

                lax.fori_loop(0, self.line, one, 0)
            if x:
                self.scatter_start("x", 1)
        if z and 1 <= n <= 4:
            self.line_step("z", n)
        if x and n == 3:
            self.scatter_add("x", 1)
            self.scatter_start("x", 2)
        if n == 4:
            if x:
                self.scatter_add("x", 2)
                for order in (0, 1):
                    for stage in (1, 2):
                        self.scatter("x", stage, order).wait_send()
            if z:
                self.line_sent("z")
            if not self.paired:
                self.core_copy().wait_send()
        if z and n == 5:
            self.scatter_start("z", 1)
        if x and 5 <= n <= 8:
            self.line_step("x", n - 4)
        if z and n == 6:
            self.scatter_add("z", 1)
            self.scatter_start("z", 2)
        if z and n == 7:
            self.scatter_add("z", 2)
            self.gather_start("z", 1)
        if n == 8:
            if x:
                self.gather_start("x", 1)
            if z:
                self.gather_start("z", 2)
        if x and n == 9:
            self.gather_start("x", 2)
        if n == 10:
            for kind, there in (("x", x), ("z", z)):
                if there:
                    for order in (0, 1):
                        self.gather(kind, 2, order, True).wait_recv()
                        for stage in (1, 2):
                            self.gather(kind, stage, order).wait_send()
                            if kind == "z":
                                self.scatter(kind, stage, order).wait_send()
            if x:
                self.line_sent("x")
            self.done_copy().start()
        if n == 11:
            self.done_copy().wait()


class Sums:
    def __init__(self, ways, line, rows, cols, shares, plan, paired=False, does="all"):
        width = cols // len(shares)
        self.shape, self.plan, self.does = (rows, cols), plan, does
        self.parts = [
            Reduce(ways, line, rows, width, int(rows * share) // 32 * 32, i * width, paired, does)
            for i, share in enumerate(shares)
        ]

    def out(self):
        if self.does == "front":
            return [(whole(v), jax.ShapeDtypeStruct(v, BF16)) for part in self.parts for v in part.saved()]
        return [(pl.BlockSpec(memory_space=pl.ANY), jax.ShapeDtypeStruct(self.shape, BF16))]

    def ins(self):
        if self.does == "back":
            return [whole(v) for part in self.parts for v in part.saved()]
        return [pl.BlockSpec(memory_space=pl.ANY)]

    def scratch(self):
        return [s for part in self.parts for s in part.scratch()]

    def bind(self, place, sources, finals, refs):
        refs = list(refs)
        self.sources, self.finals = sources, finals
        for part in self.parts:
            many = len(part.scratch())
            part.bind(place, sources[0], finals[0], refs[:many])
            refs = refs[many:]

    def phase(self, n):
        if n == 5 and self.does == "back":
            refs = list(self.sources)
            for part in self.parts:
                many = len(part.saved())
                part.resume(refs[:many])
                refs = refs[many:]
        for part in self.parts:
            part.phase(n)
        if n == 4 and self.does == "front":
            refs = list(self.finals)
            for part in self.parts:
                many = len(part.saved())
                part.save(refs[:many])
                refs = refs[many:]


class Swap:
    def __init__(self, ways, rows, cols, plan):
        self.ways, self.shape, self.plan = ways, (ways, rows, cols), plan

    def scratch(self):
        return [pltpu.SemaphoreType.DMA((self.ways,)), pltpu.SemaphoreType.DMA((self.ways,))]

    def out(self):
        return [(pl.BlockSpec(memory_space=pl.ANY), jax.ShapeDtypeStruct(self.shape, BF16))]

    def ins(self):
        return [pl.BlockSpec(memory_space=pl.ANY)]

    def bind(self, place, sources, finals, refs):
        self.place, self.source, self.final = place, sources[0], finals[0]
        self.send, self.recv = refs

    def copy(self, k, slot):
        return pltpu.make_async_remote_copy(
            src_ref=self.source.at[k], dst_ref=self.final.at[slot],
            send_sem=self.send.at[k], recv_sem=self.recv.at[k],
            device_id=self.place.plane(k), device_id_type=MESH,
        )

    def stay(self):
        return pltpu.make_async_copy(self.source.at[0], self.final.at[self.place.me], self.send.at[0])

    def phase(self, n):
        p = self.place
        if n == 0:
            self.stay().start()
            for k in range(1, self.ways - 1):
                self.copy(k, p.me).start()
        if n == 1:
            self.copy(self.ways - 1, p.me).start()
        if n == 2:
            self.stay().wait()
            for k in range(1, self.ways):
                self.copy(k, p.partner(k)).wait_recv()
                self.copy(k, p.me).wait_send()


class PairSum:
    def __init__(self, line, rows, cols, steps, piece, cut):
        self.shape, self.steps, self.piece, self.cut = (line, rows, cols), steps, piece, cut

    def out(self):
        return pl.BlockSpec(memory_space=pl.ANY), jax.ShapeDtypeStruct(self.shape, BF16)

    def scratch(self):
        line, rows, cols = self.piece
        sems = [pltpu.SemaphoreType.DMA((self.steps,))] * 3
        return [pltpu.VMEM((3, line, 2, rows, cols), BF16), pltpu.VMEM(self.shape, BF16)] + sems

    def bind(self, place, final, refs):
        self.place, self.final = place, final
        self.stage, self.near, self.send, self.recv, self.leave = refs

    def copy(self, i):
        p = self.place
        return pltpu.make_async_remote_copy(
            src_ref=self.stage.at[lax.rem(i, 3), :, 1 - p.core], dst_ref=self.near.at[self.cut(i)],
            send_sem=self.send.at[i], recv_sem=self.recv.at[i],
            device_id=p.other_core(), device_id_type=MESH,
        )

    def leaving(self, i):
        at = self.cut(i)
        return pltpu.make_async_copy(self.near.at[at], self.final.at[at], self.leave.at[i])

    def push(self, i, value):
        line, rows, cols = self.piece
        self.stage[lax.rem(i, 3)] = value.reshape(line, 2, rows, cols)
        self.copy(i).start()

    def take_late(self, i):
        pl.when(i >= 2)(lambda: self.take(i - 2))

    def take_rest(self, i):
        self.take(i - 1)
        self.take(i)
        for n in range(self.steps):
            self.leaving(n).wait()

    def take(self, i):
        line, rows, cols = self.piece
        self.copy(i).wait_recv()
        self.copy(i).wait_send()
        at = self.cut(i)
        for j in range(line):
            here = (pl.ds(at[0].start + j, 1),) + at[1:]
            self.near[here] = (self.stage[lax.rem(i, 3), j, self.place.core] + self.near[here][0])[None]
        self.leaving(i).start()


class Side:
    def __init__(self, ways, line, jobs):
        self.ways, self.line, self.jobs = ways, line, jobs

    def in_specs(self):
        return [spec for job in self.jobs for spec in job.ins()]

    def out_specs(self):
        return [spec for job in self.jobs for spec, _ in job.out()]

    def out_shape(self):
        return [shape for job in self.jobs for _, shape in job.out()]

    def scratch(self):
        return [s for job in self.jobs for s in job.scratch()]

    def bind(self, sources, finals, refs):
        refs, finals = list(refs), list(finals)
        self.place = Place(self.ways, self.line)
        for job, source in zip(self.jobs, sources):
            many, outs = len(job.scratch()), len(job.out())
            job.bind(self.place, source, finals[:outs], refs[:many])
            refs, finals = refs[many:], finals[outs:]

    def at(self, i, point):
        for job in self.jobs:
            for n in range(12):
                if n in job.plan and job.plan[n][1] == point:
                    if isinstance(i, int):
                        job.phase(n)
                    else:
                        pl.when(i == job.plan[n][0])(functools.partial(job.phase, n))


def remote_params(ident):
    return pltpu.CompilerParams(vmem_limit_bytes=VMEM, collective_id=ident, has_side_effects=True)


def mlp_kernel(pieces, *refs):
    x, mixed, w_out, own_rows = refs[:4]
    cots = refs[4 : 4 + pieces]
    w_up, hidden, ready, gout, act, slope, grad_down = refs[4 + pieces :]
    rows = cots[0].shape[0]

    @pl.when(pl.program_id(0) == 0)
    def _():
        for k in range(pieces):
            span = slice(k * rows, (k + 1) * rows)
            gout[span] = cots[k][...] * own_rows[2:3].astype(BF16)
            h = x[span].astype(F32) + tn(mixed[:, span], w_out[...])
            hidden[span] = h
            ready[span] = (norm_rows(h)[0] * own_rows[1:2]).astype(BF16)

    u = nn(ready[...], w_up[...])
    u2 = u * u
    t = jnp.tanh(u * (GELU_C + (GELU_C * GELU_K) * u2))
    half = 0.5 + 0.5 * t
    a = (u * half).astype(BF16)
    act[...] = a
    slope[...] = (half + u * (1 - t * t) * (0.5 * GELU_C + (1.5 * GELU_C * GELU_K) * u2)).astype(BF16)
    grad_down[...] = tn(a, gout[...]).astype(BF16)


def mlp(x, mixed, w_out, own_rows, cots, w_up):
    length, width = x.shape
    inner = w_up.shape[1]
    rows = length // len(cots)
    block = min(1024, inner)
    cols = pl.BlockSpec((length, block), lambda i: (0, i))
    return pl.pallas_call(
        functools.partial(mlp_kernel, len(cots)),
        grid=(inner // block,),
        in_specs=[
            whole((length, width)),
            whole((length, width)),
            whole((width, width)),
            whole((8, width)),
        ]
        + [whole((rows, width))] * len(cots)
        + [pl.BlockSpec((width, block), lambda i: (0, i))],
        out_specs=[whole((length, width))] * 3 + [cols, cols, pl.BlockSpec((block, width), lambda i: (i, 0))],
        out_shape=[
            jax.ShapeDtypeStruct((length, width), F32),
            jax.ShapeDtypeStruct((length, width), BF16),
            jax.ShapeDtypeStruct((length, width), BF16),
            jax.ShapeDtypeStruct((length, inner), BF16),
            jax.ShapeDtypeStruct((length, inner), BF16),
            jax.ShapeDtypeStruct((inner, width), BF16),
        ],
        compiler_params=params(),
        name="mlp",
    )(x, mixed, w_out, own_rows, *cots, w_up)


def mlp_back_kernel(side, *refs):
    gout, act, slope, w_down, ready, hidden, source = refs[:7]
    many = len(side.out_shape())
    out, grad_upward, grad_up = refs[7:10]
    out_sum = refs[10 + many]
    side.bind([[source]], refs[10 : 10 + many], refs[11 + many :])
    i = pl.program_id(0)
    last = pl.num_programs(0) - 1

    @pl.when(i == 0)
    def _():
        side.place.hail()
        out_sum[...] = hidden[...]
        side.place.greet()

    side.at(i, 0)
    gu = (nt(gout[...], w_down[...]) * slope[...].astype(F32)).astype(BF16)
    grad_upward[...] = gu
    grad_up[...] = tn(ready[...], gu).astype(BF16)
    side.at(i, 1)
    out_sum[...] += nn(act[...], w_down[...])

    @pl.when(i == last)
    def _():
        out[...] = out_sum[...].astype(BF16)
        side.at(i, "end")


def mlp_back(gout, act, slope, w_down, ready, hidden, grad_down, ways):
    length, width = gout.shape
    inner = w_down.shape[0]
    line, _, down_rows, _ = grad_down.shape
    block = inner // 8
    cols = pl.BlockSpec((length, block), lambda i: (0, i))
    square = whole((length, width))
    plan = {0: (0, 0), 1: (2, 0), 2: (3, 1), 3: (6, 0), 4: (7, "end")}
    side = Side(ways, line, [Sums(ways, line, down_rows, width, DOWN_SHARES, plan, False, "front")])
    return pl.pallas_call(
        functools.partial(mlp_back_kernel, side),
        grid=(8,),
        in_specs=[
            square,
            cols,
            cols,
            pl.BlockSpec((block, width), lambda i: (i, 0)),
            square,
            square,
        ]
        + side.in_specs(),
        out_specs=[square, cols, pl.BlockSpec((width, block), lambda i: (0, i))] + side.out_specs(),
        out_shape=[
            jax.ShapeDtypeStruct((length, width), BF16),
            jax.ShapeDtypeStruct((length, inner), BF16),
            jax.ShapeDtypeStruct((width, inner), BF16),
        ]
        + side.out_shape(),
        scratch_shapes=[pltpu.VMEM((length, width), F32)] + side.scratch(),
        compiler_params=remote_params(2),
        name="mlp_back",
    )(gout, act, slope, w_down, ready, hidden, grad_down)


def attn_back_kernel(side, pair_sum, bq, *refs):
    bins, *refs = refs
    gu, w_up, hidden, gout, own_rows, mixed, w_out, packed, aux, w_qkv, ready, x = refs[:12]
    back_from = len(side.jobs[0].ins())
    carried, source_up, source_out = refs[12 : 12 + back_from], refs[12 + back_from], refs[13 + back_from]
    refs = refs[14 + back_from :]
    grad_qkv, grad_x, tables = refs[:3]
    many = len(side.out_shape())
    finals, refs = refs[3 : 3 + many], refs[3 + many :]
    back_sum, grad_hidden, grad_mixed, spare, grad_out, row_mlp, late = refs[:7]
    pairing = len(pair_sum.scratch())
    side.bind([carried, [source_up], [grad_out], [source_out]], finals, refs[7 + pairing :])
    pair_sum.bind(side.place, grad_qkv, refs[7 : 7 + pairing])
    i = pl.program_id(0)
    steps = pl.num_programs(0) // 2
    length, width = gout.shape
    line = grad_out.shape[0]
    span = math.gcd(length, 256)
    load_hidden = pltpu.make_async_copy(hidden, grad_hidden, late.at[0])
    load_w = pltpu.make_async_copy(w_out, spare, late.at[1])
    load_gout = pltpu.make_async_copy(gout, grad_x, late.at[2])
    load_x = pltpu.make_async_copy(x, spare, late.at[3])

    @pl.when(i == 0)
    def _():
        side.place.hail()
        load_hidden.start()
        load_w.start()
        load_gout.start()
        back_sum[...] = jnp.zeros_like(back_sum)

    pl.when(i == 1)(side.place.greet)
    side.at(i, 0)

    @pl.when(i < steps)
    def _():
        back_sum[...] += nt(gu[...], w_up[...])

    @pl.when(i == steps - 1)
    def _():
        load_hidden.wait()
        load_w.wait()
        load_gout.wait()
        total = jnp.zeros((1, width), F32)
        for r in range(length // span):
            here = slice(r * span, (r + 1) * span)
            normed, inverse = norm_rows(grad_hidden[here])
            g = back_sum[here]
            total = total + jnp.sum(g * normed, axis=0, keepdims=True)
            grad_hidden[here] = grad_x[here].astype(F32) + norm_back(g * own_rows[1:2], normed, inverse)
        row_mlp[...] = total
        side.at(i, "norm")
        low = grad_hidden[...].astype(BF16)
        grad_mixed[...] = nt(spare[...], low).astype(BF16)
        load_x.start()
        grad_out[...] = nn(mixed[...], low).astype(BF16).reshape(grad_out.shape)
        back_sum[...] = jnp.zeros_like(back_sum)
        side.at(i, "out")

    @pl.when(i >= steps)
    def _():
        pair = i - steps
        pair_sum.take_late(pair)
        rows = pl.ds(pl.multiple_of(pair * 2 * HEAD, 2 * HEAD), 2 * HEAD)
        parts = attend_back_head(packed, mixed[rows], aux, grad_mixed[rows], bq, 0)
        side.at(i, "mid")
        parts = parts + attend_back_head(packed, mixed[rows], aux, grad_mixed[rows], bq, 1)
        side.at(i, 1)
        gp = jnp.concatenate(parts, axis=0)
        pair_sum.push(pair, nt(ready[...], gp).astype(BF16))
        back_sum[...] += tn(gp, w_qkv[...])
        side.at(i, 2)

    @pl.when(i == pl.num_programs(0) - 1)
    def _():
        load_x.wait()
        total = jnp.zeros((1, width), F32)
        for r in range(length // span):
            here = slice(r * span, (r + 1) * span)
            normed, inverse = norm_rows(spare[here].astype(F32))
            g = back_sum[here]
            total = total + jnp.sum(g * normed, axis=0, keepdims=True)
            grad_x[here] = (grad_hidden[here] + norm_back(g * own_rows[0:1], normed, inverse)).astype(BF16)
        bins_here = tables.shape[2] // 4
        marked = lax.broadcasted_iota(jnp.int32, (2 * line * bins_here, width), 0) == bins[side.place.me]
        both = [jnp.where(marked, row, 0.0) for row in (total, row_mlp[...])]
        half = width // 2
        for b in range(2 * line):
            own = slice(b * bins_here, (b + 1) * bins_here)
            parts = [v[own, cut] for cut in (slice(0, half), slice(half, width)) for v in both]
            tables[b // 2, b % 2] = jnp.concatenate(parts, axis=0).astype(BF16)
        pair_sum.take_rest(i - steps)
        side.at(i, "end")


def attn_back(bins, gu, w_up, hidden, gout, own_rows, mixed, w_out, packed, aux, w_qkv, ready, x, carried, grad_up, out, ways):
    length, width = gout.shape
    inner = w_up.shape[1]
    cols = packed.shape[0]
    pairs = cols // (6 * HEAD)
    line, _, rows, _ = grad_up.shape
    block = inner // pairs
    square = whole((length, width))
    remote = pl.BlockSpec(memory_space=pl.ANY)
    first = lambda i: jnp.minimum(i, pairs - 1)
    second = lambda i: jnp.maximum(i - pairs, 0)
    plan_down = {5: (1, 0), 6: (5, 0), 7: (7, 0), 8: (7, "norm"), 9: (8, "mid"), 10: (9, 0), 11: (15, "end")}
    plan_up = {
        0: (1, 0), 1: (7, 0), 2: (8, 1), 3: (10, "mid"), 4: (12, 1), 5: (12, 1),
        6: (13, 0), 7: (13, 1), 8: (14, 0), 9: (14, "mid"), 10: (15, 0), 11: (15, "end"),
    }
    plan_out = {
        0: (7, "out"), 1: (8, "mid"), 2: (9, "mid"), 3: (11, 0), 4: (12, 2), 5: (12, 2),
        6: (13, "mid"), 7: (13, 2), 8: (14, "mid"), 9: (14, 1), 10: (15, "mid"), 11: (15, "end"),
    }
    plan_swap = {0: (8, "mid"), 1: (10, 1), 2: (15, 1)}
    side = Side(
        ways,
        line,
        [
            Sums(ways, line, inner // (2 * line), width, DOWN_SHARES, plan_down, False, "back"),
            Sums(ways, line, rows, inner, UP_SHARES, plan_up),
            Sums(ways, line, rows, width, OUT_SHARES, plan_out),
            Swap(ways, length // ways, width, plan_swap),
        ],
    )
    wide = 6 * HEAD
    pair_sum = PairSum(
        line, rows, cols, pairs, (line, rows, wide),
        lambda i: (pl.ds(0, line), slice(None), pl.ds(pl.multiple_of(i * wide, wide), wide)),
    )
    inner_jobs = side.jobs[0].ins() + [remote, remote]
    return pl.pallas_call(
        functools.partial(attn_back_kernel, side, pair_sum, math.gcd(length, 256)),
        grid=(2 * pairs,),
        in_specs=[
            pl.BlockSpec(memory_space=pltpu.SMEM),
            pl.BlockSpec((length, block), lambda i: (0, first(i))),
            pl.BlockSpec((width, block), lambda i: (0, first(i))),
            remote,
            remote,
            whole((8, width)),
            whole((width, length)),
            remote,
            pl.BlockSpec((wide, length), lambda i: (second(i), 0)),
            pl.BlockSpec((None, 8, length), lambda i: (second(i), 0, 0)),
            pl.BlockSpec((wide, width), lambda i: (second(i), 0)),
            whole((width, length)),
            remote,
        ]
        + inner_jobs,
        out_specs=[pair_sum.out()[0], square, whole((line, 2, 32, width // 2))] + side.out_specs(),
        out_shape=[
            pair_sum.out()[1],
            jax.ShapeDtypeStruct((length, width), BF16),
            jax.ShapeDtypeStruct((line, 2, 32, width // 2), BF16),
        ]
        + side.out_shape(),
        scratch_shapes=[
            pltpu.VMEM((length, width), F32),
            pltpu.VMEM((length, width), F32),
            pltpu.VMEM((width, length), BF16),
            pltpu.VMEM((length, width), BF16),
            pltpu.VMEM((line, 2, rows, width), BF16),
            pltpu.VMEM((1, width), F32),
            pltpu.SemaphoreType.DMA((4,)),
        ]
        + pair_sum.scratch()
        + side.scratch(),
        compiler_params=remote_params(3),
        name="attn_back",
    )(bins, gu, w_up, hidden, gout, own_rows, mixed, w_out, packed, aux, w_qkv, ready, x, *carried, grad_up, out)


def tail_kernel(side, *refs):
    jobs = len(side.jobs)
    side.bind([[ref] for ref in refs[:jobs]], refs[jobs : 2 * jobs], refs[2 * jobs :])
    side.place.hail()
    side.place.greet()
    for n in range(12):
        side.at(0, n)
        side.at(0, ("after", n))


def tail(ways, line, sums, pieces):
    plan = {n: (0, n) for n in range(12)}
    behind = {n: (0, ("after", n)) for n in range(12)}
    jobs = [
        Sums(ways, line, v.shape[-2], v.shape[-1], shares, plan if paired else behind, paired)
        for v, shares, paired in sums
    ]
    side = Side(ways, line, jobs + [Swap(ways, pieces.shape[1], pieces.shape[2], {0: (0, ("after", 1)), 1: (0, ("after", 3)), 2: (0, 11)})])
    arrays = [v for v, _, _ in sums] + [pieces]
    return pl.pallas_call(
        functools.partial(tail_kernel, side),
        in_specs=[pl.BlockSpec(memory_space=pl.ANY)] * len(arrays),
        out_specs=side.out_specs(),
        out_shape=side.out_shape(),
        scratch_shapes=side.scratch(),
        compiler_params=remote_params(4),
        name="tail",
    )(*arrays)


def finish_kernel(many, *refs):
    tables, refs = refs[0], refs[1:]
    sources, refs = refs[:many], refs[many:]
    table_attn, table_mlp = refs[:2]
    targets, refs = refs[2 : 2 + many], refs[2 + many :]
    low, wide, (came, left) = refs[:many], refs[many : 2 * many], refs[2 * many :]
    parts = 4

    def span(n, part):
        rows = low[n].shape[0] // parts
        return pl.ds(part * rows, rows)

    def load(n, part):
        at = span(n, part)
        return pltpu.make_async_copy(sources[n].at[at], low[n].at[at], came.at[n, part])

    def store(n, part):
        at = span(n, part)
        return pltpu.make_async_copy((wide[n] if changed(n) else low[n]).at[at], targets[n].at[at], left.at[n, part])

    def changed(n):
        return targets[n].dtype != low[n].dtype

    pieces = [(n, part) for n in range(many) for part in range(parts)]
    for piece in pieces:
        load(*piece).start()
    half = tables.shape[1]
    for first, table in ((0, table_attn), (8, table_mlp)):
        table[:, :half] = tables[first : first + 8].astype(F32)
        table[:, half:] = tables[first + 16 : first + 24].astype(F32)
    for n, part in pieces:
        load(n, part).wait()
        if not changed(n):
            store(n, part).start()
            continue
        rows, cols = low[n].shape[0] // parts, low[n].shape[1]
        step = row_step(rows, cols)

        def one(r, carry, n=n, part=part, rows=rows, step=step):
            at = pl.ds(pl.multiple_of(part * rows + r * step, step), step)
            wide[n][at] = low[n][at].astype(F32)
            return carry

        lax.fori_loop(0, rows // step, one, 0)
        store(n, part).start()
    for piece in pieces:
        store(*piece).wait()


def finish(tables, arrays, kinds):
    many = len(arrays)
    remote = pl.BlockSpec(memory_space=pl.ANY)
    here = pl.BlockSpec(memory_space=pltpu.VMEM)
    table = jax.ShapeDtypeStruct((8, 2 * tables.shape[1]), F32)
    return pl.pallas_call(
        functools.partial(finish_kernel, many),
        in_specs=[here] + [remote] * many,
        out_specs=[here, here] + [remote] * many,
        out_shape=[table, table] + [jax.ShapeDtypeStruct(v.shape, kind) for v, kind in zip(arrays, kinds)],
        scratch_shapes=[pltpu.VMEM(v.shape, BF16) for v in arrays]
        + [pltpu.VMEM(v.shape, F32) for v in arrays]
        + [pltpu.SemaphoreType.DMA((many, 4))] * 2,
        compiler_params=params(),
        name="finish",
    )(tables, *arrays)


def exchange(pieces, me, ways):
    return [pieces[0]] + [
        lax.ppermute(pieces[k], "seq", [(s, s ^ k) for s in range(ways)]) for k in range(1, ways)
    ]


def by_partner(slots, me, ways):
    return [lax.dynamic_index_in_dim(slots, me ^ k, 0, keepdims=False) for k in range(ways)]


def body(tokens, cotangent, bins, live_count, w_qkv, w_out, w_up, w_down, gain_attn, gain_mlp):
    slots, rows, width = tokens.shape
    ways = lax.axis_size("seq")
    batch_ways = lax.axis_size("batch")
    line = batch_ways // 2
    me = lax.axis_index("seq")
    x, ready_attn, packed, w_turned, own_rows = entry(bins, live_count, tokens, gain_attn, gain_mlp, w_qkv)
    packed, later = lax.optimization_barrier((packed, cotangent))
    cots = exchange(by_partner(later, me, ways), me, ways)
    mixed, aux = attend(packed)
    hidden, ready_mlp, gout, act, slope, grad_down = mlp(x, mixed, w_out, own_rows, cots, w_up)

    def blocks(v):
        return v.reshape(line, 2, v.shape[0] // batch_ways, v.shape[1])

    out, grad_upward, grad_up, *carried = mlp_back(
        gout, act, slope, w_down, ready_mlp, hidden, blocks(grad_down), ways
    )
    qkv_pair, grad_x, tables, sum_down, sum_up, sum_out, output = attn_back(
        bins, grad_upward, w_up, hidden, gout, own_rows, mixed, w_out, packed, aux, w_turned, ready_attn, x,
        carried, blocks(grad_up), out.reshape(ways, rows, width), ways,
    )
    sum_qkv, sum_tables, grad_tokens = tail(
        ways,
        line,
        [(qkv_pair, QKV_SHARES, True), (tables, (0,), False)],
        grad_x.reshape(ways, rows, width),
    )
    arrays = [v.reshape(slots * rows, width) for v in (grad_tokens, output)] + [sum_qkv, sum_out, sum_up, sum_down]
    sum_attn, sum_mlp, grad_tokens, output, *sums = finish(sum_tables, arrays, [F32, BF16] + [F32] * 4)
    return (output.reshape(tokens.shape), grad_tokens.reshape(tokens.shape), *sums, sum_attn, sum_mlp)


def plain_norm(values_in):
    centred = values_in - jnp.mean(values_in, axis=-1, keepdims=True)
    inverse = lax.rsqrt(jnp.mean(centred * centred, axis=-1, keepdims=True) + 1e-05)
    return (centred * inverse, inverse)


def plain_norm_back(grad_normed, normed, inverse):
    first_mean = jnp.mean(grad_normed, axis=-1, keepdims=True)
    second_mean = jnp.mean(grad_normed * normed, axis=-1, keepdims=True)
    return inverse * (grad_normed - first_mean - normed * second_mean)


def plain_weight_grad(left, right):
    return lax.dot_general(
        left, right, (((0,), (0,)), ((), ())), preferred_element_type=jnp.float32
    )


def plain_heads(packed, heads_here):
    shaped = packed.reshape(packed.shape[0], heads_here, 3, -1)
    return (shaped[:, :, 0], shaped[:, :, 1], shaped[:, :, 2])


def plain_attend(packed, heads_here, block_rows):
    queries, key_rows, values = plain_heads(packed, heads_here)
    length, head_size = (queries.shape[0], queries.shape[2])
    factor = head_size ** (-0.5)
    blocked = queries.reshape(length // block_rows, block_rows, heads_here, head_size)

    def per_block(query_block):
        scores = (
            jnp.einsum("qhd,khd->hqk", query_block, key_rows, preferred_element_type=jnp.float32)
            * factor
        )
        row_max = jnp.max(scores, axis=-1, keepdims=True)
        logsum = row_max + jnp.log(jnp.sum(jnp.exp(scores - row_max), axis=-1, keepdims=True))
        softmax_rows = jnp.exp(scores - logsum).astype(jnp.bfloat16)
        mixed_rows = jnp.einsum(
            "hqk,khd->qhd", softmax_rows, values, preferred_element_type=jnp.float32
        )
        return (
            mixed_rows.astype(jnp.bfloat16).reshape(block_rows, heads_here * head_size),
            logsum[..., 0],
        )

    mixed_rows, logsum = lax.map(per_block, blocked)
    return (mixed_rows.reshape(length, heads_here * head_size), logsum)


def plain_attend_back(packed, logsum, grad_mixed, heads_here, block_rows):
    queries, key_rows, values = plain_heads(packed, heads_here)
    length, head_size = (queries.shape[0], queries.shape[2])
    factor = head_size ** (-0.5)
    count_blocks = length // block_rows
    query_blocks = queries.reshape(count_blocks, block_rows, heads_here, head_size)
    grad_blocks = grad_mixed.reshape(count_blocks, block_rows, heads_here, head_size)

    def per_block(running, pieces):
        query_block, grad_block, logsum_block = pieces
        scores = (
            jnp.einsum("qhd,khd->hqk", query_block, key_rows, preferred_element_type=jnp.float32)
            * factor
        )
        softmax_rows = jnp.exp(scores - logsum_block[..., None])
        grad_values = running[1] + jnp.einsum(
            "hqk,qhd->khd",
            softmax_rows.astype(jnp.bfloat16),
            grad_block,
            preferred_element_type=jnp.float32,
        )
        grad_soft = jnp.einsum(
            "qhd,khd->hqk", grad_block, values, preferred_element_type=jnp.float32
        )
        inner = jnp.sum(softmax_rows * grad_soft, axis=-1, keepdims=True)
        grad_scores = (softmax_rows * (grad_soft - inner)).astype(jnp.bfloat16)
        grad_query = (
            jnp.einsum("hqk,khd->qhd", grad_scores, key_rows, preferred_element_type=jnp.float32)
            * factor
        )
        grad_keys = (
            running[0]
            + jnp.einsum(
                "hqk,qhd->khd", grad_scores, query_block, preferred_element_type=jnp.float32
            )
            * factor
        )
        return ((grad_keys, grad_values), grad_query)

    zeros_start = jnp.zeros((length, heads_here, head_size), jnp.float32)
    (grad_keys, grad_values), grad_queries = lax.scan(
        per_block, (zeros_start, zeros_start), (query_blocks, grad_blocks, logsum)
    )
    grad_queries = grad_queries.reshape(length, heads_here, head_size)
    stacked = jnp.stack([grad_queries, grad_keys, grad_values], axis=2)
    return stacked.reshape(length, heads_here * 3 * head_size).astype(jnp.bfloat16)


def plain_body(tokens, cotangent, bins, live_count, w_qkv, w_out, w_up, w_down, gain_attn, gain_mlp):
    slot_count, local_rows, model_width = tokens.shape
    seq_ways = lax.axis_size("seq")
    heads_here = HEADS // seq_ways
    length = local_rows * seq_ways
    block_rows = math.gcd(length, 512)
    row_count = slot_count * local_rows
    table_rows = gain_attn.shape[0]
    onehot = (bins[:, None] == jnp.arange(table_rows, dtype=jnp.int32)[None, :]).astype(jnp.float32)
    gains_attn = jnp.dot(onehot, gain_attn, precision=lax.Precision.HIGHEST)[:, None, :]
    gains_mlp = jnp.dot(onehot, gain_mlp, precision=lax.Precision.HIGHEST)[:, None, :]
    inputs = tokens.astype(jnp.float32)

    def attention_part():
        normed_attn, inverse_attn = plain_norm(inputs)
        ready_attn = (normed_attn * gains_attn).astype(jnp.bfloat16).reshape(row_count, model_width)
        packed = jnp.dot(ready_attn, w_qkv, preferred_element_type=jnp.float32).astype(jnp.bfloat16)
        packed = packed.reshape(slot_count, local_rows, 3 * model_width)
        item_rows = lax.all_to_all(packed, "seq", split_axis=2, concat_axis=1, tiled=True)
        mixed_items, logsum_items = lax.map(
            lambda single: plain_attend(single, heads_here, block_rows), item_rows
        )
        mixed_rows = lax.all_to_all(
            mixed_items, "seq", split_axis=1, concat_axis=2, tiled=True
        ).reshape(row_count, model_width)
        return (normed_attn, inverse_attn, ready_attn, item_rows, logsum_items, mixed_rows)

    def mlp_part(hidden):
        normed_mlp, inverse_mlp = plain_norm(hidden)
        ready_mlp = (normed_mlp * gains_mlp).astype(jnp.bfloat16).reshape(row_count, model_width)
        upward = jnp.dot(ready_mlp, w_up, preferred_element_type=jnp.float32)
        active = jax.nn.gelu(upward).astype(jnp.bfloat16)
        return (normed_mlp, inverse_mlp, ready_mlp, upward, active)

    saved_attn = attention_part()
    attended = jnp.dot(saved_attn[5], w_out, preferred_element_type=jnp.float32)
    hidden = inputs + attended.reshape(slot_count, local_rows, model_width)
    saved_mlp = mlp_part(hidden)
    branch = jnp.dot(saved_mlp[4], w_down, preferred_element_type=jnp.float32)
    output = (hidden + branch.reshape(slot_count, local_rows, model_width)).astype(jnp.bfloat16)
    saved_attn = attention_part()
    saved_mlp = mlp_part(hidden)
    normed_attn, inverse_attn, ready_attn, packed_heads, logsum, mixed_rows = saved_attn
    normed_mlp, inverse_mlp, ready_mlp, upward, active = saved_mlp
    alive_mask = (jnp.arange(slot_count, dtype=jnp.int32) < live_count[0]).astype(jnp.float32)
    grad_output = cotangent.astype(jnp.float32) * alive_mask[:, None, None]
    low_output = grad_output.astype(jnp.bfloat16).reshape(row_count, model_width)
    grad_down = plain_weight_grad(active, low_output)
    grad_active = jnp.dot(low_output, w_down.T, preferred_element_type=jnp.float32)
    gelu_values, gelu_pull = jax.vjp(jax.nn.gelu, upward)
    grad_upward = gelu_pull(grad_active)[0].astype(jnp.bfloat16)
    grad_up = plain_weight_grad(ready_mlp, grad_upward)
    grad_ready_mlp = jnp.dot(grad_upward, w_up.T, preferred_element_type=jnp.float32).reshape(
        slot_count, local_rows, model_width
    )
    table_mlp = jnp.dot(
        onehot.T, jnp.sum(grad_ready_mlp * normed_mlp, axis=1), precision=lax.Precision.HIGHEST
    )
    grad_hidden = grad_output + plain_norm_back(grad_ready_mlp * gains_mlp, normed_mlp, inverse_mlp)
    low_hidden = grad_hidden.astype(jnp.bfloat16).reshape(row_count, model_width)
    grad_out = plain_weight_grad(mixed_rows, low_hidden)
    grad_mixed = jnp.dot(low_hidden, w_out.T, preferred_element_type=jnp.float32).astype(
        jnp.bfloat16
    )
    grad_mixed = grad_mixed.reshape(slot_count, local_rows, model_width)
    grad_mixed_heads = lax.all_to_all(grad_mixed, "seq", split_axis=2, concat_axis=1, tiled=True)
    grad_packed_heads = lax.map(
        lambda pieces: plain_attend_back(pieces[0], pieces[1], pieces[2], heads_here, block_rows),
        (packed_heads, logsum, grad_mixed_heads),
    )
    grad_packed = lax.all_to_all(
        grad_packed_heads, "seq", split_axis=1, concat_axis=2, tiled=True
    ).reshape(row_count, 3 * model_width)
    grad_qkv = plain_weight_grad(ready_attn, grad_packed)
    grad_ready_attn = jnp.dot(grad_packed, w_qkv.T, preferred_element_type=jnp.float32).reshape(
        slot_count, local_rows, model_width
    )
    table_attn = jnp.dot(
        onehot.T, jnp.sum(grad_ready_attn * normed_attn, axis=1), precision=lax.Precision.HIGHEST
    )
    grad_tokens = grad_hidden + plain_norm_back(grad_ready_attn * gains_attn, normed_attn, inverse_attn)
    gradients = (grad_qkv, grad_out, grad_up, grad_down, table_attn, table_mlp)
    shares = (
        lax.psum_scatter(gradients[0], "batch", scatter_dimension=0, tiled=True),
        lax.psum_scatter(gradients[1], "batch", scatter_dimension=0, tiled=True),
        lax.psum_scatter(gradients[2], "batch", scatter_dimension=0, tiled=True),
        lax.psum_scatter(gradients[3], "batch", scatter_dimension=0, tiled=True),
        lax.psum_scatter(gradients[4], "batch", scatter_dimension=0, tiled=True),
        lax.psum_scatter(gradients[5], "batch", scatter_dimension=0, tiled=True),
    )
    summed = (
        lax.psum(shares[0].astype(jnp.bfloat16), "seq").astype(jnp.float32),
        lax.psum(shares[1].astype(jnp.bfloat16), "seq").astype(jnp.float32),
        lax.psum(shares[2].astype(jnp.bfloat16), "seq").astype(jnp.float32),
        lax.psum(shares[3].astype(jnp.bfloat16), "seq").astype(jnp.float32),
        lax.psum(shares[4].astype(jnp.bfloat16), "seq").astype(jnp.float32),
        lax.psum(shares[5].astype(jnp.bfloat16), "seq").astype(jnp.float32),
    )
    return (output, grad_tokens, summed[0], summed[1], summed[2], summed[3], summed[4], summed[5])


def solution(mesh):
    placed = (
        P("batch", "seq", None),
        P("batch", "seq", None),
        P("batch"),
        P("batch"),
        P(),
        P(),
        P(),
        P(),
        P(),
        P(),
    )
    fits = mesh.shape["seq"] == 4 and mesh.shape["batch"] == 8
    return jax.shard_map(
        body if fits else plain_body,
        mesh=mesh,
        in_specs=placed,
        out_specs=(
            P("batch", "seq", None),
            P("batch", "seq", None),
            P("batch", None),
            P("batch", None),
            P("batch", None),
            P("batch", None),
            P("batch", None),
            P("batch", None),
        ),
        check_vma=False,
    )
```

```python
import functools
import math

import jax
import jax.numpy as jnp
from jax import lax
from jax.experimental import pallas as pl
from jax.experimental.pallas import tpu as pltpu
from jax.sharding import PartitionSpec as P

F32 = jnp.float32
BF16 = jnp.bfloat16
HEAD = 64
HEADS = 16
LOG2E = math.log2(math.e)
GELU_C = math.sqrt(2 / math.pi)
GELU_K = 0.044715
VMEM = 63 * 2**20
DOWN_SHARES = (0.75,)
UP_SHARES = (0.5,)
OUT_SHARES = (0.5,)
QKV_SHARES = (0.5, 0.25)


def dot(a, b, ca, cb):
    return lax.dot_general(a, b, (((ca,), (cb,)), ((), ())), preferred_element_type=F32)


def nn(a, b):
    return dot(a, b, 1, 0)


def nt(a, b):
    return dot(a, b, 1, 1)


def tn(a, b):
    return dot(a, b, 0, 0)


def whole(shape):
    zeros = (0,) * len(shape)
    return pl.BlockSpec(shape, lambda i: zeros, pipeline_mode=pl.Buffered(1))


def params():
    return pltpu.CompilerParams(vmem_limit_bytes=VMEM)


def norm_rows(v):
    centred = v - jnp.mean(v, axis=-1, keepdims=True)
    inverse = lax.rsqrt(jnp.mean(centred * centred, axis=-1, keepdims=True) + 1e-05)
    return centred * inverse, inverse


def norm_back(g, normed, inverse):
    first = jnp.mean(g, axis=-1, keepdims=True)
    second = jnp.mean(g * normed, axis=-1, keepdims=True)
    return inverse * (g - first - normed * second)


def entry_kernel(ways, steps, *refs):
    bins, live, tokens, cotangent, gain_attn, gain_mlp, w = refs[:7]
    x_out, ready_out, packed_out, w_out, own_rows = refs[7:12]
    cots, refs = refs[12 : 12 + ways], refs[12 + ways :]
    here, w_here, w_turned, ready_here, packed_here, cots_here, send, recv, local, leave = refs
    place = Place(ways, 0)
    own_bin = bins[place.me]
    gain = gain_attn[pl.ds(own_bin, 1)]
    own_rows[0:1] = gain
    own_rows[1:2] = gain_mlp[pl.ds(own_bin, 1)]
    own_rows[2:3] = jnp.where(place.me < live[0], jnp.ones_like(gain), jnp.zeros_like(gain))
    own_rows[3:8] = jnp.zeros((5, gain.shape[1]), F32)
    rows, width = here.shape[1:]
    cols = w_here.shape[1]
    load_w = pltpu.make_async_copy(w, w_here, local.at[0])
    load_own = pltpu.make_async_copy(tokens.at[place.me], here.at[0], local.at[1])
    load_cots = pltpu.make_async_copy(cotangent, cots_here, local.at[3])
    load_w.start()
    load_own.start()
    load_cots.start()

    def move(k):
        return pltpu.make_async_remote_copy(
            src_ref=tokens.at[place.partner(k)], dst_ref=here.at[k],
            send_sem=send.at[k], recv_sem=recv.at[k],
            device_id=place.plane(k), device_id_type=MESH,
        )

    def sort_cots(k):
        return pltpu.make_async_copy(cots_here.at[place.partner(k)], cots[k], leave.at[3, k])

    def span(k):
        return pl.ds(k * rows, rows)

    def leaving(k):
        return [
            pltpu.make_async_copy(here.at[k], x_out.at[span(k)], leave.at[0, k]),
            pltpu.make_async_copy(ready_here.at[k], ready_out.at[:, span(k)], leave.at[1, k]),
            pltpu.make_async_copy(packed_here.at[k], packed_out.at[:, span(k)], leave.at[2, k]),
        ]

    def project(k):
        ready = (norm_rows(here[k].astype(F32))[0] * gain).astype(BF16)
        ready_here[k] = ready.T
        for c in range(0, cols, steps):
            packed_here[k, c : c + steps] = nt(w_turned[c : c + steps], ready).astype(BF16)
        for copy in leaving(k):
            copy.start()

    place.greet_plane()
    for k in range(1, ways - 1):
        move(k).start()
    load_w.wait()

    def turn(c, carry):
        at = pl.ds(pl.multiple_of(c * 256, 256), 256)
        w_turned[at] = w_here[:, at].T
        return carry

    lax.fori_loop(0, cols // 256, turn, 0)
    save_w = pltpu.make_async_copy(w_turned, w_out, local.at[2])
    save_w.start()
    load_own.wait()
    load_cots.wait()
    for k in range(ways):
        sort_cots(k).start()
    project(0)
    for k in range(1, ways - 1):
        move(k).wait_send()
    move(ways - 1).start()
    for k in range(1, ways):
        move(k).wait_recv()
        project(k)
    move(ways - 1).wait_send()
    save_w.wait()
    for k in range(ways):
        sort_cots(k).wait()
        for copy in leaving(k):
            copy.wait()


def entry(bins, live, tokens, cotangent, gain_attn, gain_mlp, w):
    ways, rows, width = tokens.shape
    cols = w.shape[1]
    length = ways * rows
    remote = pl.BlockSpec(memory_space=pl.ANY)
    return pl.pallas_call(
        functools.partial(entry_kernel, ways, math.gcd(cols, 1024)),
        in_specs=[pl.BlockSpec(memory_space=pltpu.SMEM)] * 2
        + [remote] * 2
        + [pl.BlockSpec(memory_space=pltpu.VMEM)] * 2
        + [remote],
        out_specs=[remote] * 4 + [pl.BlockSpec(memory_space=pltpu.VMEM)] + [remote] * ways,
        out_shape=[
            jax.ShapeDtypeStruct((length, width), BF16),
            jax.ShapeDtypeStruct((width, length), BF16),
            jax.ShapeDtypeStruct((cols, length), BF16),
            jax.ShapeDtypeStruct((cols, width), BF16),
            jax.ShapeDtypeStruct((8, width), F32),
        ]
        + [jax.ShapeDtypeStruct((rows, width), BF16)] * ways,
        scratch_shapes=[
            pltpu.VMEM((ways, rows, width), BF16),
            pltpu.VMEM((width, cols), BF16),
            pltpu.VMEM((cols, width), BF16),
            pltpu.VMEM((ways, width, rows), BF16),
            pltpu.VMEM((ways, cols, rows), BF16),
            pltpu.VMEM((ways, rows, width), BF16),
            pltpu.SemaphoreType.DMA((ways,)),
            pltpu.SemaphoreType.DMA((ways,)),
            pltpu.SemaphoreType.DMA((4,)),
            pltpu.SemaphoreType.DMA((4, ways)),
        ],
        compiler_params=pltpu.CompilerParams(vmem_limit_bytes=VMEM, collective_id=0, has_side_effects=True),
        name="entry",
    )(bins, live, tokens, cotangent, gain_attn, gain_mlp, w)


def split2(v):
    hi = v.astype(BF16)
    return hi, (v - hi.astype(F32)).astype(BF16)


def split3(v):
    a = v.astype(BF16).astype(F32)
    b = (v - a).astype(BF16).astype(F32)
    return a, b, v - a - b


def in_rows(rows, cols):
    at = lax.broadcasted_iota(jnp.int32, (16, cols), 0)
    out = jnp.zeros((16, cols), F32)
    for i, row in enumerate(rows):
        out = jnp.where(at == i, row, out)
    return out.astype(BF16)


def ones_rows(many, cols):
    return (lax.broadcasted_iota(jnp.int32, (16, cols), 0) < many).astype(F32).astype(BF16)


def head_parts(p, h):
    base = 3 * HEAD * h
    return [p[base + HEAD * j : base + HEAD * (j + 1)] for j in range(3)]


def attend_kernel(p_ref, o_ref, aux_ref, *, bq):
    length = p_ref.shape[1]

    def run(exact):
        work, low, high = [], [], []
        for h in range(2):
            q, k, v = head_parts(p_ref, h)
            scaled = q.astype(F32) * (LOG2E * HEAD**-0.5)
            qhi, qlo = split2(scaled)
            if exact:
                shift = None
                qq = jnp.concatenate([qhi, qlo], axis=0)
                kk = jnp.concatenate([k, k], axis=0).T
            else:
                k32 = k.astype(F32)
                longest = jnp.sqrt(jnp.max(jnp.sum(k32 * k32, axis=0, keepdims=True)))
                bound = jnp.sqrt(jnp.sum(scaled * scaled, axis=0, keepdims=True)) * longest
                shift = bound.astype(BF16).astype(F32)
                qq = jnp.concatenate([qhi, qlo, in_rows([-shift], length)], axis=0)
                kk = jnp.concatenate([k, k, ones_rows(1, length)], axis=0).T
            vv = jnp.concatenate([v, ones_rows(1, length)], axis=0)
            for i in range(length // bq):
                span = slice(i * bq, (i + 1) * bq)
                work.append((h, span, kk, qq[:, span], vv, None if exact else shift[:, span]))
        following = nn(work[0][2], work[0][3])
        for n, (h, span, _, _, vv, m) in enumerate(work):
            s = following
            if n + 1 < len(work):
                following = nn(work[n + 1][2], work[n + 1][3])
            if exact:
                m = jnp.max(s, axis=0, keepdims=True)
                s = s - m
            o = nn(vv, jnp.exp2(s).astype(BF16))
            total = o[HEAD : HEAD + 1]
            o_ref[HEAD * h : HEAD * (h + 1), span] = (o[:HEAD] * (1.0 / total)).astype(BF16)
            aux_ref[h : h + 1, span] = -(m + jnp.log2(total))
            low.append(jnp.min(total))
            high.append(jnp.max(total))
        return functools.reduce(jnp.minimum, low), functools.reduce(jnp.maximum, high)

    low, high = run(False)
    fine = (low > 2.0**-80) & (high < 2.0**80)

    @pl.when(jnp.logical_not(fine))
    def _():
        run(True)


def attend(packed):
    cols, length = packed.shape
    pairs = cols // (6 * HEAD)
    return pl.pallas_call(
        functools.partial(attend_kernel, bq=math.gcd(length, 256)),
        grid=(pairs,),
        in_specs=[pl.BlockSpec((6 * HEAD, length), lambda i: (i, 0))],
        out_specs=[
            pl.BlockSpec((2 * HEAD, length), lambda i: (i, 0)),
            pl.BlockSpec((None, 8, length), lambda i: (i, 0, 0)),
        ],
        out_shape=[
            jax.ShapeDtypeStruct((pairs * 2 * HEAD, length), BF16),
            jax.ShapeDtypeStruct((pairs, 8, length), F32),
        ],
        compiler_params=params(),
        name="attend",
    )(packed)


def attend_back_head(p_ref, o_ref, aux_ref, do_ref, bq, h):
    length = p_ref.shape[1]
    q, k, v = head_parts(p_ref, h)
    do = do_ref[HEAD * h : HEAD * (h + 1)]
    o = o_ref[HEAD * h : HEAD * (h + 1)]
    qhi, qlo = split2(q.astype(F32) * (LOG2E * HEAD**-0.5))
    qq = jnp.concatenate([qhi, qlo, in_rows(split3(aux_ref[h : h + 1]), length)], axis=0).T
    kk = jnp.concatenate([k, k, ones_rows(3, length)], axis=0)
    minus = -jnp.sum(do.astype(F32) * o.astype(F32), axis=0, keepdims=True)
    dd = jnp.concatenate([do, in_rows(split3(minus), length)], axis=0).T
    vv = jnp.concatenate([v, ones_rows(3, length)], axis=0)
    dv = jnp.zeros((HEAD, length), F32)
    dk = jnp.zeros((HEAD, length), F32)
    dq = []
    spans = [slice(i * bq, (i + 1) * bq) for i in range(length // bq)]
    following = nn(qq[spans[0]], kk), nn(dd[spans[0]], vv)
    for i, span in enumerate(spans):
        s, g = following
        if i + 1 < len(spans):
            following = nn(qq[spans[i + 1]], kk), nn(dd[spans[i + 1]], vv)
        p = jnp.exp2(s)
        ds = (p * g).astype(BF16)
        dv = dv + nn(do[:, span], p.astype(BF16))
        dk = dk + nn(q[:, span], ds)
        dq.append((nt(k, ds) * HEAD**-0.5).astype(BF16))
    return [jnp.concatenate(dq, axis=1), (dk * HEAD**-0.5).astype(BF16), dv.astype(BF16)]


MESH = pl.DeviceIdType.MESH


class Place:
    def __init__(self, ways, line):
        self.ways, self.line = ways, line
        self.me = lax.axis_index("seq")
        self.b = lax.axis_index("batch")
        self.core = lax.rem(self.b, 2)
        self.z = self.b // 2

    def other_core(self):
        return {"batch": self.b + 1 - 2 * self.core}

    def along(self, step):
        return {"batch": self.b + 2 * step}

    def plane(self, k):
        return {"seq": self.partner(k)}

    def partner(self, k):
        out = self.me
        for bit in range(k.bit_length()):
            if k >> bit & 1:
                out = out + (1 << bit) * (1 - 2 * lax.rem(self.me // (1 << bit), 2))
        return out

    def greet_core(self):
        barrier = pltpu.get_barrier_semaphore()
        pl.semaphore_signal(barrier, inc=1, device_id=self.other_core(), device_id_type=MESH)
        pl.semaphore_wait(barrier, 1)

    def greet_plane(self):
        barrier = pltpu.get_barrier_semaphore()
        for k in range(1, self.ways):
            pl.semaphore_signal(barrier, inc=1, device_id=self.plane(k), device_id_type=MESH)
        pl.semaphore_wait(barrier, self.ways - 1)

    def hail(self):
        barrier = pltpu.get_barrier_semaphore()

        def tell(where):
            pl.semaphore_signal(barrier, inc=1, device_id=where, device_id_type=MESH)

        tell(self.other_core())
        for k in range(1, self.ways):
            tell(self.plane(k))

        @pl.when(self.z > 0)
        def _():
            tell(self.along(-1))

        @pl.when(self.z < self.line - 1)
        def _():
            tell(self.along(1))

    def greet(self):
        ends = (self.z == 0).astype(jnp.int32) + (self.z == self.line - 1).astype(jnp.int32)
        pl.semaphore_wait(pltpu.get_barrier_semaphore(), self.ways + 2 - ends)


def add_rows(dst, srcs, rows, cols):
    step = row_step(rows, cols)

    def one(i, carry):
        at = pl.multiple_of(i * step, step)
        total = dst(at, step)[...]
        for src in srcs:
            total = total + src(at, step)[...]
        dst(at, step)[...] = total
        return carry

    lax.fori_loop(0, rows // step, one, 0)


def row_step(rows, cols):
    for step in (64, 48, 32):
        if rows % step == 0 and step * cols <= 32768:
            return step
    return 16


class Way:
    def __init__(self, place, order, part):
        bits = lax.rem(place.me, 2), place.me // 2
        self.a, self.b = (bits[0], bits[1]) if order == 0 else (bits[1], bits[0])
        self.first, self.second = (1, 2) if order == 0 else (2, 1)
        self.part = part

    def half(self, a):
        return pl.ds(pl.multiple_of(a * 2 * self.part, 2 * self.part), 2 * self.part)

    def quarter(self, a, b):
        return pl.ds(pl.multiple_of((2 * a + b) * self.part, self.part), self.part)


class Reduce:
    def __init__(self, ways, line, rows, cols, split, first, paired, does):
        self.ways, self.line, self.rows, self.cols, self.split = ways, line, rows, cols, split
        self.front, self.back = does != "back", does != "front"
        self.here = pl.ds(first, cols)
        self.part = cols // 4
        self.paired = paired

    def buffers(self):
        line, rows, cols, split, part = self.line, self.rows, self.cols, self.split, self.part
        hops, rest = line - 1, rows - split
        shapes = {}
        if self.front:
            shapes["own"] = (line, rows, cols)
            if not self.paired:
                shapes["near"] = (line, rows, cols)
            if rest:
                shapes["z_right"] = shapes["z_left"] = (hops, rest, cols)
            if split:
                shapes["x_half"] = (line, split, 2 * part)
        if self.back:
            if rest:
                shapes["z_half"] = (rest, 2 * part)
                shapes["z_part"] = (rest, part)
                if not self.front:
                    shapes["z_row"] = (rest, cols)
            if split:
                shapes["x_right"] = shapes["x_left"] = (hops, split, part)
            shapes["final"] = (rows, cols)
        if split:
            shapes["x_part"] = (line, split, part)
        return shapes

    def scratch(self):
        n = 2 + 2 * 2 * (self.line - 1) + 2 * 8
        return [pltpu.VMEM(shape, BF16) for shape in self.buffers().values()] + [
            pltpu.SemaphoreType.DMA((n,)),
            pltpu.SemaphoreType.DMA((n,)),
        ]

    def bind(self, place, source, final, refs):
        refs = list(refs)
        self.place, self.source, self.result = place, source, final
        for name in self.buffers():
            setattr(self, name, refs.pop(0))
        self.send, self.recv = refs
        self.orders = [Way(place, order, self.part) for order in (0, 1)]
        self.ids = {}
        return self

    def copy(self, key, src, dst, where):
        n = self.ids.setdefault(key, len(self.ids) + 1)
        return pltpu.make_async_remote_copy(
            src_ref=src, dst_ref=dst, send_sem=self.send.at[n], recv_sem=self.recv.at[n],
            device_id=where, device_id_type=MESH,
        )

    def core_copy(self):
        p = self.place
        return self.copy("core", self.source.at[:, 1 - p.core, :, self.here], self.near, p.other_core())

    def own_copy(self):
        p = self.place
        if self.paired:
            return pltpu.make_async_copy(self.source.at[:, :, self.here], self.own, self.send.at[0])
        return pltpu.make_async_copy(self.source.at[:, p.core, :, self.here], self.own, self.send.at[0])

    def done_copy(self):
        return pltpu.make_async_copy(self.final, self.result.at[:, self.here], self.send.at[0])

    def kind_rows(self, kind):
        return (0, self.split) if kind == "x" else (self.split, self.rows - self.split)

    def mine(self, kind, start, many, columns):
        if kind == "x":
            return self.own.at[:, pl.ds(start, many), columns]
        if not self.front:
            return self.z_row.at[pl.ds(start - self.split, many), columns]
        return self.own.at[self.place.z, pl.ds(start, many), columns]

    def landing(self, buffer, kind, start, many):
        return buffer.at[:, pl.ds(start, many)] if kind == "x" else buffer.at[pl.ds(start, many)]

    def scatter(self, kind, stage, order):
        way = self.orders[order]
        first, many = self.kind_rows(kind)
        many = many // 2
        at = order * many
        if stage == 1:
            columns, where, buffer = way.half(1 - way.a), way.first, self.x_half if kind == "x" else self.z_half
        else:
            columns, where, buffer = way.quarter(way.a, 1 - way.b), way.second, self.x_part if kind == "x" else self.z_part
        return self.copy(
            (kind, "scatter", stage, order),
            self.mine(kind, first + at, many, columns),
            self.landing(buffer, kind, at, many),
            self.place.plane(where),
        )

    def gather(self, kind, stage, order, arriving=False):
        way = self.orders[order]
        first, many = self.kind_rows(kind)
        many = many // 2
        rows = pl.ds(first + order * many, many)
        if stage == 1:
            columns, where = way.quarter(way.a, 1 - way.b if arriving else way.b), way.second
        else:
            columns, where = way.half(1 - way.a if arriving else way.a), way.first
        view = self.final.at[rows, columns]
        return self.copy((kind, "gather", stage, order), view, view, self.place.plane(where))

    def scatter_start(self, kind, stage):
        for order in (0, 1):
            self.scatter(kind, stage, order).start()

    def scatter_add(self, kind, stage):
        first, many = self.kind_rows(kind)
        many = many // 2
        for order in (0, 1):
            self.scatter(kind, stage, order).wait_recv()
        for order in (0, 1):
            way = self.orders[order]
            at = order * many
            columns = way.half(way.a) if stage == 1 else way.quarter(way.a, way.b)
            if kind == "x":
                buffer = self.x_half if stage == 1 else self.x_part

                def each(j, carry, buffer=buffer, columns=columns, at=at):
                    here = lambda r, n: self.own.at[j, pl.ds(first + at + r, n), columns]
                    came = lambda r, n: buffer.at[j, pl.ds(at + r, n)]
                    add_rows(*((here, [came]) if stage == 1 else (came, [here])), many, buffer.shape[-1])
                    return carry

                lax.fori_loop(0, self.line, each, 0)
            else:
                buffer = self.z_half if stage == 1 else self.z_part
                here = lambda r, n, at=at, columns=columns: self.mine("z", first + at + r, n, columns)
                came = lambda r, n, at=at, buffer=buffer: buffer.at[pl.ds(at + r, n)]
                add_rows(*((here, [came]) if stage == 1 else (came, [here])), many, buffer.shape[-1])

    def gather_start(self, kind, stage):
        if stage == 1:
            first, many = self.kind_rows(kind)
            many = many // 2
            for order in (0, 1):
                way = self.orders[order]
                rows = pl.ds(order * many, many)
                done = self.x_part[self.place.z, rows] if kind == "x" else self.z_part[rows]
                self.final[pl.ds(first + order * many, many), way.quarter(way.a, way.b)] = done
        for order in (0, 1):
            if stage == 2:
                self.gather(kind, 1, order, True).wait_recv()
            self.gather(kind, stage, order).start()

    def line_row(self, kind, j):
        if kind == "x":
            return self.x_part.at[j]
        return self.own.at[j, pl.ds(self.split, self.rows - self.split)]

    def line_in(self, kind, right):
        if kind == "x":
            return self.x_right if right else self.x_left
        return self.z_right if right else self.z_left

    def line_copy(self, kind, right, t, j):
        return self.copy(
            (kind, right, t),
            self.line_row(kind, j),
            self.line_in(kind, right).at[t - 1],
            self.place.along(1 if right else -1),
        )

    def line_step(self, kind, t):
        p, line = self.place, self.line
        for right in (True, False):
            at = p.z if right else line - 1 - p.z
            if t < line:
                j = line + p.z - t if right else p.z + t - line

                @pl.when(at <= t - 1)
                def _(right=right, at=at, j=j):
                    if t > 1:

                        @pl.when(at >= 1)
                        def _():
                            self.line_arrive(kind, right, t - 1, j)

                    self.line_copy(kind, right, t, j).start()

            else:

                @pl.when(at >= 1)
                def _(right=right):
                    self.line_arrive(kind, right, t - 1, p.z)

    def line_arrive(self, kind, right, t, j):
        buffer = self.line_in(kind, right)
        self.copy(
            (kind, right, t),
            self.line_row(kind, j),
            buffer.at[t - 1],
            self.place.along(-1 if right else 1),
        ).wait_recv()
        if kind == "x":
            mine = lambda r, n: self.x_part.at[j, pl.ds(r, n)]
        else:
            mine = lambda r, n: self.own.at[j, pl.ds(self.split + r, n)]
        add_rows(mine, [lambda r, n: buffer.at[t - 1, pl.ds(r, n)]], self.kind_rows(kind)[1], buffer.shape[-1])

    def line_sent(self, kind):
        p, line = self.place, self.line
        for t in range(1, line):
            for right in (True, False):
                at = p.z if right else line - 1 - p.z

                @pl.when(at <= t - 1)
                def _(right=right, t=t):
                    self.line_copy(kind, right, t, p.z).wait_send()

    def saved(self):
        shapes = []
        if self.rows - self.split:
            shapes.append((self.rows - self.split, self.cols))
        if self.split:
            shapes.append((self.line, self.split, self.part))
        return shapes

    def save(self, refs):
        refs = list(refs)
        if self.rows - self.split:
            refs.pop(0)[...] = self.own[self.place.z, pl.ds(self.split, self.rows - self.split)]
        if self.split:
            refs.pop(0)[...] = self.x_part[...]

    def resume(self, refs):
        refs = list(refs)
        if self.rows - self.split:
            self.z_row[...] = refs.pop(0)[...]
        if self.split:
            self.x_part[...] = refs.pop(0)[...]

    def phase(self, n):
        x, z = bool(self.split), bool(self.rows - self.split)
        if n == 0:
            self.own_copy().start()
            if not self.paired:
                self.core_copy().start()
        if n == 1:
            self.own_copy().wait()
            if not self.paired:
                self.core_copy().wait_recv()

                def one(j, carry):
                    add_rows(
                        lambda r, n: self.own.at[j, pl.ds(r, n)],
                        [lambda r, n: self.near.at[j, pl.ds(r, n)]],
                        self.rows,
                        self.cols,
                    )
                    return carry

                lax.fori_loop(0, self.line, one, 0)
            if x:
                self.scatter_start("x", 1)
        if z and 1 <= n <= 4:
            self.line_step("z", n)
        if x and n == 3:
            self.scatter_add("x", 1)
            self.scatter_start("x", 2)
        if n == 4:
            if x:
                self.scatter_add("x", 2)
                for order in (0, 1):
                    for stage in (1, 2):
                        self.scatter("x", stage, order).wait_send()
            if z:
                self.line_sent("z")
            if not self.paired:
                self.core_copy().wait_send()
        if z and n == 5:
            self.scatter_start("z", 1)
        if x and 5 <= n <= 8:
            self.line_step("x", n - 4)
        if z and n == 6:
            self.scatter_add("z", 1)
            self.scatter_start("z", 2)
        if z and n == 7:
            self.scatter_add("z", 2)
            self.gather_start("z", 1)
        if n == 8:
            if x:
                self.gather_start("x", 1)
            if z:
                self.gather_start("z", 2)
        if x and n == 9:
            self.gather_start("x", 2)
        if n == 10:
            for kind, there in (("x", x), ("z", z)):
                if there:
                    for order in (0, 1):
                        self.gather(kind, 2, order, True).wait_recv()
                        for stage in (1, 2):
                            self.gather(kind, stage, order).wait_send()
                            if kind == "z":
                                self.scatter(kind, stage, order).wait_send()
            if x:
                self.line_sent("x")
            self.done_copy().start()
        if n == 11:
            self.done_copy().wait()


class Sums:
    def __init__(self, ways, line, rows, cols, shares, plan, paired=False, does="all"):
        width = cols // len(shares)
        self.shape, self.plan, self.does = (rows, cols), plan, does
        self.parts = [
            Reduce(ways, line, rows, width, int(rows * share) // 32 * 32, i * width, paired, does)
            for i, share in enumerate(shares)
        ]

    def out(self):
        if self.does == "front":
            return [(whole(v), jax.ShapeDtypeStruct(v, BF16)) for part in self.parts for v in part.saved()]
        return [(pl.BlockSpec(memory_space=pl.ANY), jax.ShapeDtypeStruct(self.shape, BF16))]

    def ins(self):
        if self.does == "back":
            return [whole(v) for part in self.parts for v in part.saved()]
        return [pl.BlockSpec(memory_space=pl.ANY)]

    def scratch(self):
        return [s for part in self.parts for s in part.scratch()]

    def bind(self, place, sources, finals, refs):
        refs = list(refs)
        self.sources, self.finals = sources, finals
        for part in self.parts:
            many = len(part.scratch())
            part.bind(place, sources[0], finals[0], refs[:many])
            refs = refs[many:]

    def phase(self, n):
        if n == 5 and self.does == "back":
            refs = list(self.sources)
            for part in self.parts:
                many = len(part.saved())
                part.resume(refs[:many])
                refs = refs[many:]
        for part in self.parts:
            part.phase(n)
        if n == 4 and self.does == "front":
            refs = list(self.finals)
            for part in self.parts:
                many = len(part.saved())
                part.save(refs[:many])
                refs = refs[many:]


class Swap:
    def __init__(self, ways, rows, cols, plan):
        self.ways, self.shape, self.plan = ways, (ways, rows, cols), plan

    def scratch(self):
        return [pltpu.SemaphoreType.DMA((self.ways,)), pltpu.SemaphoreType.DMA((self.ways,))]

    def out(self):
        return [(pl.BlockSpec(memory_space=pl.ANY), jax.ShapeDtypeStruct(self.shape, BF16))]

    def ins(self):
        return [pl.BlockSpec(memory_space=pl.ANY)]

    def bind(self, place, sources, finals, refs):
        self.place, self.source, self.final = place, sources[0], finals[0]
        self.send, self.recv = refs

    def copy(self, k, slot):
        return pltpu.make_async_remote_copy(
            src_ref=self.source.at[k], dst_ref=self.final.at[slot],
            send_sem=self.send.at[k], recv_sem=self.recv.at[k],
            device_id=self.place.plane(k), device_id_type=MESH,
        )

    def stay(self):
        return pltpu.make_async_copy(self.source.at[0], self.final.at[self.place.me], self.send.at[0])

    def phase(self, n):
        p = self.place
        if n == 0:
            self.stay().start()
            for k in range(1, self.ways - 1):
                self.copy(k, p.me).start()
        if n == 1:
            self.copy(self.ways - 1, p.me).start()
        if n == 2:
            self.stay().wait()
            for k in range(1, self.ways):
                self.copy(k, p.partner(k)).wait_recv()
                self.copy(k, p.me).wait_send()


class PairSum:
    def __init__(self, line, rows, cols, steps, piece, cut):
        self.shape, self.steps, self.piece, self.cut = (line, rows, cols), steps, piece, cut

    def out(self):
        return pl.BlockSpec(memory_space=pl.ANY), jax.ShapeDtypeStruct(self.shape, BF16)

    def scratch(self):
        line, rows, cols = self.piece
        sems = [pltpu.SemaphoreType.DMA((self.steps,))] * 3
        return [pltpu.VMEM((3, line, 2, rows, cols), BF16), pltpu.VMEM(self.shape, BF16)] + sems

    def bind(self, place, final, refs):
        self.place, self.final = place, final
        self.stage, self.near, self.send, self.recv, self.leave = refs

    def copy(self, i):
        p = self.place
        return pltpu.make_async_remote_copy(
            src_ref=self.stage.at[lax.rem(i, 3), :, 1 - p.core], dst_ref=self.near.at[self.cut(i)],
            send_sem=self.send.at[i], recv_sem=self.recv.at[i],
            device_id=p.other_core(), device_id_type=MESH,
        )

    def leaving(self, i):
        at = self.cut(i)
        return pltpu.make_async_copy(self.near.at[at], self.final.at[at], self.leave.at[i])

    def push(self, i, value):
        line, rows, cols = self.piece
        self.stage[lax.rem(i, 3)] = value.reshape(line, 2, rows, cols)
        self.copy(i).start()

    def take_late(self, i):
        pl.when(i >= 2)(lambda: self.take(i - 2))

    def take_rest(self, i):
        self.take(i - 1)
        self.take(i)
        for n in range(self.steps):
            self.leaving(n).wait()

    def take(self, i):
        line, rows, cols = self.piece
        self.copy(i).wait_recv()
        self.copy(i).wait_send()
        at = self.cut(i)
        for j in range(line):
            here = (pl.ds(at[0].start + j, 1),) + at[1:]
            self.near[here] = (self.stage[lax.rem(i, 3), j, self.place.core] + self.near[here][0])[None]
        self.leaving(i).start()


class Side:
    def __init__(self, ways, line, jobs):
        self.ways, self.line, self.jobs = ways, line, jobs

    def in_specs(self):
        return [spec for job in self.jobs for spec in job.ins()]

    def out_specs(self):
        return [spec for job in self.jobs for spec, _ in job.out()]

    def out_shape(self):
        return [shape for job in self.jobs for _, shape in job.out()]

    def scratch(self):
        return [s for job in self.jobs for s in job.scratch()]

    def bind(self, sources, finals, refs):
        refs, finals = list(refs), list(finals)
        self.place = Place(self.ways, self.line)
        for job, source in zip(self.jobs, sources):
            many, outs = len(job.scratch()), len(job.out())
            job.bind(self.place, source, finals[:outs], refs[:many])
            refs, finals = refs[many:], finals[outs:]

    def at(self, i, point):
        for job in self.jobs:
            for n in range(12):
                if n in job.plan and job.plan[n][1] == point:
                    if isinstance(i, int):
                        job.phase(n)
                    else:
                        pl.when(i == job.plan[n][0])(functools.partial(job.phase, n))


def remote_params(ident):
    return pltpu.CompilerParams(vmem_limit_bytes=VMEM, collective_id=ident, has_side_effects=True)


def mlp_kernel(pieces, *refs):
    x, mixed, w_out, own_rows = refs[:4]
    cots = refs[4 : 4 + pieces]
    w_up, hidden, ready, gout, act, slope, grad_down = refs[4 + pieces :]
    rows = cots[0].shape[0]

    @pl.when(pl.program_id(0) == 0)
    def _():
        for k in range(pieces):
            span = slice(k * rows, (k + 1) * rows)
            gout[span] = cots[k][...] * own_rows[2:3].astype(BF16)
            h = x[span].astype(F32) + tn(mixed[:, span], w_out[...])
            hidden[span] = h
            ready[span] = (norm_rows(h)[0] * own_rows[1:2]).astype(BF16)

    u = nn(ready[...], w_up[...])
    u2 = u * u
    t = jnp.tanh(u * (GELU_C + (GELU_C * GELU_K) * u2))
    half = 0.5 + 0.5 * t
    a = (u * half).astype(BF16)
    act[...] = a
    slope[...] = (half + u * (1 - t * t) * (0.5 * GELU_C + (1.5 * GELU_C * GELU_K) * u2)).astype(BF16)
    grad_down[...] = tn(a, gout[...]).astype(BF16)


def mlp(x, mixed, w_out, own_rows, cots, w_up):
    length, width = x.shape
    inner = w_up.shape[1]
    rows = length // len(cots)
    block = min(1024, inner)
    cols = pl.BlockSpec((length, block), lambda i: (0, i))
    return pl.pallas_call(
        functools.partial(mlp_kernel, len(cots)),
        grid=(inner // block,),
        in_specs=[
            whole((length, width)),
            whole((length, width)),
            whole((width, width)),
            whole((8, width)),
        ]
        + [whole((rows, width))] * len(cots)
        + [pl.BlockSpec((width, block), lambda i: (0, i))],
        out_specs=[whole((length, width))] * 3 + [cols, cols, pl.BlockSpec((block, width), lambda i: (i, 0))],
        out_shape=[
            jax.ShapeDtypeStruct((length, width), F32),
            jax.ShapeDtypeStruct((length, width), BF16),
            jax.ShapeDtypeStruct((length, width), BF16),
            jax.ShapeDtypeStruct((length, inner), BF16),
            jax.ShapeDtypeStruct((length, inner), BF16),
            jax.ShapeDtypeStruct((inner, width), BF16),
        ],
        compiler_params=params(),
        name="mlp",
    )(x, mixed, w_out, own_rows, *cots, w_up)


def mlp_back_kernel(side, *refs):
    gout, act, slope, w_down, ready, hidden, source = refs[:7]
    many = len(side.out_shape())
    out, grad_upward, grad_up = refs[7:10]
    out_sum = refs[10 + many]
    side.bind([[source]], refs[10 : 10 + many], refs[11 + many :])
    i = pl.program_id(0)
    last = pl.num_programs(0) - 1

    @pl.when(i == 0)
    def _():
        side.place.hail()
        out_sum[...] = hidden[...]
        side.place.greet()

    side.at(i, 0)
    gu = (nt(gout[...], w_down[...]) * slope[...].astype(F32)).astype(BF16)
    grad_upward[...] = gu
    grad_up[...] = tn(ready[...], gu).astype(BF16)
    side.at(i, 1)
    out_sum[...] += nn(act[...], w_down[...])

    @pl.when(i == last)
    def _():
        out[...] = out_sum[...].astype(BF16)
        side.at(i, "end")


def mlp_back(gout, act, slope, w_down, ready, hidden, grad_down, ways):
    length, width = gout.shape
    inner = w_down.shape[0]
    line, _, down_rows, _ = grad_down.shape
    block = inner // 8
    cols = pl.BlockSpec((length, block), lambda i: (0, i))
    square = whole((length, width))
    plan = {0: (0, 0), 1: (2, 0), 2: (3, 1), 3: (6, 0), 4: (7, "end")}
    side = Side(ways, line, [Sums(ways, line, down_rows, width, DOWN_SHARES, plan, False, "front")])
    return pl.pallas_call(
        functools.partial(mlp_back_kernel, side),
        grid=(8,),
        in_specs=[
            square,
            cols,
            cols,
            pl.BlockSpec((block, width), lambda i: (i, 0)),
            square,
            square,
        ]
        + side.in_specs(),
        out_specs=[square, cols, pl.BlockSpec((width, block), lambda i: (0, i))] + side.out_specs(),
        out_shape=[
            jax.ShapeDtypeStruct((length, width), BF16),
            jax.ShapeDtypeStruct((length, inner), BF16),
            jax.ShapeDtypeStruct((width, inner), BF16),
        ]
        + side.out_shape(),
        scratch_shapes=[pltpu.VMEM((length, width), F32)] + side.scratch(),
        compiler_params=remote_params(2),
        name="mlp_back",
    )(gout, act, slope, w_down, ready, hidden, grad_down)


def attn_back_kernel(side, pair_sum, bq, *refs):
    bins, *refs = refs
    gu, w_up, hidden, gout, own_rows, mixed, w_out, packed, aux, w_qkv, ready, x = refs[:12]
    back_from = len(side.jobs[0].ins())
    carried, source_up, source_out = refs[12 : 12 + back_from], refs[12 + back_from], refs[13 + back_from]
    refs = refs[14 + back_from :]
    grad_qkv, grad_x, tables = refs[:3]
    many = len(side.out_shape())
    finals, refs = refs[3 : 3 + many], refs[3 + many :]
    back_sum, grad_hidden, grad_mixed, spare, grad_out, row_mlp, late = refs[:7]
    pairing = len(pair_sum.scratch())
    side.bind([carried, [source_up], [grad_out], [source_out]], finals, refs[7 + pairing :])
    pair_sum.bind(side.place, grad_qkv, refs[7 : 7 + pairing])
    i = pl.program_id(0)
    steps = pl.num_programs(0) // 2
    length, width = gout.shape
    line = grad_out.shape[0]
    span = math.gcd(length, 256)
    load_hidden = pltpu.make_async_copy(hidden, grad_hidden, late.at[0])
    load_w = pltpu.make_async_copy(w_out, spare, late.at[1])
    load_gout = pltpu.make_async_copy(gout, grad_x, late.at[2])
    load_x = pltpu.make_async_copy(x, spare, late.at[3])

    @pl.when(i == 0)
    def _():
        side.place.hail()
        load_hidden.start()
        load_w.start()
        load_gout.start()
        back_sum[...] = jnp.zeros_like(back_sum)

    pl.when(i == 1)(side.place.greet)
    side.at(i, 0)

    @pl.when(i < steps)
    def _():
        back_sum[...] += nt(gu[...], w_up[...])

    @pl.when(i == steps - 1)
    def _():
        load_hidden.wait()
        load_w.wait()
        load_gout.wait()
        total = jnp.zeros((1, width), F32)
        for r in range(length // span):
            here = slice(r * span, (r + 1) * span)
            normed, inverse = norm_rows(grad_hidden[here])
            g = back_sum[here]
            total = total + jnp.sum(g * normed, axis=0, keepdims=True)
            grad_hidden[here] = grad_x[here].astype(F32) + norm_back(g * own_rows[1:2], normed, inverse)
        row_mlp[...] = total
        side.at(i, "norm")
        low = grad_hidden[...].astype(BF16)
        grad_mixed[...] = nt(spare[...], low).astype(BF16)
        load_x.start()
        grad_out[...] = nn(mixed[...], low).astype(BF16).reshape(grad_out.shape)
        back_sum[...] = jnp.zeros_like(back_sum)
        side.at(i, "out")

    @pl.when(i >= steps)
    def _():
        pair = i - steps
        pair_sum.take_late(pair)
        rows = pl.ds(pl.multiple_of(pair * 2 * HEAD, 2 * HEAD), 2 * HEAD)
        parts = attend_back_head(packed, mixed[rows], aux, grad_mixed[rows], bq, 0)
        side.at(i, "mid")
        parts = parts + attend_back_head(packed, mixed[rows], aux, grad_mixed[rows], bq, 1)
        side.at(i, 1)
        gp = jnp.concatenate(parts, axis=0)
        pair_sum.push(pair, nt(ready[...], gp).astype(BF16))
        back_sum[...] += tn(gp, w_qkv[...])
        side.at(i, 2)

    @pl.when(i == pl.num_programs(0) - 1)
    def _():
        load_x.wait()
        total = jnp.zeros((1, width), F32)
        for r in range(length // span):
            here = slice(r * span, (r + 1) * span)
            normed, inverse = norm_rows(spare[here].astype(F32))
            g = back_sum[here]
            total = total + jnp.sum(g * normed, axis=0, keepdims=True)
            grad_x[here] = (grad_hidden[here] + norm_back(g * own_rows[0:1], normed, inverse)).astype(BF16)
        bins_here = tables.shape[2] // 4
        marked = lax.broadcasted_iota(jnp.int32, (2 * line * bins_here, width), 0) == bins[side.place.me]
        both = [jnp.where(marked, row, 0.0) for row in (total, row_mlp[...])]
        half = width // 2
        for b in range(2 * line):
            own = slice(b * bins_here, (b + 1) * bins_here)
            parts = [v[own, cut] for cut in (slice(0, half), slice(half, width)) for v in both]
            tables[b // 2, b % 2] = jnp.concatenate(parts, axis=0).astype(BF16)
        pair_sum.take_rest(i - steps)
        side.at(i, "end")


def attn_back(bins, gu, w_up, hidden, gout, own_rows, mixed, w_out, packed, aux, w_qkv, ready, x, carried, grad_up, out, ways):
    length, width = gout.shape
    inner = w_up.shape[1]
    cols = packed.shape[0]
    pairs = cols // (6 * HEAD)
    line, _, rows, _ = grad_up.shape
    block = inner // pairs
    square = whole((length, width))
    remote = pl.BlockSpec(memory_space=pl.ANY)
    first = lambda i: jnp.minimum(i, pairs - 1)
    second = lambda i: jnp.maximum(i - pairs, 0)
    plan_down = {5: (1, 0), 6: (5, 0), 7: (7, 0), 8: (7, "norm"), 9: (8, "mid"), 10: (9, 0), 11: (15, "end")}
    plan_up = {
        0: (1, 0), 1: (7, 0), 2: (8, 1), 3: (10, "mid"), 4: (12, 1), 5: (12, 1),
        6: (13, 0), 7: (13, 1), 8: (14, 0), 9: (14, "mid"), 10: (15, 0), 11: (15, "end"),
    }
    plan_out = {
        0: (7, "out"), 1: (8, "mid"), 2: (9, "mid"), 3: (11, 0), 4: (12, 2), 5: (12, 2),
        6: (13, "mid"), 7: (13, 2), 8: (14, "mid"), 9: (14, 1), 10: (15, "mid"), 11: (15, "end"),
    }
    plan_swap = {0: (8, "mid"), 1: (10, 1), 2: (15, 1)}
    side = Side(
        ways,
        line,
        [
            Sums(ways, line, inner // (2 * line), width, DOWN_SHARES, plan_down, False, "back"),
            Sums(ways, line, rows, inner, UP_SHARES, plan_up),
            Sums(ways, line, rows, width, OUT_SHARES, plan_out),
            Swap(ways, length // ways, width, plan_swap),
        ],
    )
    wide = 6 * HEAD
    pair_sum = PairSum(
        line, rows, cols, pairs, (line, rows, wide),
        lambda i: (pl.ds(0, line), slice(None), pl.ds(pl.multiple_of(i * wide, wide), wide)),
    )
    inner_jobs = side.jobs[0].ins() + [remote, remote]
    return pl.pallas_call(
        functools.partial(attn_back_kernel, side, pair_sum, math.gcd(length, 256)),
        grid=(2 * pairs,),
        in_specs=[
            pl.BlockSpec(memory_space=pltpu.SMEM),
            pl.BlockSpec((length, block), lambda i: (0, first(i))),
            pl.BlockSpec((width, block), lambda i: (0, first(i))),
            remote,
            remote,
            whole((8, width)),
            whole((width, length)),
            remote,
            pl.BlockSpec((wide, length), lambda i: (second(i), 0)),
            pl.BlockSpec((None, 8, length), lambda i: (second(i), 0, 0)),
            pl.BlockSpec((wide, width), lambda i: (second(i), 0)),
            whole((width, length)),
            remote,
        ]
        + inner_jobs,
        out_specs=[pair_sum.out()[0], square, whole((line, 2, 32, width // 2))] + side.out_specs(),
        out_shape=[
            pair_sum.out()[1],
            jax.ShapeDtypeStruct((length, width), BF16),
            jax.ShapeDtypeStruct((line, 2, 32, width // 2), BF16),
        ]
        + side.out_shape(),
        scratch_shapes=[
            pltpu.VMEM((length, width), F32),
            pltpu.VMEM((length, width), F32),
            pltpu.VMEM((width, length), BF16),
            pltpu.VMEM((length, width), BF16),
            pltpu.VMEM((line, 2, rows, width), BF16),
            pltpu.VMEM((1, width), F32),
            pltpu.SemaphoreType.DMA((4,)),
        ]
        + pair_sum.scratch()
        + side.scratch(),
        compiler_params=remote_params(3),
        name="attn_back",
    )(bins, gu, w_up, hidden, gout, own_rows, mixed, w_out, packed, aux, w_qkv, ready, x, *carried, grad_up, out)


def tail_kernel(side, *refs):
    jobs = len(side.jobs)
    side.bind([[ref] for ref in refs[:jobs]], refs[jobs : 2 * jobs], refs[2 * jobs :])
    side.place.hail()
    side.place.greet()
    for n in range(12):
        side.at(0, n)
        side.at(0, ("after", n))


def tail(ways, line, sums, pieces):
    plan = {n: (0, n) for n in range(12)}
    behind = {n: (0, ("after", n)) for n in range(12)}
    jobs = [
        Sums(ways, line, v.shape[-2], v.shape[-1], shares, plan if paired else behind, paired)
        for v, shares, paired in sums
    ]
    side = Side(ways, line, jobs + [Swap(ways, pieces.shape[1], pieces.shape[2], {0: (0, ("after", 1)), 1: (0, ("after", 3)), 2: (0, 11)})])
    arrays = [v for v, _, _ in sums] + [pieces]
    return pl.pallas_call(
        functools.partial(tail_kernel, side),
        in_specs=[pl.BlockSpec(memory_space=pl.ANY)] * len(arrays),
        out_specs=side.out_specs(),
        out_shape=side.out_shape(),
        scratch_shapes=side.scratch(),
        compiler_params=remote_params(4),
        name="tail",
    )(*arrays)


def finish_kernel(many, *refs):
    tables, refs = refs[0], refs[1:]
    sources, refs = refs[:many], refs[many:]
    table_attn, table_mlp = refs[:2]
    targets, refs = refs[2 : 2 + many], refs[2 + many :]
    low, wide, (came, left) = refs[:many], refs[many : 2 * many], refs[2 * many :]
    parts = 4

    def span(n, part):
        rows = low[n].shape[0] // parts
        return pl.ds(part * rows, rows)

    def load(n, part):
        at = span(n, part)
        return pltpu.make_async_copy(sources[n].at[at], low[n].at[at], came.at[n, part])

    def store(n, part):
        at = span(n, part)
        return pltpu.make_async_copy((wide[n] if changed(n) else low[n]).at[at], targets[n].at[at], left.at[n, part])

    def changed(n):
        return targets[n].dtype != low[n].dtype

    pieces = [(n, part) for n in range(many) for part in range(parts)]
    for piece in pieces:
        load(*piece).start()
    half = tables.shape[1]
    for first, table in ((0, table_attn), (8, table_mlp)):
        table[:, :half] = tables[first : first + 8].astype(F32)
        table[:, half:] = tables[first + 16 : first + 24].astype(F32)
    for n, part in pieces:
        load(n, part).wait()
        if not changed(n):
            store(n, part).start()
            continue
        rows, cols = low[n].shape[0] // parts, low[n].shape[1]
        step = row_step(rows, cols)

        def one(r, carry, n=n, part=part, rows=rows, step=step):
            at = pl.ds(pl.multiple_of(part * rows + r * step, step), step)
            wide[n][at] = low[n][at].astype(F32)
            return carry

        lax.fori_loop(0, rows // step, one, 0)
        store(n, part).start()
    for piece in pieces:
        store(*piece).wait()


def finish(tables, arrays, kinds):
    many = len(arrays)
    remote = pl.BlockSpec(memory_space=pl.ANY)
    here = pl.BlockSpec(memory_space=pltpu.VMEM)
    table = jax.ShapeDtypeStruct((8, 2 * tables.shape[1]), F32)
    return pl.pallas_call(
        functools.partial(finish_kernel, many),
        in_specs=[here] + [remote] * many,
        out_specs=[here, here] + [remote] * many,
        out_shape=[table, table] + [jax.ShapeDtypeStruct(v.shape, kind) for v, kind in zip(arrays, kinds)],
        scratch_shapes=[pltpu.VMEM(v.shape, BF16) for v in arrays]
        + [pltpu.VMEM(v.shape, F32) for v in arrays]
        + [pltpu.SemaphoreType.DMA((many, 4))] * 2,
        compiler_params=params(),
        name="finish",
    )(tables, *arrays)


def exchange(pieces, me, ways):
    return [pieces[0]] + [
        lax.ppermute(pieces[k], "seq", [(s, s ^ k) for s in range(ways)]) for k in range(1, ways)
    ]


def by_partner(slots, me, ways):
    return [lax.dynamic_index_in_dim(slots, me ^ k, 0, keepdims=False) for k in range(ways)]


def body(tokens, cotangent, bins, live_count, w_qkv, w_out, w_up, w_down, gain_attn, gain_mlp):
    slots, rows, width = tokens.shape
    ways = lax.axis_size("seq")
    batch_ways = lax.axis_size("batch")
    line = batch_ways // 2
    me = lax.axis_index("seq")
    x, ready_attn, packed, w_turned, own_rows, *pieces = entry(
        bins, live_count, tokens, cotangent, gain_attn, gain_mlp, w_qkv
    )
    cots = exchange(pieces, me, ways)
    mixed, aux = attend(packed)
    hidden, ready_mlp, gout, act, slope, grad_down = mlp(x, mixed, w_out, own_rows, cots, w_up)

    def blocks(v):
        return v.reshape(line, 2, v.shape[0] // batch_ways, v.shape[1])

    out, grad_upward, grad_up, *carried = mlp_back(
        gout, act, slope, w_down, ready_mlp, hidden, blocks(grad_down), ways
    )
    qkv_pair, grad_x, tables, sum_down, sum_up, sum_out, output = attn_back(
        bins, grad_upward, w_up, hidden, gout, own_rows, mixed, w_out, packed, aux, w_turned, ready_attn, x,
        carried, blocks(grad_up), out.reshape(ways, rows, width), ways,
    )
    sum_qkv, sum_tables, grad_tokens = tail(
        ways,
        line,
        [(qkv_pair, QKV_SHARES, True), (tables, (0,), False)],
        grad_x.reshape(ways, rows, width),
    )
    arrays = [v.reshape(slots * rows, width) for v in (grad_tokens, output)] + [sum_qkv, sum_out, sum_up, sum_down]
    sum_attn, sum_mlp, grad_tokens, output, *sums = finish(sum_tables, arrays, [F32, BF16] + [F32] * 4)
    return (output.reshape(tokens.shape), grad_tokens.reshape(tokens.shape), *sums, sum_attn, sum_mlp)


def plain_norm(values_in):
    centred = values_in - jnp.mean(values_in, axis=-1, keepdims=True)
    inverse = lax.rsqrt(jnp.mean(centred * centred, axis=-1, keepdims=True) + 1e-05)
    return (centred * inverse, inverse)


def plain_norm_back(grad_normed, normed, inverse):
    first_mean = jnp.mean(grad_normed, axis=-1, keepdims=True)
    second_mean = jnp.mean(grad_normed * normed, axis=-1, keepdims=True)
    return inverse * (grad_normed - first_mean - normed * second_mean)


def plain_weight_grad(left, right):
    return lax.dot_general(
        left, right, (((0,), (0,)), ((), ())), preferred_element_type=jnp.float32
    )


def plain_heads(packed, heads_here):
    shaped = packed.reshape(packed.shape[0], heads_here, 3, -1)
    return (shaped[:, :, 0], shaped[:, :, 1], shaped[:, :, 2])


def plain_attend(packed, heads_here, block_rows):
    queries, key_rows, values = plain_heads(packed, heads_here)
    length, head_size = (queries.shape[0], queries.shape[2])
    factor = head_size ** (-0.5)
    blocked = queries.reshape(length // block_rows, block_rows, heads_here, head_size)

    def per_block(query_block):
        scores = (
            jnp.einsum("qhd,khd->hqk", query_block, key_rows, preferred_element_type=jnp.float32)
            * factor
        )
        row_max = jnp.max(scores, axis=-1, keepdims=True)
        logsum = row_max + jnp.log(jnp.sum(jnp.exp(scores - row_max), axis=-1, keepdims=True))
        softmax_rows = jnp.exp(scores - logsum).astype(jnp.bfloat16)
        mixed_rows = jnp.einsum(
            "hqk,khd->qhd", softmax_rows, values, preferred_element_type=jnp.float32
        )
        return (
            mixed_rows.astype(jnp.bfloat16).reshape(block_rows, heads_here * head_size),
            logsum[..., 0],
        )

    mixed_rows, logsum = lax.map(per_block, blocked)
    return (mixed_rows.reshape(length, heads_here * head_size), logsum)


def plain_attend_back(packed, logsum, grad_mixed, heads_here, block_rows):
    queries, key_rows, values = plain_heads(packed, heads_here)
    length, head_size = (queries.shape[0], queries.shape[2])
    factor = head_size ** (-0.5)
    count_blocks = length // block_rows
    query_blocks = queries.reshape(count_blocks, block_rows, heads_here, head_size)
    grad_blocks = grad_mixed.reshape(count_blocks, block_rows, heads_here, head_size)

    def per_block(running, pieces):
        query_block, grad_block, logsum_block = pieces
        scores = (
            jnp.einsum("qhd,khd->hqk", query_block, key_rows, preferred_element_type=jnp.float32)
            * factor
        )
        softmax_rows = jnp.exp(scores - logsum_block[..., None])
        grad_values = running[1] + jnp.einsum(
            "hqk,qhd->khd",
            softmax_rows.astype(jnp.bfloat16),
            grad_block,
            preferred_element_type=jnp.float32,
        )
        grad_soft = jnp.einsum(
            "qhd,khd->hqk", grad_block, values, preferred_element_type=jnp.float32
        )
        inner = jnp.sum(softmax_rows * grad_soft, axis=-1, keepdims=True)
        grad_scores = (softmax_rows * (grad_soft - inner)).astype(jnp.bfloat16)
        grad_query = (
            jnp.einsum("hqk,khd->qhd", grad_scores, key_rows, preferred_element_type=jnp.float32)
            * factor
        )
        grad_keys = (
            running[0]
            + jnp.einsum(
                "hqk,qhd->khd", grad_scores, query_block, preferred_element_type=jnp.float32
            )
            * factor
        )
        return ((grad_keys, grad_values), grad_query)

    zeros_start = jnp.zeros((length, heads_here, head_size), jnp.float32)
    (grad_keys, grad_values), grad_queries = lax.scan(
        per_block, (zeros_start, zeros_start), (query_blocks, grad_blocks, logsum)
    )
    grad_queries = grad_queries.reshape(length, heads_here, head_size)
    stacked = jnp.stack([grad_queries, grad_keys, grad_values], axis=2)
    return stacked.reshape(length, heads_here * 3 * head_size).astype(jnp.bfloat16)


def plain_body(tokens, cotangent, bins, live_count, w_qkv, w_out, w_up, w_down, gain_attn, gain_mlp):
    slot_count, local_rows, model_width = tokens.shape
    seq_ways = lax.axis_size("seq")
    heads_here = HEADS // seq_ways
    length = local_rows * seq_ways
    block_rows = math.gcd(length, 512)
    row_count = slot_count * local_rows
    table_rows = gain_attn.shape[0]
    onehot = (bins[:, None] == jnp.arange(table_rows, dtype=jnp.int32)[None, :]).astype(jnp.float32)
    gains_attn = jnp.dot(onehot, gain_attn, precision=lax.Precision.HIGHEST)[:, None, :]
    gains_mlp = jnp.dot(onehot, gain_mlp, precision=lax.Precision.HIGHEST)[:, None, :]
    inputs = tokens.astype(jnp.float32)

    def attention_part():
        normed_attn, inverse_attn = plain_norm(inputs)
        ready_attn = (normed_attn * gains_attn).astype(jnp.bfloat16).reshape(row_count, model_width)
        packed = jnp.dot(ready_attn, w_qkv, preferred_element_type=jnp.float32).astype(jnp.bfloat16)
        packed = packed.reshape(slot_count, local_rows, 3 * model_width)
        item_rows = lax.all_to_all(packed, "seq", split_axis=2, concat_axis=1, tiled=True)
        mixed_items, logsum_items = lax.map(
            lambda single: plain_attend(single, heads_here, block_rows), item_rows
        )
        mixed_rows = lax.all_to_all(
            mixed_items, "seq", split_axis=1, concat_axis=2, tiled=True
        ).reshape(row_count, model_width)
        return (normed_attn, inverse_attn, ready_attn, item_rows, logsum_items, mixed_rows)

    def mlp_part(hidden):
        normed_mlp, inverse_mlp = plain_norm(hidden)
        ready_mlp = (normed_mlp * gains_mlp).astype(jnp.bfloat16).reshape(row_count, model_width)
        upward = jnp.dot(ready_mlp, w_up, preferred_element_type=jnp.float32)
        active = jax.nn.gelu(upward).astype(jnp.bfloat16)
        return (normed_mlp, inverse_mlp, ready_mlp, upward, active)

    saved_attn = attention_part()
    attended = jnp.dot(saved_attn[5], w_out, preferred_element_type=jnp.float32)
    hidden = inputs + attended.reshape(slot_count, local_rows, model_width)
    saved_mlp = mlp_part(hidden)
    branch = jnp.dot(saved_mlp[4], w_down, preferred_element_type=jnp.float32)
    output = (hidden + branch.reshape(slot_count, local_rows, model_width)).astype(jnp.bfloat16)
    saved_attn = attention_part()
    saved_mlp = mlp_part(hidden)
    normed_attn, inverse_attn, ready_attn, packed_heads, logsum, mixed_rows = saved_attn
    normed_mlp, inverse_mlp, ready_mlp, upward, active = saved_mlp
    alive_mask = (jnp.arange(slot_count, dtype=jnp.int32) < live_count[0]).astype(jnp.float32)
    grad_output = cotangent.astype(jnp.float32) * alive_mask[:, None, None]
    low_output = grad_output.astype(jnp.bfloat16).reshape(row_count, model_width)
    grad_down = plain_weight_grad(active, low_output)
    grad_active = jnp.dot(low_output, w_down.T, preferred_element_type=jnp.float32)
    gelu_values, gelu_pull = jax.vjp(jax.nn.gelu, upward)
    grad_upward = gelu_pull(grad_active)[0].astype(jnp.bfloat16)
    grad_up = plain_weight_grad(ready_mlp, grad_upward)
    grad_ready_mlp = jnp.dot(grad_upward, w_up.T, preferred_element_type=jnp.float32).reshape(
        slot_count, local_rows, model_width
    )
    table_mlp = jnp.dot(
        onehot.T, jnp.sum(grad_ready_mlp * normed_mlp, axis=1), precision=lax.Precision.HIGHEST
    )
    grad_hidden = grad_output + plain_norm_back(grad_ready_mlp * gains_mlp, normed_mlp, inverse_mlp)
    low_hidden = grad_hidden.astype(jnp.bfloat16).reshape(row_count, model_width)
    grad_out = plain_weight_grad(mixed_rows, low_hidden)
    grad_mixed = jnp.dot(low_hidden, w_out.T, preferred_element_type=jnp.float32).astype(
        jnp.bfloat16
    )
    grad_mixed = grad_mixed.reshape(slot_count, local_rows, model_width)
    grad_mixed_heads = lax.all_to_all(grad_mixed, "seq", split_axis=2, concat_axis=1, tiled=True)
    grad_packed_heads = lax.map(
        lambda pieces: plain_attend_back(pieces[0], pieces[1], pieces[2], heads_here, block_rows),
        (packed_heads, logsum, grad_mixed_heads),
    )
    grad_packed = lax.all_to_all(
        grad_packed_heads, "seq", split_axis=1, concat_axis=2, tiled=True
    ).reshape(row_count, 3 * model_width)
    grad_qkv = plain_weight_grad(ready_attn, grad_packed)
    grad_ready_attn = jnp.dot(grad_packed, w_qkv.T, preferred_element_type=jnp.float32).reshape(
        slot_count, local_rows, model_width
    )
    table_attn = jnp.dot(
        onehot.T, jnp.sum(grad_ready_attn * normed_attn, axis=1), precision=lax.Precision.HIGHEST
    )
    grad_tokens = grad_hidden + plain_norm_back(grad_ready_attn * gains_attn, normed_attn, inverse_attn)
    gradients = (grad_qkv, grad_out, grad_up, grad_down, table_attn, table_mlp)
    shares = (
        lax.psum_scatter(gradients[0], "batch", scatter_dimension=0, tiled=True),
        lax.psum_scatter(gradients[1], "batch", scatter_dimension=0, tiled=True),
        lax.psum_scatter(gradients[2], "batch", scatter_dimension=0, tiled=True),
        lax.psum_scatter(gradients[3], "batch", scatter_dimension=0, tiled=True),
        lax.psum_scatter(gradients[4], "batch", scatter_dimension=0, tiled=True),
        lax.psum_scatter(gradients[5], "batch", scatter_dimension=0, tiled=True),
    )
    summed = (
        lax.psum(shares[0].astype(jnp.bfloat16), "seq").astype(jnp.float32),
        lax.psum(shares[1].astype(jnp.bfloat16), "seq").astype(jnp.float32),
        lax.psum(shares[2].astype(jnp.bfloat16), "seq").astype(jnp.float32),
        lax.psum(shares[3].astype(jnp.bfloat16), "seq").astype(jnp.float32),
        lax.psum(shares[4].astype(jnp.bfloat16), "seq").astype(jnp.float32),
        lax.psum(shares[5].astype(jnp.bfloat16), "seq").astype(jnp.float32),
    )
    return (output, grad_tokens, summed[0], summed[1], summed[2], summed[3], summed[4], summed[5])


def solution(mesh):
    placed = (
        P("batch", "seq", None),
        P("batch", "seq", None),
        P("batch"),
        P("batch"),
        P(),
        P(),
        P(),
        P(),
        P(),
        P(),
    )
    fits = mesh.shape["seq"] == 4 and mesh.shape["batch"] == 8
    return jax.shard_map(
        body if fits else plain_body,
        mesh=mesh,
        in_specs=placed,
        out_specs=(
            P("batch", "seq", None),
            P("batch", "seq", None),
            P("batch", None),
            P("batch", None),
            P("batch", None),
            P("batch", None),
            P("batch", None),
            P("batch", None),
        ),
        check_vma=False,
    )
```
